32 devices in a mesh: dp: 16 (over z, y, core), tensor: 2 (over x).
Axes of the slice: x: 2, y: 2, z: 4, core: 2. Of those that a mesh axis runs over, the one named last changes fastest.
Arguments:
- tokens: bfloat16 [576, 32, 768], P('tensor', 'dp'), may hold values from -6 to 6
- valid: int32 [32], P('dp'), may hold values 0 or 1
- cotangent: bfloat16 [576, 32, 768], P('tensor', 'dp'), may hold values from -6 to 6
- row_gain: bfloat16 [2, 2, 768], P(None, None, 'dp'), may hold values from 0.099609375 to 1.8984375
- row_bias: bfloat16 [2, 4, 768], P(None, None, 'dp'), may hold values from -3 to 3
- w_qkv: bfloat16 [2, 768, 3, 768], P(None, 'dp', None, 'tensor'), may hold values from -0.21875 to 0.21875
- qv_bias: bfloat16 [2, 2, 768], P(None, None, 'tensor'), may hold values from -3 to 3
- w_proj: bfloat16 [2, 768, 768], P(None, 'tensor', 'dp'), may hold values from -0.75 to 0.75
- w_fc1: bfloat16 [2, 768, 3072], P(None, 'dp', 'tensor'), may hold values from -0.21875 to 0.21875
- fc1_bias: bfloat16 [2, 3072], P(None, 'tensor'), may hold values from -3 to 3
- w_fc2: bfloat16 [2, 3072, 768], P(None, 'tensor', 'dp'), may hold values from -0.109375 to 0.109375
- rel_table: float32 [2, 24, 529], P(None, 'tensor'), may hold values from -5 to 5
Outputs:
- block_out: bfloat16 [576, 32, 768], P('tensor', 'dp')
- grad_tokens: float32 [576, 32, 768], P('tensor', 'dp')
- grad_row_gain: float32 [2, 2, 768], P(None, None, 'dp')
- grad_row_bias: float32 [2, 4, 768], P(None, None, 'dp')
- grad_w_qkv: float32 [2, 768, 3, 768], P(None, 'dp', None, 'tensor')
- grad_qv_bias: float32 [2, 2, 768], P(None, None, 'tensor')
- grad_w_proj: float32 [2, 768, 768], P(None, 'tensor', 'dp')
- grad_w_fc1: float32 [2, 768, 3072], P(None, 'dp', 'tensor')
- grad_fc1_bias: float32 [2, 3072], P(None, 'tensor')
- grad_w_fc2: float32 [2, 3072, 768], P(None, 'tensor', 'dp')
- grad_rel_table: float32 [2, 24, 529], P(None, 'tensor')
The draws below stay inside these ranges and needn't reach their ends.
All inputs are finite; a program needn't handle non-finite values. No bound on the sum of `valid` on one device may be relied on, other than what follows from the above.
Results may differ from the reference program's by a relative error of at most 0.02.
Values may be sent and summed in bfloat16 or wider, within the bound.
A program may use at most 256 MiB of HBM per device.

```python
import jax
import jax.numpy as jnp
from jax import lax

D = 768
HEADS = 24
FF = 3072
WIN = 12
LAYERS = 2
SLOT_DEV = 2
HDIM = 32
SIDE = 24
SHIFT = 6
RELS = 529
TOK_IMG = 576
SLOTS = 32


def touch_ends(drawn, stream_key, least, top_value):
    extent = drawn.shape
    spot = [jax.random.randint(jax.random.fold_in(stream_key, axis), (), 0, extent[axis]) for axis in range(len(extent))]
    drawn = drawn.at[tuple(spot)].set(least)
    longest = extent.index(max(extent))
    spot[longest] = (spot[longest] + 1) % extent[longest]
    return drawn.at[tuple(spot)].set(top_value)


def raised(values, key, source, target, shards_of, factor):
    def block_of(axis_at):
        return (jnp.arange(values.shape[axis_at]) // (values.shape[axis_at] // shards_of)).reshape((-1,) + (1,) * (values.ndim - 1 - axis_at))

    one_side = jax.random.permutation(key, shards_of)[block_of(target)]
    second = (block_of(target) + shards_of // 2) % shards_of
    return jnp.where((block_of(source) == one_side) | (block_of(source) == second), factor * values, values)


def steps_of(rng, extent, pieces, low, high):
    def one(axis_at, parts):
        steps = jax.random.uniform(jax.random.fold_in(jax.random.fold_in(rng, 6), axis_at), (parts,), jnp.float32, low / len(pieces), high / len(pieces))
        return jnp.repeat(jnp.exp(steps), extent[axis_at] // parts).reshape((-1,) + (1,) * (len(extent) - axis_at - 1))

    factor_of = one(*pieces[0])
    for cut in pieces[1:]:
        factor_of = factor_of * one(*cut)
    return factor_of


def bell_draw(stream_key, dims, scale, bound, split=(), kind=jnp.bfloat16):
    values = scale * jax.random.normal(stream_key, dims, jnp.float32)
    if split:
        values = values * steps_of(stream_key, dims, split, -0.22, 0.18)
    return jnp.clip(values, -bound, bound).astype(kind)


def bell_draw_with(own_key, shape, width, most, pieces, heavy, kind=jnp.bfloat16):
    values = width * jax.random.normal(own_key, shape, jnp.float32)
    if pieces:
        values = values * steps_of(own_key, shape, pieces, -0.22, 0.18)
    return jnp.clip(raised(values, jax.random.fold_in(own_key, 3), *heavy), -most, most).astype(kind)


def setup_inputs(seed: int = 0) -> dict:
    keys = jax.random.split(jax.random.key(seed), 13)
    tokens = bell_draw(keys[0], (TOK_IMG, SLOTS, D), 1.0, 6.0, ((0, 2), (1, 16)))
    valid = touch_ends((jax.random.randint(keys[1], (SLOTS,), 0, 4) < 3).astype(jnp.int32), jax.random.fold_in(keys[1], 1), 0, 1)
    cotangent = bell_draw_with(keys[2], (TOK_IMG, SLOTS, D), 1.0, 6.0, ((0, 2), (1, 16)), (1, 2, 16, 2.0))
    row_gain = jnp.clip(1.0 + 0.18 * jax.random.normal(keys[3], (LAYERS, 2, D), jnp.float32), 0.099609375, 1.8984375).astype(jnp.bfloat16)
    row_bias = bell_draw(keys[4], (LAYERS, 4, D), 0.5, 3.0, ((2, 16),))
    w_qkv = bell_draw(keys[5], (LAYERS, D, 3, D), D ** -0.5, 0.21875, ((1, 16), (3, 2)))
    qv_bias = bell_draw(keys[6], (LAYERS, 2, D), 0.5, 3.0, ((2, 2),))
    w_proj = bell_draw(keys[7], (LAYERS, D, D), (D // WIN) ** -0.5, 0.75, ((1, 2), (2, 16)))
    w_fc1 = bell_draw(keys[8], (LAYERS, D, FF), D ** -0.5, 0.21875, ((1, 16), (2, 2)))
    fc1_bias = bell_draw(keys[9], (LAYERS, FF), 0.5, 3.0, ((1, 2),))
    w_fc2 = bell_draw(keys[10], (LAYERS, FF, D), FF ** -0.5, 0.109375, ((1, 2), (2, 16)))
    rel_table = bell_draw(keys[11], (LAYERS, HEADS, RELS), 1.0, 5.0, ((1, 2),), jnp.float32)
    return {"tokens": tokens, "valid": valid, "cotangent": cotangent, "row_gain": row_gain, "row_bias": row_bias, "w_qkv": w_qkv, "qv_bias": qv_bias, "w_proj": w_proj, "w_fc1": w_fc1, "fc1_bias": fc1_bias, "w_fc2": w_fc2, "rel_table": rel_table}


@jax.custom_vjp
def low(v):
    return lax.optimization_barrier(v.astype(jnp.bfloat16)).astype(jnp.float32)

@jax.custom_vjp
def low_back(v):
    return v

def low_keep(v):
    return (low(v), None)

def low_pass(kept, grad):
    return (grad,)

def back_keep(v):
    return (v, None)

def back_low(kept, grad):
    return (low(grad),)
low.defvjp(low_keep, low_pass)
low_back.defvjp(back_keep, back_low)
EPSILON = 1e-05
MASK_FILL = -100.0

def round_both(values):
    return low(low_back(values))

def layer_norm(values, row_gain, row_shift):
    average = lax.optimization_barrier(jnp.mean(values, axis=-1, keepdims=True))
    centred = values - average
    variance = lax.optimization_barrier(jnp.mean(centred * centred, axis=-1, keepdims=True))
    return centred * lax.rsqrt(variance + EPSILON) * row_gain + row_shift

def to_windows(rows_data, shifted):
    slot_count = rows_data.shape[1]
    trailing = rows_data.shape[2:]
    image_grid = rows_data.reshape((SIDE, SIDE, slot_count) + trailing)
    if shifted:
        image_grid = jnp.roll(image_grid, (-SHIFT, -SHIFT), axis=(0, 1))
    image_grid = image_grid.reshape((2, WIN, 2, WIN, slot_count) + trailing)
    axes_order = (4, 0, 2, 1, 3) + tuple(range(5, 5 + len(trailing)))
    return jnp.transpose(image_grid, axes_order).reshape((slot_count, 4, WIN * WIN) + trailing)

def from_windows(window_data, shifted):
    slot_count = window_data.shape[0]
    trailing = window_data.shape[3:]
    image_grid = window_data.reshape((slot_count, 2, 2, WIN, WIN) + trailing)
    axes_order = (1, 3, 2, 4, 0) + tuple(range(5, 5 + len(trailing)))
    image_grid = jnp.transpose(image_grid, axes_order).reshape((SIDE, SIDE, slot_count) + trailing)
    if shifted:
        image_grid = jnp.roll(image_grid, (SHIFT, SHIFT), axis=(0, 1))
    return image_grid.reshape((SIDE * SIDE, slot_count) + trailing)

def relative_index():
    positions = jnp.arange(WIN * WIN, dtype=jnp.int32)
    row_pos = positions // WIN
    col_pos = positions % WIN
    return (row_pos[:, None] - row_pos[None, :] + WIN - 1) * (2 * WIN - 1) + (col_pos[:, None] - col_pos[None, :] + WIN - 1)

def shift_mask():
    places = jnp.arange(SIDE, dtype=jnp.int32)
    band_of = (places >= SIDE - WIN).astype(jnp.int32) + (places >= SIDE - SHIFT).astype(jnp.int32)
    region = band_of[:, None] * 3 + band_of[None, :]
    region = region.reshape(2, WIN, 2, WIN).transpose(0, 2, 1, 3).reshape(4, WIN * WIN)
    same_region = region[:, :, None] == region[:, None, :]
    return jnp.where(same_region, 0.0, MASK_FILL).astype(jnp.float32)

def forward(residual, valid_slots, params):
    row_gain, row_bias, w_qkv, qv_bias, w_proj, w_fc1, fc1_bias, w_fc2, rel_table = params
    slot_count = residual.shape[1]
    relative = relative_index()
    head_shape = (slot_count, 4, WIN * WIN, HEADS, HDIM)
    for layer_index in range(LAYERS):
        shifted = layer_index % 2 == 1
        normed = low(layer_norm(residual, row_gain[layer_index, 0], row_bias[layer_index, 0]))
        projected = jnp.einsum('tsd,dke->tske', normed, w_qkv[layer_index], precision=lax.Precision.HIGHEST)
        queries = round_both(projected[:, :, 0] + qv_bias[layer_index, 0])
        key_rows = round_both(projected[:, :, 1])
        value_rows = round_both(projected[:, :, 2] + qv_bias[layer_index, 1])
        queries = to_windows(queries, shifted).reshape(head_shape)
        key_rows = to_windows(key_rows, shifted).reshape(head_shape)
        value_rows = to_windows(value_rows, shifted).reshape(head_shape)
        bias_add = rel_table[layer_index][:, relative][None]
        if shifted:
            bias_add = bias_add + shift_mask()[:, None]
        scores = jnp.einsum('swqhc,swkhc->swhqk', queries, key_rows, precision=lax.Precision.HIGHEST) * HDIM ** (-0.5) + bias_add
        scores = low_back(scores)
        weights = low(jax.nn.softmax(scores, axis=-1))
        blended = round_both(jnp.einsum('swhqk,swkhc->swqhc', weights, value_rows, precision=lax.Precision.HIGHEST))
        blended_rows = from_windows(blended.reshape(slot_count, 4, WIN * WIN, D), shifted)
        attention = low_back(jnp.einsum('tse,ed->tsd', blended_rows, w_proj[layer_index], precision=lax.Precision.HIGHEST))
        residual = residual + attention + row_bias[layer_index, 1]
        normed_mid = low(layer_norm(residual, row_gain[layer_index, 1], row_bias[layer_index, 2]))
        hidden = low_back(jnp.einsum('tsd,df->tsf', normed_mid, w_fc1[layer_index], precision=lax.Precision.HIGHEST) + fc1_bias[layer_index])
        activated = low(jax.nn.gelu(hidden, approximate=False))
        feed = low_back(jnp.einsum('tsf,fd->tsd', activated, w_fc2[layer_index], precision=lax.Precision.HIGHEST))
        residual = residual + feed + row_bias[layer_index, 3]
    return residual * valid_slots[None, :, None]

def reference(tokens, valid, cotangent, row_gain, row_bias, w_qkv, qv_bias, w_proj, w_fc1, fc1_bias, w_fc2, rel_table):
    params = tuple((member.astype(jnp.float32) for member in (row_gain, row_bias, w_qkv, qv_bias, w_proj, w_fc1, fc1_bias, w_fc2, rel_table)))
    groups = SLOTS // SLOT_DEV

    def regroup(array):
        return jnp.transpose(array.reshape(TOK_IMG, groups, SLOT_DEV, D), (1, 0, 2, 3))

    def ungroup(array):
        return jnp.transpose(array, (1, 0, 2, 3)).reshape(TOK_IMG, SLOTS, D)
    token_groups = regroup(tokens.astype(jnp.float32))
    cot_groups = regroup(cotangent.astype(jnp.float32))
    valid_groups = valid.reshape(groups, SLOT_DEV).astype(jnp.float32)

    def step(totals, inputs):
        group_tokens, group_valid, group_cot = inputs
        output, pullback = jax.vjp(lambda residual, weights: forward(residual, group_valid, weights), group_tokens, params)
        grad_group, grad_params = pullback(group_cot)
        totals = jax.tree.map(jnp.add, totals, grad_params)
        return (totals, (output, grad_group))
    zeros = jax.tree.map(jnp.zeros_like, params)
    totals, (outputs, grad_groups) = lax.scan(step, zeros, (token_groups, valid_groups, cot_groups))
    grad_row_gain, grad_row_bias, grad_w_qkv, grad_qv_bias, grad_w_proj, grad_w_fc1, grad_fc1_bias, grad_w_fc2, grad_rel_table = totals
    return (ungroup(outputs).astype(jnp.bfloat16), ungroup(grad_groups), grad_row_gain, grad_row_bias, grad_w_qkv, grad_qv_bias, grad_w_proj, grad_w_fc1, grad_fc1_bias, grad_w_fc2, grad_rel_table)
```

```python
import functools
import numpy as np
import jax
import jax.numpy as jnp
from jax import lax
from jax.experimental import pallas as pl
from jax.experimental.pallas import tpu as pltpu
from jax.sharding import PartitionSpec as P

WIN = 12
LAYERS = 2
HDIM = 32
SIDE = 24
SHIFT = 6
RELS = 529
EPSILON = 1e-05
MASK_FILL = -100.0

D = 768
HEADS = 24
FF = 3072
TOK = 576
WT = 144
UC = 384
NU = 12
HG = 4
NG = HEADS // HG
SCALE = HDIM ** -0.5
BF = jnp.bfloat16
F32 = jnp.float32


def nn(a, b):
    return lax.dot_general(a, b, (((1,), (0,)), ((), ())), preferred_element_type=F32)


def nt(a, b):
    return lax.dot_general(a, b, (((1,), (1,)), ((), ())), preferred_element_type=F32)


def norm_parts(x):
    mean = jnp.mean(x, axis=-1, keepdims=True)
    c = x - mean
    var = jnp.mean(c * c, axis=-1, keepdims=True)
    rstd = lax.rsqrt(var + EPSILON)
    return c * rstd, rstd


def gelu_parts(u):
    phi_big = 0.5 * (1.0 + lax.erf(u * (0.5 ** 0.5)))
    phi = jnp.exp(-0.5 * u * u) * (1.0 / (2.0 * np.pi) ** 0.5)
    return u * phi_big, phi_big + u * phi


def window_order():
    out = []
    for shift in (0, SHIFT):
        p = np.arange(SIDE)
        src = (p + shift) % SIDE
        grid = src[:, None] * SIDE + src[None, :]
        grid = grid.reshape(2, WIN, 2, WIN).transpose(0, 2, 1, 3).reshape(TOK)
        out.append(grid)
    return np.stack(out)


def perm_matrices():
    order = window_order()
    return (order[:, :, None] == np.arange(TOK)[None, None, :]).astype(np.float32)


def shift_mask():
    places = np.arange(SIDE)
    band_of = (places >= SIDE - WIN).astype(np.int32) + (places >= SIDE - SHIFT).astype(np.int32)
    region = band_of[:, None] * 3 + band_of[None, :]
    region = region.reshape(2, WIN, 2, WIN).transpose(0, 2, 1, 3).reshape(4, WT)
    same = region[:, :, None] == region[:, None, :]
    masked = np.where(same, 0.0, MASK_FILL).astype(np.float32)
    return np.stack([np.zeros_like(masked), masked])


def rows_loop(n, body):
    def step(i, c):
        body(i)
        return c
    lax.fori_loop(0, n, step, 0)


def w2d(wbuf, slot, t):
    return wbuf[slot, t].reshape(D, UC)


class Place:
    def __init__(self):
        d, self.t = lax.axis_index("dp"), lax.axis_index("tensor")
        self.z = lax.div(d, 4)
        self.y = lax.rem(lax.div(d, 2), 2)
        self.c = lax.rem(d, 2)
        t, y, even = self.t, self.y, self.c == 0
        self.x_side, self.y_side = (1 - t, y), (t, 1 - y)
        self.first = tuple(jnp.where(even, a, b) for a, b in zip(self.x_side, self.y_side))
        self.second = tuple(jnp.where(even, b, a) for a, b in zip(self.x_side, self.y_side))
        self.diagonal = (1 - t, 1 - y)

    def device(self, z, ty, c):
        return {"dp": (z * 2 + ty[1]) * 2 + c, "tensor": ty[0]}

    def side(self, ty):
        return self.device(self.z, ty, self.c)

    def along(self, k):
        return lax.rem(self.z + k, 4)

    def above(self, k):
        return self.device(self.along(k), (self.t, self.y), self.c)

    def sibling(self):
        return self.device(self.z, (self.t, self.y), 1 - self.c)

    def barrier(self):
        sem = pltpu.get_barrier_semaphore()
        peers = [self.above(k) for k in (1, 2, 3)] + [self.side(self.x_side), self.side(self.y_side), self.sibling()]
        for peer in peers:
            pl.semaphore_signal(sem, inc=1, device_id=peer, device_id_type=MESH)
        pl.semaphore_wait(sem, len(peers))


MESH = pl.DeviceIdType.MESH
GATHER_LAGS = (1, 2, 3, 4)
GATHER_SEMS = 8
TICK_EVERY = 4


class Gather:
    def __init__(self, at, shard, whole, send, recv, local, units):
        self.at, self.shard, self.whole, self.units = at, shard, whole, units
        self.send, self.recv, self.local = send, recv, local

    def copy(self, g, n, src, dst, device):
        slot = lax.rem(g, GATHER_SEMS) if self.units > 1 else 0
        return pltpu.make_async_remote_copy(
            src_ref=src, dst_ref=dst, send_sem=self.send.at[slot, n], recv_sem=self.recv.at[slot, n],
            device_id=device, device_id_type=MESH)

    def mine(self, g):
        p = self.at
        return pltpu.make_async_copy(self.shard.at[g], self.whole.at[g, p.t, p.z, p.y, p.c],
                                     self.local.at[lax.rem(g, GATHER_SEMS) if self.units > 1 else 0])

    def up(self, g, k):
        p = self.at
        return self.copy(g, k - 1, self.shard.at[g], self.whole.at[g, p.t, p.z, p.y, p.c], p.above(k))

    def group(self, g, n, ty, to):
        ref = self.whole.at[g, ty[0], :, ty[1], self.at.c]
        return self.copy(g, n, ref, ref, self.at.side(to))

    def first(self, g):
        return self.group(g, 3, (self.at.t, self.at.y), self.at.first)

    def second(self, g):
        return self.group(g, 4, (self.at.t, self.at.y), self.at.second)

    def onward(self, g):
        return self.group(g, 5, self.at.first, self.at.second)

    def core(self, g):
        ref = self.whole.at[g, :, :, :, self.at.c]
        return self.copy(g, 6, ref, ref, self.at.sibling())

    def stage(self, n, g):
        if n == 0:
            self.mine(g).start()
            for k in (1, 2, 3):
                self.up(g, k).start()
        elif n == 1:
            self.mine(g).wait()
            for k in (1, 2, 3):
                self.up(g, k).wait_recv()
            self.first(g).start()
            self.second(g).start()
        elif n == 2:
            self.first(g).wait_recv()
            self.onward(g).start()
        elif n == 3:
            self.second(g).wait_recv()
            self.onward(g).wait_recv()
            self.core(g).start()
        else:
            self.core(g).wait()
            for k in (1, 2, 3):
                self.up(g, k).wait_send()
            self.first(g).wait_send()
            self.second(g).wait_send()
            self.onward(g).wait_send()

    def tick(self, n):
        for st in (4, 3, 2, 1, 0):
            g = n - (GATHER_LAGS[st - 1] if st else 0)
            if isinstance(g, int):
                if 0 <= g < self.units:
                    self.stage(st, g)
            else:
                @pl.when((g >= 0) & (g < self.units))
                def _(st=st, g=g):
                    self.stage(st, g)


def fold_places():
    lane = np.arange(UC)
    j, xb = lane // WIN, lane % WIN
    return np.where(j < 2 * WIN - 1, (2 * WIN - 2 - j) * (2 * WIN - 1) - xb + WIN - 1, -4 * PAY).astype(np.int32)[None]


def fold_matrix(places, xa):
    rows = lax.broadcasted_iota(jnp.int32, (PAY, UC), 0)
    return jnp.where(rows == places + xa, 1.0, 0.0).astype(BF)


def split3(x):
    hi = x.astype(BF)
    rest = x - hi.astype(F32)
    mid = rest.astype(BF)
    return hi, mid, (rest - mid.astype(F32)).astype(BF)


def half_rows(t):
    return pl.ds(pl.multiple_of(t * HALF, HALF), HALF)


def forward_kernel(tok, cot, valid, vshard, pay, places, mask, perm, permt, shard,
                   out, vec, cot_h, w_hbm, x0_h, x1_h, n1_h, qkv_h, pw_h, o_h, n2_h, gg_h,
                   wbuf, x0, x1, n1, qkv, ow, n2, acc, pst, gst, ubuf,
                   xin, vall, pays, ext, bias,
                   wsem, ssem, psem, gsem, gsend, grecv, glocal, vsend, vrecv, vlocal, xsend, xrecv, xlocal):
    at = Place()
    ag = Gather(at, shard, w_hbm, gsend, grecv, glocal, LAYERS * NU)
    vg = Gather(at, vshard, vall, vsend, vrecv, vlocal, 1)
    at.barrier()
    lag = GATHER_LAGS[-1]
    t = at.t
    mine, theirs = half_rows(t), half_rows(1 - t)
    swaps, keeps = [], []
    for n, (src, here, src_keep) in enumerate((
            (tok.at[1 - t], xin.at[mine], tok.at[t]),
            (pay, pays.at[t], pay),
            (cot.at[1 - t], cot_h.at[mine], cot.at[t]))):
        swaps.append(pltpu.make_async_remote_copy(
            src_ref=src, dst_ref=here, send_sem=xsend.at[n], recv_sem=xrecv.at[n],
            device_id=at.side(at.x_side), device_id_type=MESH))
        keeps.append(pltpu.make_async_copy(src_keep, here, xlocal.at[n]))
    for n in range(2):
        swaps[n].start()
        keeps[n].start()
    for n in range(lag + 1):
        vg.tick(n)
        ag.tick(n)
        if n == 0:
            swaps[1].wait()
            keeps[1].wait()
            table = jnp.concatenate([pays[0, 16:40], pays[1, 16:40]], axis=0)
            parts = jnp.concatenate(split3(table), axis=0)
            for xa in range(WIN):
                y = nn(parts, fold_matrix(places[...], xa))
                ext[:, xa, :] = y[:48] + y[48:96] + y[96:]
    for n in range(2, 3):
        swaps[n].start()
        keeps[n].start()

    def spread(i, c):
        half, l, h = lax.div(i, 24), lax.rem(lax.div(i, 12), 2), lax.rem(i, 12)
        x = ext[i]
        for ya in range(WIN):
            off = (WIN - 1 - ya) * WIN
            bias[l, half * 12 + h, ya * WIN:(ya + 1) * WIN, :] = x[:, off:off + WT]
        return c
    lax.fori_loop(0, 48, spread, 0)
    vec[...] = vall[0, 0].reshape(D, 128).astype(F32).T[:16]
    swaps[0].wait()
    keeps[0].wait()

    def vrow(l, i):
        return vec[pl.ds(l * 6 + i, 1)]

    def fetch(g, u):
        return pltpu.make_async_copy(w_hbm.at[g], wbuf.at[u % 2], wsem.at[u % 2])

    def tick_base(l, u):
        inside = 4 * NG // TICK_EVERY
        return lag + 1 + l * (NU + inside) + u + (inside if u > 3 else 0)

    def step_unit(l, u):
        g = l * NU + u
        fetch(g, u).wait()
        ag.tick(tick_base(l, u) + (4 * NG // TICK_EVERY if u == 3 else 0))

        @pl.when(g + 1 < LAYERS * NU)
        def _():
            fetch(g + 1, u + 1).start()

    fetch(0, 0).start()
    x0[0] = xin[...].astype(F32)
    lanes = lax.shift_right_logical(lax.broadcasted_iota(jnp.int32, (WT, HG * HDIM), 1), 5)

    def layer(l, carry):
        x0_l, x1_l, n1_l, n2_l, ow_l = x0.at[l], x1.at[l], n1.at[l], n2.at[l], ow.at[l]

        def ln1(i):
            r = pl.ds(i * WT, WT)
            xh, _ = norm_parts(x0_l[r])
            ow_l[r] = (xh * vrow(l, 0) + vrow(l, 2)).astype(BF)
        rows_loop(4, ln1)
        n1_l[...] = nn(perm[l], ow_l[...]).astype(BF)
        for j in range(3):
            step_unit(l, j)
            for t in range(2):
                cols = slice(t * UC, (t + 1) * UC)
                y = nn(n1_l[...], w2d(wbuf, j % 2, t))
                if j == 0:
                    y = y + pays[t, pl.ds(l * 2, 1), :UC]
                if j == 2:
                    y = y + pays[t, pl.ds(l * 2 + 1, 1), :UC]
                qkv[l, j, :, cols] = y.astype(BF)

        def attend(it, c):
            w, hg = lax.div(it, NG), lax.rem(it, NG)
            r = pl.ds(pl.multiple_of(w * WT, WT), WT)
            cl = pl.ds(pl.multiple_of(hg * 128, 128), 128)
            slot = lax.rem(it, 2)
            q, k, v = qkv[l, 0, r, cl], qkv[l, 1, r, cl], qkv[l, 2, r, cl]
            put = pltpu.make_async_copy(pst.at[slot], pw_h.at[l, w, pl.ds(hg * HG, HG)], psem.at[slot])

            @pl.when((it >= 2) | (l > 0))
            def _():
                put.wait()
            o = jnp.zeros((WT, 128), F32)
            for h in range(HG):
                qm = jnp.where(lanes == h, q, jnp.zeros_like(q))
                s = nt(qm, k) * SCALE + bias[l, hg * HG + h] + mask[l, w]
                e = jnp.exp(s - jnp.max(s, axis=-1, keepdims=True))
                p = (e * (1.0 / jnp.sum(e, axis=-1, keepdims=True))).astype(BF)
                pst[slot, h] = p
                o = jnp.where(lanes == h, nn(p, v), o)
            ow_l[r, cl] = o.astype(BF)
            put.start()

            @pl.when(lax.rem(it, TICK_EVERY) == TICK_EVERY - 1)
            def _():
                ag.tick(tick_base(l, 3) + lax.div(it, TICK_EVERY))
            return c
        lax.fori_loop(0, 4 * NG, attend, 0)
        n2_l[...] = nn(permt[l], ow_l[...]).astype(BF)
        step_unit(l, 3)
        for t in range(2):
            y = nt(n2_l[:, t * UC:(t + 1) * UC], w2d(wbuf, 1, t))
            if t == 0:
                acc[...] = y
            else:
                acc[...] += y

        def ln2(i):
            r = pl.ds(i * WT, WT)
            x = x0_l[r] + acc[r] + vrow(l, 3)
            x1_l[r] = x
            xh, _ = norm_parts(x)
            n2_l[r] = (xh * vrow(l, 1) + vrow(l, 4)).astype(BF)
            acc[r] = x + vrow(l, 5)
        rows_loop(4, ln2)
        for i in range(4):
            step_unit(l, 4 + 2 * i)
            for t in range(2):
                put = pltpu.make_async_copy(gst.at[t], gg_h.at[l, i, t], gsem.at[t])
                if i > 0:
                    put.wait()
                else:
                    @pl.when(l > 0)
                    def _():
                        put.wait()
                ubuf[...] = nn(n2_l[...], w2d(wbuf, 0, t)) + pays[t, pl.ds(4 + l * 4 + i, 1), :UC]

                def act(n):
                    r = pl.ds(n * 96, 96)
                    g, gp = gelu_parts(ubuf[r])
                    gst[t, 0, r] = g.astype(BF)
                    gst[t, 1, r] = gp.astype(BF)
                rows_loop(6, act)
                put.start()
            step_unit(l, 5 + 2 * i)
            for t in range(2):
                acc[...] += nt(gst[t, 0], w2d(wbuf, 1, t))

        for ref, dst in ((x0, x0_h), (x1, x1_h), (n1, n1_h), (qkv, qkv_h), (ow, o_h), (n2, n2_h)):
            pltpu.make_async_copy(ref.at[l], dst.at[l], ssem.at[l]).start()

        @pl.when(l == 0)
        def _():
            x0[1] = acc[...]

        @pl.when(l == 1)
        def _():
            out[...] = (acc[...] * valid[0].astype(F32)).astype(BF)
        return carry
    lax.fori_loop(0, LAYERS, layer, 0)
    for l in range(LAYERS):
        for ref, dst in ((x0, x0_h), (x1, x1_h), (n1, n1_h), (qkv, qkv_h), (ow, o_h), (n2, n2_h)):
            pltpu.make_async_copy(ref.at[l], dst.at[l], ssem.at[l]).wait()
    for s in range(2):
        pltpu.make_async_copy(pst.at[s], pw_h.at[0, 0, pl.ds(0, HG)], psem.at[s]).wait()
        pltpu.make_async_copy(gst.at[s], gg_h.at[0, 0, s], gsem.at[s]).wait()
    swaps[2].wait()
    keeps[2].wait()


def sds(shape, dtype):
    return jax.ShapeDtypeStruct(shape, dtype)


VM = pl.BlockSpec(memory_space=pltpu.VMEM)
AN = pl.BlockSpec(memory_space=pl.ANY)
SM = pl.BlockSpec(memory_space=pltpu.SMEM)

SAVED = [
    sds((LAYERS, TOK, D), F32), sds((LAYERS, TOK, D), F32), sds((LAYERS, TOK, D), BF),
    sds((LAYERS, 3, TOK, D), BF), sds((LAYERS, 4, HEADS, WT, WT), BF),
    sds((LAYERS, TOK, D), BF), sds((LAYERS, TOK, D), BF), sds((LAYERS, 4, 2, 2, TOK, UC), BF),
]


def forward_call(tok, cot, valid, vshard, pay, shard):
    perm = perm_matrices()
    permt = jnp.asarray(perm.transpose(0, 2, 1), BF)
    return pl.pallas_call(
        forward_kernel,
        out_shape=[sds((TOK, D), BF), sds((16, D), F32), sds((TOK, D), BF),
                   sds((LAYERS * NU, 2, 4, 2, 2, 48, UC), BF)] + SAVED,
        in_specs=[AN, AN, SM, AN, AN, VM, VM, VM, VM, AN],
        out_specs=[VM, VM] + [AN] * 10,
        scratch_shapes=[
            pltpu.VMEM((2, 2, 4, 2, 2, 48, UC), BF),
            pltpu.VMEM((2, TOK, D), F32), pltpu.VMEM((2, TOK, D), F32),
            pltpu.VMEM((2, TOK, D), BF), pltpu.VMEM((2, 3, TOK, D), BF),
            pltpu.VMEM((2, TOK, D), BF), pltpu.VMEM((2, TOK, D), BF),
            pltpu.VMEM((TOK, D), F32), pltpu.VMEM((2, HG, WT, WT), BF),
            pltpu.VMEM((2, 2, TOK, UC), BF), pltpu.VMEM((TOK, UC), F32),
            pltpu.VMEM((TOK, D), BF), pltpu.VMEM((1, 2, 4, 2, 2, 48, 128), BF),
            pltpu.VMEM((2, 40, PAY), F32), pltpu.VMEM((48, WIN, UC), F32),
            pltpu.VMEM((LAYERS, HEADS, WT, WT), F32),
            pltpu.SemaphoreType.DMA((2,)), pltpu.SemaphoreType.DMA((2,)),
            pltpu.SemaphoreType.DMA((2,)), pltpu.SemaphoreType.DMA((2,)),
            pltpu.SemaphoreType.DMA((GATHER_SEMS, 7)), pltpu.SemaphoreType.DMA((GATHER_SEMS, 7)),
            pltpu.SemaphoreType.DMA((GATHER_SEMS,)),
            pltpu.SemaphoreType.DMA((1, 7)), pltpu.SemaphoreType.DMA((1, 7)), pltpu.SemaphoreType.DMA((1,)),
            pltpu.SemaphoreType.DMA((3,)), pltpu.SemaphoreType.DMA((3,)), pltpu.SemaphoreType.DMA((3,)),
        ],
        compiler_params=pltpu.CompilerParams(vmem_limit_bytes=60 * 2**20, collective_id=0, has_side_effects=True),
        name="forward",
    )(tok, cot, valid, vshard, pay, fold_places(), shift_mask(), jnp.asarray(perm, BF), permt, shard)


BACK_ORDER = (5, 4, 7, 6, 9, 8, 11, 10, 3, 0, 1, 2)


def norm_back(x, dn, gain):
    xh, rstd = norm_parts(x)
    dx = dn * gain
    grad = rstd * (dx - jnp.mean(dx, axis=-1, keepdims=True)
                   - xh * jnp.mean(dx * xh, axis=-1, keepdims=True))
    return grad, jnp.sum(dn * xh, axis=0, keepdims=True), jnp.sum(dn, axis=0, keepdims=True)


REDUCE_SLOTS = 8
PAY = 640
HALF = TOK // 2
VIRT = 16
GAP = (9, 13)
REDUCE_LAGS = (1, 2, 3, 4)


class Reduce:
    def __init__(self, at, own, core_in, first_in, second_in, z_in, total, send, recv):
        self.at, self.own, self.total = at, own, total
        self.core_in, self.first_in, self.second_in, self.z_in = core_in, first_in, second_in, z_in
        self.send, self.recv = send, recv

    def copy(self, v, n, src, dst, device):
        slot = lax.rem(v, REDUCE_SLOTS)
        return pltpu.make_async_remote_copy(
            src_ref=src, dst_ref=dst, send_sem=self.send.at[slot, n], recv_sem=self.recv.at[slot, n],
            device_id=device, device_id_type=MESH)

    def core(self, v):
        slot = lax.rem(v, REDUCE_SLOTS)
        return self.copy(v, 0, self.own.at[slot, :, :, :, 1 - self.at.c], self.core_in.at[slot], self.at.sibling())

    def group(self, v, ty):
        return self.own.at[lax.rem(v, REDUCE_SLOTS), ty[0], :, ty[1], self.at.c]

    def first(self, v, n):
        p = self.at
        ty = p.diagonal if n == 0 else p.second
        return self.copy(v, 1 + n, self.group(v, ty), self.first_in.at[lax.rem(v, REDUCE_SLOTS), n], p.side(p.second))

    def second(self, v):
        p = self.at
        return self.copy(v, 3, self.group(v, p.first), self.second_in.at[lax.rem(v, REDUCE_SLOTS)], p.side(p.first))

    def up(self, v, k):
        p, slot = self.at, lax.rem(v, REDUCE_SLOTS)
        return self.copy(v, 3 + k, self.own.at[slot, p.t, p.along(k), p.y, p.c], self.z_in.at[slot, k - 1], p.above(k))

    def add(self, ref, other):
        def one(z):
            ref[z] = ref[z] + other[z]
        rows_loop(4, one)

    def stage(self, n, v):
        p, slot = self.at, lax.rem(v, REDUCE_SLOTS)
        if n == 0:
            self.core(v).start()
        elif n == 1:
            self.core(v).wait_recv()

            def one(i):
                t, z = lax.div(i, 4), lax.rem(i, 4)
                self.own[slot, t, z, :, p.c] = self.own[slot, t, z, :, p.c] + self.core_in[slot, t, z]
            rows_loop(8, one)
            self.first(v, 0).start()
            self.first(v, 1).start()
        elif n == 2:
            self.first(v, 0).wait_recv()
            self.add(self.group(v, p.first), self.first_in.at[slot, 0])
            self.second(v).start()
            self.first(v, 1).wait_recv()
            self.add(self.group(v, (p.t, p.y)), self.first_in.at[slot, 1])
        elif n == 3:
            self.second(v).wait_recv()
            self.add(self.group(v, (p.t, p.y)), self.second_in.at[slot])
            for k in (1, 2, 3):
                self.up(v, k).start()
        else:
            total = self.own[slot, p.t, p.z, p.y, p.c].astype(F32)
            for k in (1, 2, 3):
                self.up(v, k).wait_recv()
                total = total + self.z_in[slot, k - 1].astype(F32)
            self.total[v] = total
            self.core(v).wait_send()
            for n in range(2):
                self.first(v, n).wait_send()
            self.second(v).wait_send()
            for k in (1, 2, 3):
                self.up(v, k).wait_send()

    def tick(self, n):
        for st in (4, 3, 2, 1, 0):
            v = n - (REDUCE_LAGS[st - 1] if st else 0)
            place = lax.rem(v, VIRT)

            @pl.when((v >= 0) & (v < LAYERS * VIRT) & ((place < GAP[0]) | (place >= GAP[1])))
            def _(st=st, v=v):
                self.stage(st, v)


def backward_kernel(cot, valid, vec, places, perm, permt, block, w_hbm, x0_h, x1_h, n1_h, qkv_h, pw_h, o_h, n2_h, gg_h,
                    gt, block2, total, small,
                    e, sums, folded, dsum, sm_core, sm_x, sm_y, sm_z, gin,
                    wbuf, xb, n1, n2, qkv, ow, do, dqkv, acc, em, emt, n2t, pst, gst, ubuf, dub, gbuf,
                    core_in, first_in, second_in, z_in,
                    wsem, lsem, psem, gsem, rsend, rrecv, xsend, xrecv, xlocal, ssend, srecv):
    at = Place()
    t_here = at.t
    mine, theirs = half_rows(t_here), half_rows(1 - t_here)
    rs = Reduce(at, gbuf, core_in, first_in, second_in, z_in, total, rsend, rrecv)

    def fetch(g, pos):
        return pltpu.make_async_copy(w_hbm.at[g], wbuf.at[pos % 2], wsem.at[pos % 2])

    def step_unit(l, pos):
        fetch(0, pos).wait()
        if pos + 1 < NU:
            fetch(l * NU + BACK_ORDER[pos + 1], pos + 1).start()
        else:
            @pl.when(l > 0)
            def _():
                fetch((l - 1) * NU + BACK_ORDER[0], 0).start()

    def place_of(pos):
        return pos if pos < GAP[0] else pos + GAP[1] - GAP[0]

    def emit(l, pos, t, value):
        v = place_of(pos)
        gbuf[v % REDUCE_SLOTS, t] = value.astype(BF).reshape(4, 2, 2, 48, UC)
        if t == 1:
            rs.tick((LAYERS - 1 - l) * VIRT + v)

    fetch((LAYERS - 1) * NU + BACK_ORDER[0], 0).start()
    at.barrier()
    block_swap = pltpu.make_async_remote_copy(
        src_ref=block.at[theirs], dst_ref=block2.at[t_here], send_sem=xsend.at[0], recv_sem=xrecv.at[0],
        device_id=at.side(at.x_side), device_id_type=MESH)
    block_keep = pltpu.make_async_copy(block.at[mine], block2.at[t_here], xlocal.at[0])
    block_swap.start()
    block_keep.start()
    total[...] = jnp.zeros_like(total)
    e[...] = cot[...].astype(F32) * valid[0].astype(F32)
    sums[...] = jnp.zeros_like(sums)
    lanes = lax.shift_right_logical(lax.broadcasted_iota(jnp.int32, (WT, HG * HDIM), 1), 5)

    def layer(step, carry):
        l = LAYERS - 1 - step
        loads = [pltpu.make_async_copy(src.at[l], dst, lsem.at[n]) for n, (src, dst) in enumerate((
            (n2_h, n2), (x1_h, xb.at[1]), (o_h, ow), (qkv_h, qkv), (n1_h, n1), (x0_h, xb.at[0])))]
        for cp in loads:
            cp.start()

        def load_gg(k):
            return pltpu.make_async_copy(gg_h.at[l, k // 2, k % 2], gst.at[k % 2], gsem.at[k % 2])
        load_gg(0).start()
        load_gg(1).start()

        def ends(i):
            r = pl.ds(i * WT, WT)
            x = e[r]
            em[r] = x.astype(BF)
            sums[l, 2, 5:6] += jnp.sum(x, axis=0, keepdims=True)
        rows_loop(4, ends)
        emt[...] = em[...].T
        loads[0].wait()
        n2t[...] = n2[...].T
        for i in range(4):
            step_unit(l, 2 * i)
            for t in range(2):
                load_gg(2 * i + t).wait()
                ubuf[...] = nn(em[...], w2d(wbuf, 0, t))

                def act(n):
                    r = pl.ds(n * 96, 96)
                    du = (ubuf[r] * gst[t, 1, r].astype(F32)).astype(BF)
                    dub[t, r] = du
                    sums[l, t, 14 + i // 2:15 + i // 2, (i % 2) * UC:(i % 2 + 1) * UC] += jnp.sum(du.astype(F32), axis=0, keepdims=True)
                rows_loop(6, act)
                emit(l, 2 * i, t, nn(emt[...], gst[t, 0]))
                if i < 3:
                    load_gg(2 * i + t + 2).start()
            step_unit(l, 2 * i + 1)
            for t in range(2):
                y = nt(dub[t], w2d(wbuf, 1, t))
                if i == 0 and t == 0:
                    acc[...] = y
                else:
                    acc[...] += y
                emit(l, 2 * i + 1, t, nn(n2t[...], dub[t]))
        loads[1].wait()

        def ln2(i):
            r = pl.ds(i * WT, WT)
            grad, gsum, bsum = norm_back(xb[1, r], acc[r], vec[pl.ds(l * 6 + 1, 1)])
            x = e[r] + grad
            e[r] = x
            em[r] = x.astype(BF)
            sums[l, 2, 1:2] += gsum
            sums[l, 2, 4:5] += bsum
            sums[l, 2, 3:4] += jnp.sum(x, axis=0, keepdims=True)
        rows_loop(4, ln2)
        n2[...] = nn(perm[l], em[...]).astype(BF)
        emt[...] = n2[...].T
        step_unit(l, 8)
        loads[2].wait()
        for t in range(2):
            cols = slice(t * UC, (t + 1) * UC)
            do[:, cols] = nn(n2[...], w2d(wbuf, 0, t)).astype(BF)
            emit(l, 8, t, nn(emt[...], ow[:, cols]))
        loads[3].wait()

        def load_pw(it):
            w, hg = lax.div(it, NG), lax.rem(it, NG)
            return pltpu.make_async_copy(pw_h.at[l, w, pl.ds(hg * HG, HG)], pst.at[lax.rem(it, 2)], psem.at[lax.rem(it, 2)])
        load_pw(0).start()
        dsum[...] = jnp.zeros_like(dsum)

        def attend(it, c):
            w, hg = lax.div(it, NG), lax.rem(it, NG)
            r = pl.ds(pl.multiple_of(w * WT, WT), WT)
            cl = pl.ds(pl.multiple_of(hg * 128, 128), 128)
            slot = lax.rem(it, 2)

            @pl.when(it + 1 < 4 * NG)
            def _():
                load_pw(it + 1).start()
            q, k, v, d = qkv[0, r, cl], qkv[1, r, cl], qkv[2, r, cl], do[r, cl]
            qt, dt = q.T, d.T
            load_pw(it).wait()
            dq = jnp.zeros((WT, 128), F32)
            dkt, dvt = [], []
            for h in range(HG):
                pw = pst[slot, h]
                p = pw.astype(F32)
                dp = nt(jnp.where(lanes == h, d, jnp.zeros_like(d)), v)
                mean = jnp.sum(p * dp, axis=-1, keepdims=True) / jnp.sum(p, axis=-1, keepdims=True)
                ds = (p * (dp - mean)).astype(BF)
                dsum[hg * HG + h, :, :WT] += ds.astype(F32)
                hr = slice(h * HDIM, (h + 1) * HDIM)
                dvt.append(nn(dt[hr], pw))
                dkt.append(nn(qt[hr], ds))
                dq = jnp.where(lanes == h, nn(ds, k), dq)
            dqkv[0, r, cl] = (dq * SCALE).astype(BF)
            dqkv[1, r, cl] = (jnp.concatenate(dkt, axis=0) * SCALE).T.astype(BF)
            dqkv[2, r, cl] = jnp.concatenate(dvt, axis=0).T.astype(BF)

            @pl.when(lax.rem(it, 6) == 5)
            def _():
                rs.tick(step * VIRT + GAP[0] + lax.div(it, 6))
            return c
        lax.fori_loop(0, 4 * NG, attend, 0)

        def fold(h, c):
            x = jnp.zeros((WIN, UC), F32)
            for ya in range(WIN):
                x = x + pltpu.roll(dsum[h, ya * WIN:(ya + 1) * WIN, :], (WIN - 1 - ya) * WIN, 1)
            folded[h] = x
            return c
        lax.fori_loop(0, HEADS, fold, 0)
        y = jnp.zeros((2 * HEADS, PAY), F32)
        for xa in range(WIN):
            hi, lo, _ = split3(folded[:, xa, :])
            y = y + nt(jnp.concatenate([hi, lo], axis=0), fold_matrix(places[...], xa))
        y = y[:HEADS] + y[HEADS:]
        for t in range(2):
            sums[l, t, :12, :PAY] = y[t * 12:(t + 1) * 12]
        for n, j in ((0, 0), (1, 2)):
            y = jnp.sum(dqkv[j].astype(F32), axis=0, keepdims=True)
            for t in range(2):
                sums[l, t, 12 + n:13 + n, :UC] = y[:, t * UC:(t + 1) * UC]
        loads[4].wait()
        emt[...] = n1[...].T
        for j in range(3):
            step_unit(l, 9 + j)
            for t in range(2):
                cols = slice(t * UC, (t + 1) * UC)
                y = nt(dqkv[j, :, cols], w2d(wbuf, (9 + j) % 2, t))
                if j == 0 and t == 0:
                    acc[...] = y
                else:
                    acc[...] += y
                emit(l, 9 + j, t, nn(emt[...], dqkv[j, :, cols]))
        acc[...] = nn(permt[l], acc[...].astype(BF))
        loads[5].wait()

        def ln1(i):
            r = pl.ds(i * WT, WT)
            grad, gsum, bsum = norm_back(xb[0, r], acc[r], vec[pl.ds(l * 6, 1)])
            e[r] += grad
            sums[l, 2, 0:1] += gsum
            sums[l, 2, 2:3] += bsum
        rows_loop(4, ln1)
        return carry
    lax.fori_loop(0, LAYERS, layer, 0)
    em[...] = e[...].astype(BF)
    grad_swap = pltpu.make_async_remote_copy(
        src_ref=em.at[theirs], dst_ref=gin, send_sem=xsend.at[1], recv_sem=xrecv.at[1],
        device_id=at.side(at.x_side), device_id_type=MESH)
    grad_swap.start()
    gt[t_here] = e[mine]

    def small_copy(n, src, dst, device):
        return pltpu.make_async_remote_copy(src_ref=src, dst_ref=dst, send_sem=ssend.at[n], recv_sem=srecv.at[n],
                                            device_id=device, device_id_type=MESH)
    c = at.c
    core_swap = small_copy(0, sums.at[1 - c], sm_core, at.sibling())
    core_swap.start()
    base = LAYERS * VIRT
    rs.tick(base)
    core_swap.wait_recv()
    for n in range(3):
        sums[c, n] += sm_core[n]
    x_swaps = [small_copy(1, sums.at[c, 1 - t_here], sm_x.at[0], at.side(at.x_side)),
               small_copy(2, sums.at[c, 2], sm_x.at[1], at.side(at.x_side))]
    for cp in x_swaps:
        cp.start()
    rs.tick(base + 1)
    for cp in x_swaps:
        cp.wait_recv()
    sm_y[0, 0] = sums[c, t_here] + sm_x[0]
    sm_y[0, 1] = sums[c, 2] + sm_x[1]
    y_swap = small_copy(3, sm_y.at[0], sm_y.at[1], at.side(at.y_side))
    y_swap.start()
    rs.tick(base + 2)
    y_swap.wait_recv()
    sm_z[at.z] = sm_y[0] + sm_y[1]
    z_swaps = [small_copy(3 + k, sm_z.at[at.z], sm_z.at[at.z], at.above(k)) for k in (1, 2, 3)]
    for cp in z_swaps:
        cp.start()
    rs.tick(base + 3)
    for cp in z_swaps:
        cp.wait_recv()
    small[c] = (sm_z[0] + sm_z[1]) + (sm_z[2] + sm_z[3])
    last = small_copy(7, small.at[c], small.at[c], at.sibling())
    last.start()
    grad_swap.wait()
    gt[1 - t_here] = gin[...].astype(F32)
    for n in range(4, REDUCE_LAGS[-1]):
        rs.tick(base + n)
    last.wait()
    for cp in [core_swap, y_swap] + x_swaps + z_swaps:
        cp.wait_send()
    block_swap.wait()
    block_keep.wait()


def backward_call(cot, valid, vec, block, w, *saved):
    perm = perm_matrices()
    permt = jnp.asarray(perm.transpose(0, 2, 1), BF)
    return pl.pallas_call(
        backward_kernel,
        out_shape=[sds((2, HALF, D), F32), sds((2, HALF, D), BF), sds((LAYERS * VIRT, 48, UC), F32),
                   sds((LAYERS, 2, 16, D), F32)],
        in_specs=[VM, SM, VM, VM, VM, VM, AN, AN] + [AN] * 8,
        out_specs=[VM, AN, VM, VM],
        scratch_shapes=[
            pltpu.VMEM((TOK, D), F32), pltpu.VMEM((LAYERS, 3, 16, D), F32), pltpu.VMEM((HEADS, WIN, UC), F32),
            pltpu.VMEM((HEADS, WT, UC), F32), pltpu.VMEM((3, 16, D), F32), pltpu.VMEM((2, 16, D), F32),
            pltpu.VMEM((2, 2, 16, D), F32), pltpu.VMEM((4, 2, 16, D), F32), pltpu.VMEM((HALF, D), BF),
            pltpu.VMEM((2, 2, 4, 2, 2, 48, UC), BF),
            pltpu.VMEM((2, TOK, D), F32), pltpu.VMEM((TOK, D), BF), pltpu.VMEM((TOK, D), BF),
            pltpu.VMEM((3, TOK, D), BF), pltpu.VMEM((TOK, D), BF), pltpu.VMEM((TOK, D), BF),
            pltpu.VMEM((3, TOK, D), BF), pltpu.VMEM((TOK, D), F32), pltpu.VMEM((TOK, D), BF),
            pltpu.VMEM((D, TOK), BF), pltpu.VMEM((D, TOK), BF), pltpu.VMEM((2, HG, WT, WT), BF),
            pltpu.VMEM((2, 2, TOK, UC), BF), pltpu.VMEM((TOK, UC), F32), pltpu.VMEM((2, TOK, UC), BF),
            pltpu.VMEM((REDUCE_SLOTS, 2, 4, 2, 2, 48, UC), BF),
            pltpu.VMEM((REDUCE_SLOTS, 2, 4, 2, 48, UC), BF), pltpu.VMEM((REDUCE_SLOTS, 2, 4, 48, UC), BF),
            pltpu.VMEM((REDUCE_SLOTS, 4, 48, UC), BF), pltpu.VMEM((REDUCE_SLOTS, 3, 48, UC), BF),
            pltpu.SemaphoreType.DMA((2,)), pltpu.SemaphoreType.DMA((6,)),
            pltpu.SemaphoreType.DMA((2,)), pltpu.SemaphoreType.DMA((2,)),
            pltpu.SemaphoreType.DMA((REDUCE_SLOTS, 7)), pltpu.SemaphoreType.DMA((REDUCE_SLOTS, 7)),
            pltpu.SemaphoreType.DMA((2,)), pltpu.SemaphoreType.DMA((2,)), pltpu.SemaphoreType.DMA((1,)),
            pltpu.SemaphoreType.DMA((8,)), pltpu.SemaphoreType.DMA((8,)),
        ],
        compiler_params=pltpu.CompilerParams(vmem_limit_bytes=62 * 2**20, collective_id=1, has_side_effects=True),
        name="backward",
    )(cot, valid, vec, fold_places(), jnp.asarray(perm, BF), permt, block, w, *saved)


def layer_norm(values, row_gain, row_shift):
    average = jnp.mean(values, axis=-1, keepdims=True)
    centred = values - average
    variance = jnp.mean(centred * centred, axis=-1, keepdims=True)
    return centred * lax.rsqrt(variance + EPSILON) * row_gain + row_shift


def gelu_exact(values):
    return jax.nn.gelu(values, approximate=False)


def to_windows(rows_data, shifted):
    slot_count = rows_data.shape[1]
    trailing = rows_data.shape[2:]
    image_grid = rows_data.reshape((SIDE, SIDE, slot_count) + trailing)
    if shifted:
        image_grid = jnp.roll(image_grid, (-SHIFT, -SHIFT), axis=(0, 1))
    image_grid = image_grid.reshape((2, WIN, 2, WIN, slot_count) + trailing)
    axes_order = (4, 0, 2, 1, 3) + tuple(range(5, 5 + len(trailing)))
    return jnp.transpose(image_grid, axes_order).reshape((slot_count, 4, WIN * WIN) + trailing)


def from_windows(window_data, shifted):
    slot_count = window_data.shape[0]
    trailing = window_data.shape[3:]
    image_grid = window_data.reshape((slot_count, 2, 2, WIN, WIN) + trailing)
    axes_order = (1, 3, 2, 4, 0) + tuple(range(5, 5 + len(trailing)))
    image_grid = jnp.transpose(image_grid, axes_order).reshape((SIDE, SIDE, slot_count) + trailing)
    if shifted:
        image_grid = jnp.roll(image_grid, (SHIFT, SHIFT), axis=(0, 1))
    return image_grid.reshape((SIDE * SIDE, slot_count) + trailing)


def plan_mask():
    places = jnp.arange(SIDE, dtype=jnp.int32)
    band_of = (places >= SIDE - WIN).astype(jnp.int32) + (places >= SIDE - SHIFT).astype(jnp.int32)
    region = band_of[:, None] * 3 + band_of[None, :]
    region = region.reshape(2, WIN, 2, WIN).transpose(0, 2, 1, 3).reshape(4, WIN * WIN)
    same_region = region[:, :, None] == region[:, None, :]
    return jnp.where(same_region, 0.0, MASK_FILL).astype(jnp.float32)


def offset_table():
    places = jnp.arange(WIN, dtype=jnp.int32)
    targets = jnp.arange(2 * WIN - 1, dtype=jnp.int32)
    offsets = places[:, None] - places[None, :] + WIN - 1
    return (targets[None, None, :] == offsets[:, :, None]).astype(jnp.float32)


def table_bias(table_rows):
    one_hot = offset_table()
    shaped = table_rows.reshape(table_rows.shape[0], 2 * WIN - 1, 2 * WIN - 1)
    spread = jnp.einsum(
        "acr,bds,hrs->habcd", one_hot, one_hot, shaped, precision=lax.Precision.HIGHEST
    )
    return spread.reshape(table_rows.shape[0], WIN * WIN, WIN * WIN)


def table_back(score_sum):
    one_hot = offset_table()
    shaped = score_sum.reshape(score_sum.shape[0], WIN, WIN, WIN, WIN)
    folded = jnp.einsum(
        "acr,bds,habcd->hrs", one_hot, one_hot, shaped, precision=lax.Precision.HIGHEST
    )
    return folded.reshape(score_sum.shape[0], RELS)


def attend_image(pieces, bias_add, scale_factor):
    queries, key_rows, value_rows = pieces
    scores = (
        jnp.einsum("wqhc,wkhc->whqk", queries, key_rows, preferred_element_type=jnp.float32)
        * scale_factor
        + bias_add
    )
    row_top = jnp.max(scores, axis=-1, keepdims=True)
    log_total = row_top + jnp.log(jnp.sum(jnp.exp(scores - row_top), axis=-1, keepdims=True))
    prob_rows = jnp.exp(scores - log_total)
    blended = jnp.einsum(
        "whqk,wkhc->wqhc",
        prob_rows.astype(jnp.bfloat16),
        value_rows,
        preferred_element_type=jnp.float32,
    )
    return (blended.astype(jnp.bfloat16), log_total[..., 0])


def attend_back(pieces, bias_add, scale_factor):
    queries, key_rows, value_rows, log_total, grad_out = pieces
    scores = (
        jnp.einsum("wqhc,wkhc->whqk", queries, key_rows, preferred_element_type=jnp.float32)
        * scale_factor
        + bias_add
    )
    prob_rows = jnp.exp(scores - log_total[..., None])
    prob_low = prob_rows.astype(jnp.bfloat16)
    grad_prob = jnp.einsum(
        "wqhc,wkhc->whqk", grad_out, value_rows, preferred_element_type=jnp.float32
    )
    grad_value = jnp.einsum(
        "whqk,wqhc->wkhc", prob_low, grad_out, preferred_element_type=jnp.float32
    ).astype(jnp.bfloat16)
    grad_score = (
        prob_rows * (grad_prob - jnp.sum(grad_prob * prob_rows, axis=-1, keepdims=True))
    ).astype(jnp.bfloat16)
    grad_query = (
        jnp.einsum("whqk,wkhc->wqhc", grad_score, key_rows, preferred_element_type=jnp.float32)
        * scale_factor
    ).astype(jnp.bfloat16)
    grad_key = (
        jnp.einsum("whqk,wqhc->wkhc", grad_score, queries, preferred_element_type=jnp.float32)
        * scale_factor
    ).astype(jnp.bfloat16)
    score_sum = jnp.sum(grad_score, axis=0, dtype=jnp.float32)
    return (grad_query, grad_key, grad_value, score_sum)


def shards(
    tokens,
    valid,
    cotangent,
    row_gain,
    row_bias,
    w_qkv,
    qv_bias,
    w_proj,
    w_fc1,
    fc1_bias,
    w_fc2,
    rel_table,
):
    slot_count = tokens.shape[1]
    heads_here = rel_table.shape[1]
    head_shape = (slot_count, 4, WIN * WIN, heads_here, HDIM)
    window_shape = (slot_count, 4, WIN * WIN, heads_here * HDIM)
    scale_factor = HDIM ** (-0.5)
    residual = tokens.astype(jnp.float32)
    stored = []
    for layer_index in range(LAYERS):
        shifted = layer_index % 2 == 1
        gain_rows, bias_rows, qkv_full, proj_full, fc1_full, fc2_full = (
            lax.all_gather(row_gain[layer_index], "dp", axis=1, tiled=True),
            lax.all_gather(row_bias[layer_index], "dp", axis=1, tiled=True),
            lax.all_gather(w_qkv[layer_index], "dp", axis=0, tiled=True),
            lax.all_gather(w_proj[layer_index], "dp", axis=1, tiled=True),
            lax.all_gather(w_fc1[layer_index], "dp", axis=0, tiled=True),
            lax.all_gather(w_fc2[layer_index], "dp", axis=1, tiled=True),
        )
        gain_rows = gain_rows.astype(jnp.float32)
        bias_rows = bias_rows.astype(jnp.float32)
        normed, norm_back = jax.vjp(layer_norm, residual, gain_rows[0], bias_rows[0])
        full_normed = lax.all_gather(normed.astype(jnp.bfloat16), "tensor", axis=0, tiled=True)
        projected = jnp.einsum(
            "tsd,dke->tske", full_normed, qkv_full, preferred_element_type=jnp.float32
        )
        pair_bias = qv_bias[layer_index].astype(jnp.float32)
        queries = to_windows(
            (projected[:, :, 0] + pair_bias[0]).astype(jnp.bfloat16), shifted
        ).reshape(head_shape)
        key_rows = to_windows(projected[:, :, 1].astype(jnp.bfloat16), shifted).reshape(head_shape)
        value_rows = to_windows(
            (projected[:, :, 2] + pair_bias[1]).astype(jnp.bfloat16), shifted
        ).reshape(head_shape)
        bias_add = table_bias(rel_table[layer_index])[None]
        if shifted:
            bias_add = bias_add + plan_mask()[:, None]
        blended, log_total = lax.map(
            lambda pieces: attend_image(pieces, bias_add, scale_factor),
            (queries, key_rows, value_rows),
        )
        out_rows = from_windows(blended.reshape(window_shape), shifted)
        attention = lax.psum_scatter(
            jnp.einsum(
                "tse,ed->tsd", out_rows, proj_full, preferred_element_type=jnp.float32
            ).astype(jnp.bfloat16),
            "tensor",
            scatter_dimension=0,
            tiled=True,
        ).astype(jnp.float32)
        residual_mid = residual + attention + bias_rows[1]
        normed_mid, mid_back = jax.vjp(layer_norm, residual_mid, gain_rows[1], bias_rows[2])
        mid_low = normed_mid.astype(jnp.bfloat16)
        fc1_use, fc2_use, fc1_bias_use = (fc1_full, fc2_full, fc1_bias[layer_index])
        mlp_input = lax.all_gather(mid_low, "tensor", axis=0, tiled=True)
        hidden_pre = jnp.einsum(
            "tsd,df->tsf", mlp_input, fc1_use, preferred_element_type=jnp.float32
        ) + fc1_bias_use.astype(jnp.float32)
        activated, gelu_back = jax.vjp(gelu_exact, hidden_pre)
        act_low = activated.astype(jnp.bfloat16)
        mlp_sum = lax.psum_scatter(
            jnp.einsum("tsf,fd->tsd", act_low, fc2_use, preferred_element_type=jnp.float32).astype(
                jnp.bfloat16
            ),
            "tensor",
            scatter_dimension=0,
            tiled=True,
        ).astype(jnp.float32)
        residual = residual_mid + mlp_sum + bias_rows[3]
        stored.append(
            (
                shifted,
                norm_back,
                mid_back,
                gelu_back,
                full_normed,
                queries,
                key_rows,
                value_rows,
                log_total,
                bias_add,
                out_rows,
                mlp_input,
                act_low,
                qkv_full,
                proj_full,
                fc1_use,
                fc2_use,
            )
        )
    valid_rows = valid.astype(jnp.float32)[None, :, None]
    block_out = (residual * valid_rows).astype(jnp.bfloat16)
    grad_stream = cotangent.astype(jnp.float32) * valid_rows
    results = [None] * LAYERS
    for layer_index in reversed(range(LAYERS)):
        (
            shifted,
            norm_back,
            mid_back,
            gelu_back,
            full_normed,
            queries,
            key_rows,
            value_rows,
            log_total,
            bias_add,
            out_rows,
            mlp_input,
            act_low,
            qkv_full,
            proj_full,
            fc1_use,
            fc2_use,
        ) = stored[layer_index]
        grad_bias_last = jnp.sum(grad_stream, axis=(0, 1))
        grad_low = grad_stream.astype(jnp.bfloat16)
        grad_full = lax.all_gather(grad_low, "tensor", axis=0, tiled=True)
        grad_act = jnp.einsum("tsd,fd->tsf", grad_full, fc2_use, preferred_element_type=jnp.float32)
        grad_pre = gelu_back(grad_act)[0].astype(jnp.bfloat16)
        fc2_grad = jnp.einsum("tsf,tsd->fd", act_low, grad_full, preferred_element_type=jnp.float32)
        fc1_grad = jnp.einsum(
            "tsd,tsf->df", mlp_input, grad_pre, preferred_element_type=jnp.float32
        )
        fc1_bias_grad = jnp.sum(grad_pre, axis=(0, 1), dtype=jnp.float32)
        grad_mid = lax.psum_scatter(
            jnp.einsum("tsf,df->tsd", grad_pre, fc1_use, preferred_element_type=jnp.float32).astype(
                jnp.bfloat16
            ),
            "tensor",
            scatter_dimension=0,
            tiled=True,
        ).astype(jnp.float32)
        grad_res, grad_gain_mid, grad_bias_mid = mid_back(grad_mid)
        grad_stream = grad_stream + grad_res
        grad_bias_attn = jnp.sum(grad_stream, axis=(0, 1))
        grad_attn = lax.all_gather(grad_stream.astype(jnp.bfloat16), "tensor", axis=0, tiled=True)
        proj_grad = jnp.einsum(
            "tse,tsd->ed", out_rows, grad_attn, preferred_element_type=jnp.float32
        )
        grad_out = jnp.einsum(
            "tsd,ed->tse", grad_attn, proj_full, preferred_element_type=jnp.float32
        ).astype(jnp.bfloat16)
        grad_out = to_windows(grad_out, shifted).reshape(head_shape)
        grad_query, grad_key, grad_value, score_sums = lax.map(
            lambda pieces: attend_back(pieces, bias_add, scale_factor),
            (queries, key_rows, value_rows, log_total, grad_out),
        )
        table_grad = table_back(jnp.sum(score_sums, axis=0))
        grad_qkv = jnp.stack(
            [
                from_windows(member.reshape(window_shape), shifted)
                for member in (grad_query, grad_key, grad_value)
            ],
            axis=2,
        )
        qv_grad = jnp.stack(
            [
                jnp.sum(grad_qkv[:, :, 0], axis=(0, 1), dtype=jnp.float32),
                jnp.sum(grad_qkv[:, :, 2], axis=(0, 1), dtype=jnp.float32),
            ]
        )
        qkv_grad = jnp.einsum(
            "tsd,tske->dke", full_normed, grad_qkv, preferred_element_type=jnp.float32
        )
        grad_normed = lax.psum_scatter(
            jnp.einsum(
                "tske,dke->tsd", grad_qkv, qkv_full, preferred_element_type=jnp.float32
            ).astype(jnp.bfloat16),
            "tensor",
            scatter_dimension=0,
            tiled=True,
        ).astype(jnp.float32)
        grad_res, grad_gain_first, grad_bias_first = norm_back(grad_normed)
        grad_stream = grad_stream + grad_res
        gain_grads = jnp.stack([grad_gain_first, grad_gain_mid])
        bias_grads = jnp.stack([grad_bias_first, grad_bias_attn, grad_bias_mid, grad_bias_last])
        gain_grads, bias_grads = lax.psum((gain_grads, bias_grads), "tensor")
        shard_grads = (
            lax.psum_scatter(
                gain_grads.astype(jnp.bfloat16), "dp", scatter_dimension=1, tiled=True
            ).astype(jnp.float32),
            lax.psum_scatter(
                bias_grads.astype(jnp.bfloat16), "dp", scatter_dimension=1, tiled=True
            ).astype(jnp.float32),
            lax.psum_scatter(
                qkv_grad.astype(jnp.bfloat16), "dp", scatter_dimension=0, tiled=True
            ).astype(jnp.float32),
            lax.psum_scatter(
                proj_grad.astype(jnp.bfloat16), "dp", scatter_dimension=1, tiled=True
            ).astype(jnp.float32),
            lax.psum_scatter(
                fc1_grad.astype(jnp.bfloat16), "dp", scatter_dimension=0, tiled=True
            ).astype(jnp.float32),
            lax.psum_scatter(
                fc2_grad.astype(jnp.bfloat16), "dp", scatter_dimension=1, tiled=True
            ).astype(jnp.float32),
        )
        small_grads = lax.psum((qv_grad, fc1_bias_grad, table_grad), "dp")
        results[layer_index] = tuple(shard_grads) + tuple(small_grads)
    stacked = [
        jnp.stack([results[which_layer][member] for which_layer in range(LAYERS)])
        for member in range(9)
    ]
    (
        grad_row_gain,
        grad_row_bias,
        grad_w_qkv,
        grad_w_proj,
        grad_w_fc1,
        grad_w_fc2,
        grad_qv_bias,
        grad_fc1_bias,
        grad_rel_table,
    ) = stacked
    return (
        block_out,
        grad_stream,
        grad_row_gain,
        grad_row_bias,
        grad_w_qkv,
        grad_qv_bias,
        grad_w_proj,
        grad_w_fc1,
        grad_fc1_bias,
        grad_w_fc2,
        grad_rel_table,
    )


def unit_stack(w_qkv, w_proj, w_fc1, w_fc2):
    layers, rows = w_qkv.shape[:2]
    qkv = jnp.transpose(w_qkv, (0, 2, 1, 3))
    proj = jnp.swapaxes(w_proj, 1, 2)[:, None]
    fc1 = jnp.transpose(w_fc1.reshape(layers, rows, 4, UC), (0, 2, 1, 3))
    fc2 = jnp.transpose(w_fc2.reshape(layers, 4, UC, rows), (0, 1, 3, 2))
    ff = jnp.stack([fc1, fc2], axis=2).reshape(layers, 8, rows, UC)
    return jnp.concatenate([qkv, proj, ff], axis=1).reshape(layers * NU, rows, UC)


def unit_split(units):
    rows = units.shape[1]
    units = units.reshape(LAYERS, VIRT, rows, UC)[::-1]
    back = [p if p < GAP[0] else p + GAP[1] - GAP[0] for p in range(NU)]
    units = jnp.stack([units[:, back[BACK_ORDER.index(u)]] for u in range(NU)], axis=1)
    qkv = jnp.transpose(units[:, :3], (0, 2, 1, 3))
    proj = jnp.swapaxes(units[:, 3], 1, 2)
    ff = units[:, 4:].reshape(LAYERS, 4, 2, rows, UC)
    fc1 = jnp.transpose(ff[:, :, 0], (0, 2, 1, 3)).reshape(LAYERS, rows, 4 * UC)
    fc2 = jnp.transpose(ff[:, :, 1], (0, 1, 3, 2)).reshape(LAYERS, 4 * UC, rows)
    return qkv, proj, fc1, fc2


def image_shards(tokens, valid, cotangent, row_gain, row_bias, w_qkv, qv_bias, w_proj, w_fc1, fc1_bias, w_fc2, rel_table):
    t, d = lax.axis_index("tensor"), lax.axis_index("dp")
    here = lax.dynamic_slice(valid, (t,), (1,))
    shard = unit_stack(w_qkv, w_proj, w_fc1, w_fc2)
    vecs = jnp.concatenate([row_gain, row_bias], axis=1).reshape(LAYERS * 6, 48)
    vshard = jnp.pad(vecs.T, ((0, 0), (0, 128 - LAYERS * 6)))[None]
    rows = jnp.concatenate([qv_bias.reshape(2 * LAYERS, UC), fc1_bias.reshape(4 * LAYERS, UC)]).astype(F32)
    pay = jnp.concatenate([jnp.pad(rows, ((0, 4), (0, PAY - UC))),
                           jnp.pad(rel_table.reshape(LAYERS * 12, RELS), ((0, 0), (0, PAY - RELS)))])
    block, vec, cot, w, *saved = forward_call(
        jnp.swapaxes(tokens, 0, 1), jnp.swapaxes(cotangent, 0, 1), here, vshard, pay, shard)
    gt, block, total, small = backward_call(cot, here, vec, block, w, *saved)
    qkv_g, proj_g, fc1_g, fc2_g = unit_split(total)
    rowg = lax.dynamic_slice(small[:, 1], (0, 0, d * 48), (LAYERS, 6, 48))
    own = small[:, 0]
    return (jnp.swapaxes(block, 0, 1), jnp.swapaxes(gt, 0, 1), rowg[:, :2], rowg[:, 2:], qkv_g, own[:, 12:14, :UC],
            proj_g, fc1_g, own[:, 14:16].reshape(LAYERS, 4 * UC), fc2_g, own[:, :12, :RELS])


def solution(mesh):
    whole_images = mesh.shape["tensor"] == 2 and mesh.shape["dp"] == 16
    return jax.shard_map(
        image_shards if whole_images else shards,
        mesh=mesh,
        in_specs=(
            P("tensor", "dp", None),
            P("dp"),
            P("tensor", "dp", None),
            P(None, None, "dp"),
            P(None, None, "dp"),
            P(None, "dp", None, "tensor"),
            P(None, None, "tensor"),
            P(None, "tensor", "dp"),
            P(None, "dp", "tensor"),
            P(None, "tensor"),
            P(None, "tensor", "dp"),
            P(None, "tensor", None),
        ),
        out_specs=(
            P("tensor", "dp", None),
            P("tensor", "dp", None),
            P(None, None, "dp"),
            P(None, None, "dp"),
            P(None, "dp", None, "tensor"),
            P(None, None, "tensor"),
            P(None, "tensor", "dp"),
            P(None, "dp", "tensor"),
            P(None, "tensor"),
            P(None, "tensor", "dp"),
            P(None, "tensor", None),
        ),
        check_vma=False,
    )
```

```python
import functools
import numpy as np
import jax
import jax.numpy as jnp
from jax import lax
from jax.experimental import pallas as pl
from jax.experimental.pallas import tpu as pltpu
from jax.sharding import PartitionSpec as P

WIN = 12
LAYERS = 2
HDIM = 32
SIDE = 24
SHIFT = 6
RELS = 529
EPSILON = 1e-05
MASK_FILL = -100.0

D = 768
HEADS = 24
FF = 3072
TOK = 576
WT = 144
UC = 384
NU = 12
HG = 4
NG = HEADS // HG
SCALE = HDIM ** -0.5
BF = jnp.bfloat16
F32 = jnp.float32


def nn(a, b):
    return lax.dot_general(a, b, (((1,), (0,)), ((), ())), preferred_element_type=F32)


def nt(a, b):
    return lax.dot_general(a, b, (((1,), (1,)), ((), ())), preferred_element_type=F32)


def norm_parts(x):
    mean = jnp.mean(x, axis=-1, keepdims=True)
    c = x - mean
    var = jnp.mean(c * c, axis=-1, keepdims=True)
    rstd = lax.rsqrt(var + EPSILON)
    return c * rstd, rstd


def gelu_parts(u):
    phi_big = 0.5 * (1.0 + lax.erf(u * (0.5 ** 0.5)))
    phi = jnp.exp(-0.5 * u * u) * (1.0 / (2.0 * np.pi) ** 0.5)
    return u * phi_big, phi_big + u * phi


def window_order():
    out = []
    for shift in (0, SHIFT):
        p = np.arange(SIDE)
        src = (p + shift) % SIDE
        grid = src[:, None] * SIDE + src[None, :]
        grid = grid.reshape(2, WIN, 2, WIN).transpose(0, 2, 1, 3).reshape(TOK)
        out.append(grid)
    return np.stack(out)


def perm_matrices():
    order = window_order()
    return (order[:, :, None] == np.arange(TOK)[None, None, :]).astype(np.float32)


def shift_mask():
    places = np.arange(SIDE)
    band_of = (places >= SIDE - WIN).astype(np.int32) + (places >= SIDE - SHIFT).astype(np.int32)
    region = band_of[:, None] * 3 + band_of[None, :]
    region = region.reshape(2, WIN, 2, WIN).transpose(0, 2, 1, 3).reshape(4, WT)
    same = region[:, :, None] == region[:, None, :]
    masked = np.where(same, 0.0, MASK_FILL).astype(np.float32)
    return np.tile(np.stack([np.zeros_like(masked), masked]), (1, 1, 1, HG))


def rows_loop(n, body):
    def step(i, c):
        body(i)
        return c
    lax.fori_loop(0, n, step, 0)


def w2d(wbuf, slot):
    return wbuf[slot].reshape(D, 2 * UC)


class Fetch:
    def __init__(self, w_hbm, wbuf, sem, g, slot):
        self.copies = [pltpu.make_async_copy(w_hbm.at[g, t], wbuf.at[slot, :, :, :, :, t * UC:(t + 1) * UC], sem.at[slot, t])
                       for t in range(2)]

    def start(self):
        for cp in self.copies:
            cp.start()

    def wait(self):
        for cp in self.copies:
            cp.wait()


class Place:
    def __init__(self):
        d, self.t = lax.axis_index("dp"), lax.axis_index("tensor")
        self.z = lax.div(d, 4)
        self.y = lax.rem(lax.div(d, 2), 2)
        self.c = lax.rem(d, 2)
        t, y, even = self.t, self.y, self.c == 0
        self.x_side, self.y_side = (1 - t, y), (t, 1 - y)
        self.first = tuple(jnp.where(even, a, b) for a, b in zip(self.x_side, self.y_side))
        self.second = tuple(jnp.where(even, b, a) for a, b in zip(self.x_side, self.y_side))
        self.diagonal = (1 - t, 1 - y)

    def device(self, z, ty, c):
        return {"dp": (z * 2 + ty[1]) * 2 + c, "tensor": ty[0]}

    def side(self, ty):
        return self.device(self.z, ty, self.c)

    def along(self, k):
        return lax.rem(self.z + k, 4)

    def above(self, k):
        return self.device(self.along(k), (self.t, self.y), self.c)

    def sibling(self):
        return self.device(self.z, (self.t, self.y), 1 - self.c)

    def barrier(self):
        sem = pltpu.get_barrier_semaphore()
        peers = [self.above(k) for k in (1, 2, 3)] + [self.side(self.x_side), self.side(self.y_side), self.sibling()]
        for peer in peers:
            pl.semaphore_signal(sem, inc=1, device_id=peer, device_id_type=MESH)
        pl.semaphore_wait(sem, len(peers))


MESH = pl.DeviceIdType.MESH
GATHER_LAGS = (2, 4, 6, 7)
GATHER_SEMS = 12
TICK_EVERY = 6


class Gather:
    def __init__(self, at, shard, whole, send, recv, local, units):
        self.at, self.shard, self.whole, self.units = at, shard, whole, units
        self.send, self.recv, self.local = send, recv, local

    def copy(self, g, n, src, dst, device):
        slot = lax.rem(g, GATHER_SEMS) if self.units > 1 else 0
        return pltpu.make_async_remote_copy(
            src_ref=src, dst_ref=dst, send_sem=self.send.at[slot, n], recv_sem=self.recv.at[slot, n],
            device_id=device, device_id_type=MESH)

    def mine(self, g):
        p = self.at
        return pltpu.make_async_copy(self.shard.at[g], self.whole.at[g, p.t, p.z, p.y, p.c],
                                     self.local.at[lax.rem(g, GATHER_SEMS) if self.units > 1 else 0])

    def up(self, g, k):
        p = self.at
        return self.copy(g, k - 1, self.shard.at[g], self.whole.at[g, p.t, p.z, p.y, p.c], p.above(k))

    def group(self, g, n, ty, to):
        ref = self.whole.at[g, ty[0], :, ty[1], self.at.c]
        return self.copy(g, n, ref, ref, self.at.side(to))

    def first(self, g):
        return self.group(g, 3, (self.at.t, self.at.y), self.at.first)

    def second(self, g):
        return self.group(g, 4, (self.at.t, self.at.y), self.at.second)

    def onward(self, g):
        return self.group(g, 5, self.at.first, self.at.second)

    def core(self, g):
        ref = self.whole.at[g, :, :, :, self.at.c]
        return self.copy(g, 6, ref, ref, self.at.sibling())

    def stage(self, n, g):
        if n == 0:
            self.mine(g).start()
            for k in (1, 2, 3):
                self.up(g, k).start()
        elif n == 1:
            self.mine(g).wait()
            for k in (1, 2, 3):
                self.up(g, k).wait_recv()
            self.first(g).start()
            self.second(g).start()
        elif n == 2:
            self.first(g).wait_recv()
            self.onward(g).start()
        elif n == 3:
            self.second(g).wait_recv()
            self.onward(g).wait_recv()
            self.core(g).start()
        else:
            self.core(g).wait()
            for k in (1, 2, 3):
                self.up(g, k).wait_send()
            self.first(g).wait_send()
            self.second(g).wait_send()
            self.onward(g).wait_send()

    def tick(self, n):
        for st in (4, 3, 2, 1, 0):
            g = n - (GATHER_LAGS[st - 1] if st else 0)
            if isinstance(g, int):
                if 0 <= g < self.units:
                    self.stage(st, g)
            else:
                @pl.when((g >= 0) & (g < self.units))
                def _(st=st, g=g):
                    self.stage(st, g)


def fold_places():
    lane = np.arange(UC)
    j, xa = lane // WIN, lane % WIN
    return np.where(j < 2 * WIN - 1, j * (2 * WIN - 1) + xa + WIN - 1, -4 * PAY).astype(np.int32)[None]


def fold_matrix(places, xb):
    rows = lax.broadcasted_iota(jnp.int32, (PAY, UC), 0)
    return jnp.where(rows == places - xb, 1.0, 0.0).astype(BF)


def split3(x):
    hi = x.astype(BF)
    rest = x - hi.astype(F32)
    mid = rest.astype(BF)
    return hi, mid, (rest - mid.astype(F32)).astype(BF)


HT = HG * WT
CHUNKS = [slice(i, min(i + 128, HT)) for i in range(0, HT, 128)]


def by_head(x, lanes):
    return jnp.concatenate([jnp.where(lanes == h, x, jnp.zeros_like(x)) for h in range(HG)], axis=0)


def own_blocks(x):
    return jnp.concatenate([x[h * HDIM:(h + 1) * HDIM, h * WT:(h + 1) * WT] for h in range(HG)], axis=0).T


def half_rows(t):
    return pl.ds(pl.multiple_of(t * HALF, HALF), HALF)


def forward_kernel(tok, cot, valid, vshard, pay, places, mask, perm, permt, shard,
                   out, vec, cot_h, w_hbm, x0_h, x1_h, n1_h, qkv_h, pw_h, o_h, n2_h, gg_h,
                   wbuf, x0, x1, n1, qkv, ow, n2, acc, pst, gst, ubuf,
                   xin, vall, pays, ext, bias, scores,
                   wsem, ssem, psem, gsem, gsend, grecv, glocal, vsend, vrecv, vlocal, xsend, xrecv, xlocal):
    at = Place()
    ag = Gather(at, shard, w_hbm, gsend, grecv, glocal, LAYERS * NU)
    vg = Gather(at, vshard, vall, vsend, vrecv, vlocal, 1)
    at.barrier()
    lag = GATHER_LAGS[-1]
    t = at.t
    mine, theirs = half_rows(t), half_rows(1 - t)
    swaps, keeps = [], []
    for n, (src, here, src_keep) in enumerate((
            (tok.at[1 - t], xin.at[mine], tok.at[t]),
            (pay, pays.at[t], pay),
            (cot.at[1 - t], cot_h.at[mine], cot.at[t]))):
        swaps.append(pltpu.make_async_remote_copy(
            src_ref=src, dst_ref=here, send_sem=xsend.at[n], recv_sem=xrecv.at[n],
            device_id=at.side(at.x_side), device_id_type=MESH))
        keeps.append(pltpu.make_async_copy(src_keep, here, xlocal.at[n]))
    for n in range(2):
        swaps[n].start()
        keeps[n].start()
    for n in range(lag + 1):
        vg.tick(n)
        ag.tick(n)
        if n == 0:
            swaps[1].wait()
            keeps[1].wait()
            table = jnp.concatenate([pays[0, 16:40], pays[1, 16:40]], axis=0)
            parts = jnp.concatenate(split3(table), axis=0)
            for xa in range(WIN):
                y = nn(parts, fold_matrix(places[...], xa))
                ext[:, xa, :] = y[:48] + y[48:96] + y[96:]
    def spread(i, c):
        half, l, g = lax.div(i, 6), lax.rem(lax.div(i, 3), 2), lax.rem(i, 3)
        for h in range(HG):
            x = ext[half * 24 + l * 12 + g * HG + h]
            for yb in range(WIN):
                off = (WIN - 1 - yb) * WIN
                bias[l, half * 3 + g, yb * WIN:(yb + 1) * WIN, h * WT:(h + 1) * WT] = x[:, off:off + WT]
        return c
    lax.fori_loop(0, 12, spread, 0)
    vec[...] = vall[0, 0].reshape(D, 128).astype(F32).T[:16]
    swaps[0].wait()
    keeps[0].wait()

    def both(row):
        return jnp.concatenate([pays[0, pl.ds(row, 1), :UC], pays[1, pl.ds(row, 1), :UC]], axis=1)

    def vrow(l, i):
        return vec[pl.ds(l * 6 + i, 1)]

    def fetch(g, u):
        return Fetch(w_hbm, wbuf, wsem, g, u % 2)

    def tick_base(l, u):
        inside = 4 * NG // TICK_EVERY
        return lag + 1 + l * (NU + inside) + u + (inside if u > 3 else 0)

    def step_unit(l, u):
        g = l * NU + u
        fetch(g, u).wait()
        ag.tick(tick_base(l, u) + (4 * NG // TICK_EVERY if u == 3 else 0))

        @pl.when(g + 1 < LAYERS * NU)
        def _():
            fetch(g + 1, u + 1).start()

    fetch(0, 0).start()
    x0[0] = xin[...].astype(F32)
    lanes = lax.shift_right_logical(lax.broadcasted_iota(jnp.int32, (WT, HG * HDIM), 1), 5)

    def layer(l, carry):
        x0_l, x1_l, n1_l, n2_l, ow_l = x0.at[l], x1.at[l], n1.at[l], n2.at[l], ow.at[l]

        def ln1(i):
            r = pl.ds(i * WT, WT)
            xh, _ = norm_parts(x0_l[r])
            ow_l[r] = (xh * vrow(l, 0) + vrow(l, 2)).astype(BF)
        rows_loop(4, ln1)
        n1_l[...] = nn(perm[l], ow_l[...]).astype(BF)
        for j in range(3):
            step_unit(l, j)
            y = nn(n1_l[...], w2d(wbuf, j % 2))
            if j != 1:
                y = y + both(l * 2 + j // 2)
            qkv[l, j] = y.astype(BF)

        def attend(it, c):
            w, hg = lax.div(it, NG), lax.rem(it, NG)
            r = pl.ds(pl.multiple_of(w * WT, WT), WT)
            cl = pl.ds(pl.multiple_of(hg * 128, 128), 128)
            slot = lax.rem(it, 2)
            q, k, v = qkv[l, 0, r, cl], qkv[l, 1, r, cl], qkv[l, 2, r, cl]
            put = pltpu.make_async_copy(pst.at[slot], pw_h.at[l, w, hg], psem.at[slot])

            @pl.when((it >= 2) | (l > 0))
            def _():
                put.wait()
            scores[...] = nt(k, by_head(q, lanes))
            for ch in CHUNKS:
                x = scores[:, ch] * SCALE + bias[l, hg, :, ch] + mask[l, w, :, ch]
                x = jnp.exp(x - jnp.max(x, axis=0, keepdims=True))
                pst[slot, :, ch] = (x * (1.0 / jnp.sum(x, axis=0, keepdims=True))).astype(BF)
            ow_l[r, cl] = own_blocks(nn(v.T, pst[slot])).astype(BF)
            put.start()

            @pl.when(lax.rem(it, TICK_EVERY) == TICK_EVERY - 1)
            def _():
                ag.tick(tick_base(l, 3) + lax.div(it, TICK_EVERY))
            return c
        lax.fori_loop(0, 4 * NG, attend, 0)

        @pl.when(l == LAYERS - 1)
        def _():
            swaps[2].start()
            keeps[2].start()
        n2_l[...] = nn(permt[l], ow_l[...]).astype(BF)
        step_unit(l, 3)
        acc[...] = nt(n2_l[...], w2d(wbuf, 1))

        def ln2(i):
            r = pl.ds(i * WT, WT)
            x = x0_l[r] + acc[r] + vrow(l, 3)
            x1_l[r] = x
            xh, _ = norm_parts(x)
            n2_l[r] = (xh * vrow(l, 1) + vrow(l, 4)).astype(BF)
            acc[r] = x + vrow(l, 5)
        rows_loop(4, ln2)
        for i in range(4):
            step_unit(l, 4 + 2 * i)
            put = pltpu.make_async_copy(gst.at[i % 2], gg_h.at[l, i], gsem.at[i % 2])
            if i > 1:
                put.wait()
            else:
                @pl.when(l > 0)
                def _():
                    put.wait()
            ubuf[...] = nn(n2_l[...], w2d(wbuf, 0)) + both(4 + l * 4 + i)

            def act(n):
                r = pl.ds(n * 48, 48)
                g, gp = gelu_parts(ubuf[r])
                gst[i % 2, 0, r] = g.astype(BF)
                gst[i % 2, 1, r] = gp.astype(BF)
            rows_loop(12, act)
            put.start()
            step_unit(l, 5 + 2 * i)
            acc[...] += nt(gst[i % 2, 0], w2d(wbuf, 1))

        for ref, dst in ((x0, x0_h), (x1, x1_h), (n1, n1_h), (qkv, qkv_h), (ow, o_h), (n2, n2_h)):
            pltpu.make_async_copy(ref.at[l], dst.at[l], ssem.at[l]).start()

        @pl.when(l == 0)
        def _():
            x0[1] = acc[...]

        @pl.when(l == 1)
        def _():
            out[...] = (acc[...] * valid[0].astype(F32)).astype(BF)
        return carry
    lax.fori_loop(0, LAYERS, layer, 0)
    for l in range(LAYERS):
        for ref, dst in ((x0, x0_h), (x1, x1_h), (n1, n1_h), (qkv, qkv_h), (ow, o_h), (n2, n2_h)):
            pltpu.make_async_copy(ref.at[l], dst.at[l], ssem.at[l]).wait()
    for s in range(2):
        pltpu.make_async_copy(pst.at[s], pw_h.at[0, 0, 0], psem.at[s]).wait()
        pltpu.make_async_copy(gst.at[s], gg_h.at[0, s], gsem.at[s]).wait()
    swaps[2].wait()
    keeps[2].wait()


def sds(shape, dtype):
    return jax.ShapeDtypeStruct(shape, dtype)


VM = pl.BlockSpec(memory_space=pltpu.VMEM)
AN = pl.BlockSpec(memory_space=pl.ANY)
SM = pl.BlockSpec(memory_space=pltpu.SMEM)

SAVED = [
    sds((LAYERS, TOK, D), F32), sds((LAYERS, TOK, D), F32), sds((LAYERS, TOK, D), BF),
    sds((LAYERS, 3, TOK, D), BF), sds((LAYERS, 4, NG, WT, HT), BF),
    sds((LAYERS, TOK, D), BF), sds((LAYERS, TOK, D), BF), sds((LAYERS, 4, 2, TOK, 2 * UC), BF),
]


def forward_call(tok, cot, valid, vshard, pay, shard):
    perm = perm_matrices()
    permt = jnp.asarray(perm.transpose(0, 2, 1), BF)
    return pl.pallas_call(
        forward_kernel,
        out_shape=[sds((TOK, D), BF), sds((16, D), F32), sds((TOK, D), BF),
                   sds((LAYERS * NU, 2, 4, 2, 2, 48, UC), BF)] + SAVED,
        in_specs=[AN, AN, SM, AN, AN, VM, VM, VM, VM, AN],
        out_specs=[VM, VM] + [AN] * 10,
        scratch_shapes=[
            pltpu.VMEM((2, 4, 2, 2, 48, 2 * UC), BF),
            pltpu.VMEM((2, TOK, D), F32), pltpu.VMEM((2, TOK, D), F32),
            pltpu.VMEM((2, TOK, D), BF), pltpu.VMEM((2, 3, TOK, D), BF),
            pltpu.VMEM((2, TOK, D), BF), pltpu.VMEM((2, TOK, D), BF),
            pltpu.VMEM((TOK, D), F32), pltpu.VMEM((2, WT, HT), BF),
            pltpu.VMEM((2, 2, TOK, 2 * UC), BF), pltpu.VMEM((TOK, 2 * UC), F32),
            pltpu.VMEM((TOK, D), BF), pltpu.VMEM((1, 2, 4, 2, 2, 48, 128), BF),
            pltpu.VMEM((2, 40, PAY), F32), pltpu.VMEM((48, WIN, UC), F32),
            pltpu.VMEM((LAYERS, NG, WT, HT), F32), pltpu.VMEM((WT, HT), F32),
            pltpu.SemaphoreType.DMA((2, 2)), pltpu.SemaphoreType.DMA((2,)),
            pltpu.SemaphoreType.DMA((2,)), pltpu.SemaphoreType.DMA((2,)),
            pltpu.SemaphoreType.DMA((GATHER_SEMS, 7)), pltpu.SemaphoreType.DMA((GATHER_SEMS, 7)),
            pltpu.SemaphoreType.DMA((GATHER_SEMS,)),
            pltpu.SemaphoreType.DMA((1, 7)), pltpu.SemaphoreType.DMA((1, 7)), pltpu.SemaphoreType.DMA((1,)),
            pltpu.SemaphoreType.DMA((3,)), pltpu.SemaphoreType.DMA((3,)), pltpu.SemaphoreType.DMA((3,)),
        ],
        compiler_params=pltpu.CompilerParams(vmem_limit_bytes=60 * 2**20, collective_id=0, has_side_effects=True),
        name="forward",
    )(tok, cot, valid, vshard, pay, fold_places(), shift_mask(), jnp.asarray(perm, BF), permt, shard)


BACK_ORDER = (5, 4, 7, 6, 9, 8, 11, 10, 3, 0, 1, 2)


def norm_back(x, dn, gain):
    xh, rstd = norm_parts(x)
    dx = dn * gain
    grad = rstd * (dx - jnp.mean(dx, axis=-1, keepdims=True)
                   - xh * jnp.mean(dx * xh, axis=-1, keepdims=True))
    return grad, jnp.sum(dn * xh, axis=0, keepdims=True), jnp.sum(dn, axis=0, keepdims=True)


REDUCE_SLOTS = NU
CORE_SLOTS = 4
PAY = 640
HALF = TOK // 2
VIRT = 18
GAP = (9, 15)
REDUCE_LAGS = (1, 5, 8, 11)


class Reduce:
    def __init__(self, at, own, core_in, first_in, second_in, z_in, total, send, recv):
        self.at, self.own, self.total = at, own, total
        self.core_in, self.first_in, self.second_in, self.z_in = core_in, first_in, second_in, z_in
        self.send, self.recv = send, recv

    def slot(self, v):
        place = lax.rem(v, VIRT)
        return jnp.where(place < GAP[0], place, place - (GAP[1] - GAP[0]))

    def copy(self, v, n, src, dst, device):
        slot = self.slot(v)
        return pltpu.make_async_remote_copy(
            src_ref=src, dst_ref=dst, send_sem=self.send.at[slot, n], recv_sem=self.recv.at[slot, n],
            device_id=device, device_id_type=MESH)

    def core(self, v):
        slot = lax.rem(self.slot(v), CORE_SLOTS)
        return self.copy(v, 0, self.own.at[REDUCE_SLOTS + slot], self.core_in.at[slot], self.at.sibling())

    def put(self, v, value):
        value = value.astype(BF)
        mine, other = self.slot(v), REDUCE_SLOTS + lax.rem(self.slot(v), CORE_SLOTS)
        for t in range(2):
            x = value[:, t * UC:(t + 1) * UC].reshape(4, 2, 2, 48, UC)
            for k in range(2):
                self.own[jnp.where(self.at.c == k, mine, other), t] = x[:, :, k]

    def group(self, v, ty):
        return self.own.at[self.slot(v), ty[0], :, ty[1]]

    def first(self, v, n):
        p = self.at
        ty = p.diagonal if n == 0 else p.second
        return self.copy(v, 1 + n, self.group(v, ty), self.first_in.at[self.slot(v), n], p.side(p.second))

    def second(self, v):
        p = self.at
        return self.copy(v, 3, self.group(v, p.first), self.second_in.at[self.slot(v)], p.side(p.first))

    def up(self, v, k):
        p, slot = self.at, self.slot(v)
        return self.copy(v, 3 + k, self.own.at[slot, p.t, p.along(k), p.y], self.z_in.at[slot, k - 1], p.above(k))

    def add(self, ref, other):
        def one(z):
            ref[z] = ref[z] + other[z]
        rows_loop(4, one)

    def stage(self, n, v):
        p, slot = self.at, self.slot(v)
        if n == 0:
            self.core(v).start()
        elif n == 1:
            self.core(v).wait()

            def one(i):
                t, z = lax.div(i, 4), lax.rem(i, 4)
                self.own[slot, t, z] = self.own[slot, t, z] + self.core_in[lax.rem(self.slot(v), CORE_SLOTS), t, z]
            rows_loop(8, one)
            self.first(v, 0).start()
            self.first(v, 1).start()
        elif n == 2:
            self.first(v, 0).wait_recv()
            self.add(self.group(v, p.first), self.first_in.at[slot, 0])
            self.second(v).start()
            self.first(v, 1).wait_recv()
            self.add(self.group(v, (p.t, p.y)), self.first_in.at[slot, 1])
        elif n == 3:
            self.second(v).wait_recv()
            self.add(self.group(v, (p.t, p.y)), self.second_in.at[slot])
            for k in (1, 2, 3):
                self.up(v, k).start()
        else:
            total = self.own[slot, p.t, p.z, p.y].astype(F32)
            for k in (1, 2, 3):
                self.up(v, k).wait_recv()
                total = total + self.z_in[slot, k - 1].astype(F32)
            self.total[lax.div(v, VIRT) * NU + slot] = total
            for n in range(2):
                self.first(v, n).wait_send()
            self.second(v).wait_send()
            for k in (1, 2, 3):
                self.up(v, k).wait_send()

    def tick(self, n):
        for st in (4, 3, 2, 1, 0):
            v = n - (REDUCE_LAGS[st - 1] if st else 0)
            place = lax.rem(v, VIRT)

            @pl.when((v >= 0) & (v < LAYERS * VIRT) & ((place < GAP[0]) | (place >= GAP[1])))
            def _(st=st, v=v):
                self.stage(st, v)


def backward_kernel(cot, valid, vec, places, perm, permt, block, w_hbm, x0_h, x1_h, n1_h, qkv_h, pw_h, o_h, n2_h, gg_h,
                    gt, block2, total, small,
                    e, scores, ds, sums, folded, dsum, sm_core, sm_x, sm_y, sm_z, gin,
                    wbuf, xb, n1, n2, qkv, ow, do, dqkv, acc, em, emt, n2t, pst, gst, ubuf, dub, gbuf,
                    core_in, first_in, second_in, z_in,
                    wsem, lsem, psem, gsem, rsend, rrecv, xsend, xrecv, xlocal, ssend, srecv):
    at = Place()
    t_here = at.t
    mine, theirs = half_rows(t_here), half_rows(1 - t_here)
    rs = Reduce(at, gbuf, core_in, first_in, second_in, z_in, total, rsend, rrecv)

    def fetch(g, pos):
        return Fetch(w_hbm, wbuf, wsem, g, pos % 2)

    def step_unit(l, pos):
        fetch(0, pos).wait()
        if pos + 1 < NU:
            fetch(l * NU + BACK_ORDER[pos + 1], pos + 1).start()
        else:
            @pl.when(l > 0)
            def _():
                fetch((l - 1) * NU + BACK_ORDER[0], 0).start()

    def place_of(pos):
        return pos if pos < GAP[0] else pos + GAP[1] - GAP[0]

    def emit(l, pos, value):
        v = (LAYERS - 1 - l) * VIRT + place_of(pos)
        rs.put(v, value)
        rs.tick(v)

    fetch((LAYERS - 1) * NU + BACK_ORDER[0], 0).start()
    at.barrier()
    block_swap = pltpu.make_async_remote_copy(
        src_ref=block.at[theirs], dst_ref=block2.at[t_here], send_sem=xsend.at[0], recv_sem=xrecv.at[0],
        device_id=at.side(at.x_side), device_id_type=MESH)
    block_keep = pltpu.make_async_copy(block.at[mine], block2.at[t_here], xlocal.at[0])
    block_swap.start()
    block_keep.start()
    total[...] = jnp.zeros_like(total)
    e[...] = cot[...].astype(F32) * valid[0].astype(F32)
    sums[...] = jnp.zeros_like(sums)
    lanes = lax.shift_right_logical(lax.broadcasted_iota(jnp.int32, (WT, HG * HDIM), 1), 5)

    def layer(step, carry):
        l = LAYERS - 1 - step
        loads = [pltpu.make_async_copy(src.at[l], dst, lsem.at[n]) for n, (src, dst) in enumerate((
            (n2_h, n2), (x1_h, xb.at[1]), (o_h, ow), (qkv_h, qkv), (n1_h, n1), (x0_h, xb.at[0])))]
        for cp in loads:
            cp.start()

        def load_gg(k):
            return pltpu.make_async_copy(gg_h.at[l, k], gst.at[k % 2], gsem.at[k % 2])
        load_gg(0).start()
        load_gg(1).start()

        def ends(i):
            r = pl.ds(i * WT, WT)
            x = e[r]
            em[r] = x.astype(BF)
            sums[l, 2, 5:6] += jnp.sum(x, axis=0, keepdims=True)
        rows_loop(4, ends)
        emt[...] = em[...].T
        loads[0].wait()
        n2t[...] = n2[...].T
        for i in range(4):
            step_unit(l, 2 * i)
            load_gg(i).wait()
            ubuf[...] = nn(em[...], w2d(wbuf, 0))

            def act(n, c):
                r = pl.ds(n * 48, 48)
                du = (ubuf[r] * gst[i % 2, 1, r].astype(F32)).astype(BF)
                dub[r] = du
                return c + jnp.sum(du.astype(F32), axis=0, keepdims=True)
            y = lax.fori_loop(0, 12, act, jnp.zeros((1, 2 * UC), F32))
            for t in range(2):
                sums[l, t, 14 + i // 2:15 + i // 2, (i % 2) * UC:(i % 2 + 1) * UC] = y[:, t * UC:(t + 1) * UC]
            emit(l, 2 * i, nn(emt[...], gst[i % 2, 0]))
            if i < 2:
                load_gg(i + 2).start()
            step_unit(l, 2 * i + 1)
            y = nt(dub[...], w2d(wbuf, 1))
            if i == 0:
                acc[...] = y
            else:
                acc[...] += y
            emit(l, 2 * i + 1, nn(n2t[...], dub[...]))
        loads[1].wait()

        def ln2(i):
            r = pl.ds(i * WT, WT)
            grad, gsum, bsum = norm_back(xb[1, r], acc[r], vec[pl.ds(l * 6 + 1, 1)])
            x = e[r] + grad
            e[r] = x
            em[r] = x.astype(BF)
            sums[l, 2, 1:2] += gsum
            sums[l, 2, 4:5] += bsum
            sums[l, 2, 3:4] += jnp.sum(x, axis=0, keepdims=True)
        rows_loop(4, ln2)
        n2[...] = nn(perm[l], em[...]).astype(BF)
        emt[...] = n2[...].T
        step_unit(l, 8)
        loads[2].wait()
        do[...] = nn(n2[...], w2d(wbuf, 0)).astype(BF)
        emit(l, 8, nn(emt[...], ow[...]))
        loads[3].wait()

        def load_pw(it):
            w, hg = lax.div(it, NG), lax.rem(it, NG)
            return pltpu.make_async_copy(pw_h.at[l, w, hg], pst.at[lax.rem(it, 2)], psem.at[lax.rem(it, 2)])
        load_pw(0).start()
        dsum[l] = jnp.zeros((NG, WT, HT), F32)

        def attend(it, c):
            w, hg = lax.div(it, NG), lax.rem(it, NG)
            r = pl.ds(pl.multiple_of(w * WT, WT), WT)
            cl = pl.ds(pl.multiple_of(hg * 128, 128), 128)
            slot = lax.rem(it, 2)

            @pl.when(it + 1 < 4 * NG)
            def _():
                load_pw(it + 1).start()
            q, k, v, d = qkv[0, r, cl], qkv[1, r, cl], qkv[2, r, cl], do[r, cl]
            q4, d4 = by_head(q, lanes), by_head(d, lanes)
            scores[...] = nt(v, d4)
            load_pw(it).wait()
            for ch in CHUNKS:
                p = pst[slot, :, ch].astype(F32)
                x = scores[:, ch]
                mean = jnp.sum(p * x, axis=0, keepdims=True) / jnp.sum(p, axis=0, keepdims=True)
                x = (p * (x - mean)).astype(BF)
                ds[:, ch] = x
                dsum[l, hg, :, ch] += x.astype(F32)
            dqkv[0, r, cl] = (own_blocks(nn(k.T, ds[...])) * SCALE).astype(BF)
            dqkv[1, r, cl] = (nn(ds[...], q4) * SCALE).astype(BF)
            dqkv[2, r, cl] = nn(pst[slot], d4).astype(BF)

            @pl.when(lax.rem(it, 4) == 3)
            def _():
                rs.tick(step * VIRT + GAP[0] + lax.div(it, 4))
            return c
        lax.fori_loop(0, 4 * NG, attend, 0)

        for n, j in ((0, 0), (1, 2)):
            y = jnp.sum(dqkv[j].astype(F32), axis=0, keepdims=True)
            for t in range(2):
                sums[l, t, 12 + n:13 + n, :UC] = y[:, t * UC:(t + 1) * UC]
        loads[4].wait()
        emt[...] = n1[...].T
        for j in range(3):
            step_unit(l, 9 + j)
            y = nt(dqkv[j], w2d(wbuf, (9 + j) % 2))
            if j == 0:
                acc[...] = y
            else:
                acc[...] += y
            emit(l, 9 + j, nn(emt[...], dqkv[j]))
        acc[...] = nn(permt[l], acc[...].astype(BF))
        loads[5].wait()

        def ln1(i):
            r = pl.ds(i * WT, WT)
            grad, gsum, bsum = norm_back(xb[0, r], acc[r], vec[pl.ds(l * 6, 1)])
            e[r] += grad
            sums[l, 2, 0:1] += gsum
            sums[l, 2, 2:3] += bsum
        rows_loop(4, ln1)
        return carry
    lax.fori_loop(0, LAYERS, layer, 0)
    em[...] = e[...].astype(BF)
    grad_swap = pltpu.make_async_remote_copy(
        src_ref=em.at[theirs], dst_ref=gin, send_sem=xsend.at[1], recv_sem=xrecv.at[1],
        device_id=at.side(at.x_side), device_id_type=MESH)
    grad_swap.start()
    gt[t_here] = e[mine]

    base = LAYERS * VIRT

    def fold(i, c):
        for h in range(HG):
            x = jnp.zeros((2 * WIN, UC), F32)
            for pair in range(WIN // 2):
                part = dsum[lax.div(i, NG), lax.rem(i, NG), 2 * pair * WIN:2 * (pair + 1) * WIN, h * WT:(h + 1) * WT]
                part = jnp.concatenate([part, jnp.zeros((2 * WIN, UC - WT), F32)], axis=1)
                x = x + pltpu.roll(part, (WIN - 1 - 2 * pair) * WIN, 1)
            folded[i * HG + h] = x[:WIN] + pltpu.roll(x[WIN:], UC - WIN, 1)

        @pl.when(lax.rem(i, 2) == 1)
        def _():
            rs.tick(base + lax.div(i, 2))
        return c
    lax.fori_loop(0, LAYERS * NG, fold, 0)
    y = jnp.zeros((2 * LAYERS * HEADS, PAY), F32)
    for xb in range(WIN):
        hi, lo, _ = split3(folded[:, xb, :])
        y = y + nt(jnp.concatenate([hi, lo], axis=0), fold_matrix(places[...], xb))
    y = y[:LAYERS * HEADS] + y[LAYERS * HEADS:]
    for l in range(LAYERS):
        for t in range(2):
            sums[l, t, :12, :PAY] = y[l * HEADS + t * 12:l * HEADS + t * 12 + 12]

    def small_copy(n, src, dst, device):
        return pltpu.make_async_remote_copy(src_ref=src, dst_ref=dst, send_sem=ssend.at[n], recv_sem=srecv.at[n],
                                            device_id=device, device_id_type=MESH)
    c = at.c
    core_swap = small_copy(0, sums.at[1 - c], sm_core, at.sibling())
    core_swap.start()
    base = base + LAYERS * NG // 2
    rs.tick(base)
    core_swap.wait_recv()
    for n in range(3):
        sums[c, n] += sm_core[n]
    x_swaps = [small_copy(1, sums.at[c, 1 - t_here], sm_x.at[0], at.side(at.x_side)),
               small_copy(2, sums.at[c, 2], sm_x.at[1], at.side(at.x_side))]
    for cp in x_swaps:
        cp.start()
    rs.tick(base + 1)
    for cp in x_swaps:
        cp.wait_recv()
    sm_y[0, 0] = sums[c, t_here] + sm_x[0]
    sm_y[0, 1] = sums[c, 2] + sm_x[1]
    y_swap = small_copy(3, sm_y.at[0], sm_y.at[1], at.side(at.y_side))
    y_swap.start()
    rs.tick(base + 2)
    y_swap.wait_recv()
    sm_z[at.z] = (sm_y[0] + sm_y[1]).astype(BF)
    z_swaps = [small_copy(3 + k, sm_z.at[at.z], sm_z.at[at.z], at.above(k)) for k in (1, 2, 3)]
    for cp in z_swaps:
        cp.start()
    rs.tick(base + 3)
    for cp in z_swaps:
        cp.wait_recv()
    small[c] = (sm_z[0].astype(F32) + sm_z[1].astype(F32)) + (sm_z[2].astype(F32) + sm_z[3].astype(F32))
    last = small_copy(7, small.at[c], small.at[c], at.sibling())
    last.start()
    grad_swap.wait()
    gt[1 - t_here] = gin[...].astype(F32)
    for n in range(4, REDUCE_LAGS[-1] - LAYERS * NG // 2):
        rs.tick(base + n)
    last.wait()
    for cp in [core_swap, y_swap] + x_swaps + z_swaps:
        cp.wait_send()
    block_swap.wait()
    block_keep.wait()


def backward_call(cot, valid, vec, block, w, *saved):
    perm = perm_matrices()
    permt = jnp.asarray(perm.transpose(0, 2, 1), BF)
    return pl.pallas_call(
        backward_kernel,
        out_shape=[sds((2, HALF, D), F32), sds((2, HALF, D), BF), sds((LAYERS * NU, 48, UC), F32),
                   sds((LAYERS, 2, 16, D), F32)],
        in_specs=[VM, SM, VM, VM, VM, VM, AN, AN] + [AN] * 8,
        out_specs=[VM, AN, VM, VM],
        scratch_shapes=[
            pltpu.VMEM((TOK, D), F32), pltpu.VMEM((WT, HT), F32), pltpu.VMEM((WT, HT), BF),
            pltpu.VMEM((LAYERS, 3, 16, D), F32), pltpu.VMEM((LAYERS * HEADS, WIN, UC), F32),
            pltpu.VMEM((LAYERS, NG, WT, HT), F32), pltpu.VMEM((3, 16, D), F32), pltpu.VMEM((2, 16, D), F32),
            pltpu.VMEM((2, 2, 16, D), F32), pltpu.VMEM((4, 2, 16, D), BF), pltpu.VMEM((HALF, D), BF),
            pltpu.VMEM((2, 4, 2, 2, 48, 2 * UC), BF),
            pltpu.VMEM((2, TOK, D), F32), pltpu.VMEM((TOK, D), BF), pltpu.VMEM((TOK, D), BF),
            pltpu.VMEM((3, TOK, D), BF), pltpu.VMEM((TOK, D), BF), pltpu.VMEM((TOK, D), BF),
            pltpu.VMEM((3, TOK, D), BF), pltpu.VMEM((TOK, D), F32), pltpu.VMEM((TOK, D), BF),
            pltpu.VMEM((D, TOK), BF), pltpu.VMEM((D, TOK), BF), pltpu.VMEM((2, WT, HT), BF),
            pltpu.VMEM((2, 2, TOK, 2 * UC), BF), pltpu.VMEM((TOK, 2 * UC), F32), pltpu.VMEM((TOK, 2 * UC), BF),
            pltpu.VMEM((REDUCE_SLOTS + CORE_SLOTS, 2, 4, 2, 48, UC), BF),
            pltpu.VMEM((CORE_SLOTS, 2, 4, 2, 48, UC), BF), pltpu.VMEM((REDUCE_SLOTS, 2, 4, 48, UC), BF),
            pltpu.VMEM((REDUCE_SLOTS, 4, 48, UC), BF), pltpu.VMEM((REDUCE_SLOTS, 3, 48, UC), BF),
            pltpu.SemaphoreType.DMA((2, 2)), pltpu.SemaphoreType.DMA((6,)),
            pltpu.SemaphoreType.DMA((2,)), pltpu.SemaphoreType.DMA((2,)),
            pltpu.SemaphoreType.DMA((REDUCE_SLOTS, 7)), pltpu.SemaphoreType.DMA((REDUCE_SLOTS, 7)),
            pltpu.SemaphoreType.DMA((2,)), pltpu.SemaphoreType.DMA((2,)), pltpu.SemaphoreType.DMA((1,)),
            pltpu.SemaphoreType.DMA((8,)), pltpu.SemaphoreType.DMA((8,)),
        ],
        compiler_params=pltpu.CompilerParams(vmem_limit_bytes=62 * 2**20, collective_id=1, has_side_effects=True),
        name="backward",
    )(cot, valid, vec, fold_places(), jnp.asarray(perm, BF), permt, block, w, *saved)


def layer_norm(values, row_gain, row_shift):
    average = jnp.mean(values, axis=-1, keepdims=True)
    centred = values - average
    variance = jnp.mean(centred * centred, axis=-1, keepdims=True)
    return centred * lax.rsqrt(variance + EPSILON) * row_gain + row_shift


def gelu_exact(values):
    return jax.nn.gelu(values, approximate=False)


def to_windows(rows_data, shifted):
    slot_count = rows_data.shape[1]
    trailing = rows_data.shape[2:]
    image_grid = rows_data.reshape((SIDE, SIDE, slot_count) + trailing)
    if shifted:
        image_grid = jnp.roll(image_grid, (-SHIFT, -SHIFT), axis=(0, 1))
    image_grid = image_grid.reshape((2, WIN, 2, WIN, slot_count) + trailing)
    axes_order = (4, 0, 2, 1, 3) + tuple(range(5, 5 + len(trailing)))
    return jnp.transpose(image_grid, axes_order).reshape((slot_count, 4, WIN * WIN) + trailing)


def from_windows(window_data, shifted):
    slot_count = window_data.shape[0]
    trailing = window_data.shape[3:]
    image_grid = window_data.reshape((slot_count, 2, 2, WIN, WIN) + trailing)
    axes_order = (1, 3, 2, 4, 0) + tuple(range(5, 5 + len(trailing)))
    image_grid = jnp.transpose(image_grid, axes_order).reshape((SIDE, SIDE, slot_count) + trailing)
    if shifted:
        image_grid = jnp.roll(image_grid, (SHIFT, SHIFT), axis=(0, 1))
    return image_grid.reshape((SIDE * SIDE, slot_count) + trailing)


def plan_mask():
    places = jnp.arange(SIDE, dtype=jnp.int32)
    band_of = (places >= SIDE - WIN).astype(jnp.int32) + (places >= SIDE - SHIFT).astype(jnp.int32)
    region = band_of[:, None] * 3 + band_of[None, :]
    region = region.reshape(2, WIN, 2, WIN).transpose(0, 2, 1, 3).reshape(4, WIN * WIN)
    same_region = region[:, :, None] == region[:, None, :]
    return jnp.where(same_region, 0.0, MASK_FILL).astype(jnp.float32)


def offset_table():
    places = jnp.arange(WIN, dtype=jnp.int32)
    targets = jnp.arange(2 * WIN - 1, dtype=jnp.int32)
    offsets = places[:, None] - places[None, :] + WIN - 1
    return (targets[None, None, :] == offsets[:, :, None]).astype(jnp.float32)


def table_bias(table_rows):
    one_hot = offset_table()
    shaped = table_rows.reshape(table_rows.shape[0], 2 * WIN - 1, 2 * WIN - 1)
    spread = jnp.einsum(
        "acr,bds,hrs->habcd", one_hot, one_hot, shaped, precision=lax.Precision.HIGHEST
    )
    return spread.reshape(table_rows.shape[0], WIN * WIN, WIN * WIN)


def table_back(score_sum):
    one_hot = offset_table()
    shaped = score_sum.reshape(score_sum.shape[0], WIN, WIN, WIN, WIN)
    folded = jnp.einsum(
        "acr,bds,habcd->hrs", one_hot, one_hot, shaped, precision=lax.Precision.HIGHEST
    )
    return folded.reshape(score_sum.shape[0], RELS)


def attend_image(pieces, bias_add, scale_factor):
    queries, key_rows, value_rows = pieces
    scores = (
        jnp.einsum("wqhc,wkhc->whqk", queries, key_rows, preferred_element_type=jnp.float32)
        * scale_factor
        + bias_add
    )
    row_top = jnp.max(scores, axis=-1, keepdims=True)
    log_total = row_top + jnp.log(jnp.sum(jnp.exp(scores - row_top), axis=-1, keepdims=True))
    prob_rows = jnp.exp(scores - log_total)
    blended = jnp.einsum(
        "whqk,wkhc->wqhc",
        prob_rows.astype(jnp.bfloat16),
        value_rows,
        preferred_element_type=jnp.float32,
    )
    return (blended.astype(jnp.bfloat16), log_total[..., 0])


def attend_back(pieces, bias_add, scale_factor):
    queries, key_rows, value_rows, log_total, grad_out = pieces
    scores = (
        jnp.einsum("wqhc,wkhc->whqk", queries, key_rows, preferred_element_type=jnp.float32)
        * scale_factor
        + bias_add
    )
    prob_rows = jnp.exp(scores - log_total[..., None])
    prob_low = prob_rows.astype(jnp.bfloat16)
    grad_prob = jnp.einsum(
        "wqhc,wkhc->whqk", grad_out, value_rows, preferred_element_type=jnp.float32
    )
    grad_value = jnp.einsum(
        "whqk,wqhc->wkhc", prob_low, grad_out, preferred_element_type=jnp.float32
    ).astype(jnp.bfloat16)
    grad_score = (
        prob_rows * (grad_prob - jnp.sum(grad_prob * prob_rows, axis=-1, keepdims=True))
    ).astype(jnp.bfloat16)
    grad_query = (
        jnp.einsum("whqk,wkhc->wqhc", grad_score, key_rows, preferred_element_type=jnp.float32)
        * scale_factor
    ).astype(jnp.bfloat16)
    grad_key = (
        jnp.einsum("whqk,wqhc->wkhc", grad_score, queries, preferred_element_type=jnp.float32)
        * scale_factor
    ).astype(jnp.bfloat16)
    score_sum = jnp.sum(grad_score, axis=0, dtype=jnp.float32)
    return (grad_query, grad_key, grad_value, score_sum)


def shards(
    tokens,
    valid,
    cotangent,
    row_gain,
    row_bias,
    w_qkv,
    qv_bias,
    w_proj,
    w_fc1,
    fc1_bias,
    w_fc2,
    rel_table,
):
    slot_count = tokens.shape[1]
    heads_here = rel_table.shape[1]
    head_shape = (slot_count, 4, WIN * WIN, heads_here, HDIM)
    window_shape = (slot_count, 4, WIN * WIN, heads_here * HDIM)
    scale_factor = HDIM ** (-0.5)
    residual = tokens.astype(jnp.float32)
    stored = []
    for layer_index in range(LAYERS):
        shifted = layer_index % 2 == 1
        gain_rows, bias_rows, qkv_full, proj_full, fc1_full, fc2_full = (
            lax.all_gather(row_gain[layer_index], "dp", axis=1, tiled=True),
            lax.all_gather(row_bias[layer_index], "dp", axis=1, tiled=True),
            lax.all_gather(w_qkv[layer_index], "dp", axis=0, tiled=True),
            lax.all_gather(w_proj[layer_index], "dp", axis=1, tiled=True),
            lax.all_gather(w_fc1[layer_index], "dp", axis=0, tiled=True),
            lax.all_gather(w_fc2[layer_index], "dp", axis=1, tiled=True),
        )
        gain_rows = gain_rows.astype(jnp.float32)
        bias_rows = bias_rows.astype(jnp.float32)
        normed, norm_back = jax.vjp(layer_norm, residual, gain_rows[0], bias_rows[0])
        full_normed = lax.all_gather(normed.astype(jnp.bfloat16), "tensor", axis=0, tiled=True)
        projected = jnp.einsum(
            "tsd,dke->tske", full_normed, qkv_full, preferred_element_type=jnp.float32
        )
        pair_bias = qv_bias[layer_index].astype(jnp.float32)
        queries = to_windows(
            (projected[:, :, 0] + pair_bias[0]).astype(jnp.bfloat16), shifted
        ).reshape(head_shape)
        key_rows = to_windows(projected[:, :, 1].astype(jnp.bfloat16), shifted).reshape(head_shape)
        value_rows = to_windows(
            (projected[:, :, 2] + pair_bias[1]).astype(jnp.bfloat16), shifted
        ).reshape(head_shape)
        bias_add = table_bias(rel_table[layer_index])[None]
        if shifted:
            bias_add = bias_add + plan_mask()[:, None]
        blended, log_total = lax.map(
            lambda pieces: attend_image(pieces, bias_add, scale_factor),
            (queries, key_rows, value_rows),
        )
        out_rows = from_windows(blended.reshape(window_shape), shifted)
        attention = lax.psum_scatter(
            jnp.einsum(
                "tse,ed->tsd", out_rows, proj_full, preferred_element_type=jnp.float32
            ).astype(jnp.bfloat16),
            "tensor",
            scatter_dimension=0,
            tiled=True,
        ).astype(jnp.float32)
        residual_mid = residual + attention + bias_rows[1]
        normed_mid, mid_back = jax.vjp(layer_norm, residual_mid, gain_rows[1], bias_rows[2])
        mid_low = normed_mid.astype(jnp.bfloat16)
        fc1_use, fc2_use, fc1_bias_use = (fc1_full, fc2_full, fc1_bias[layer_index])
        mlp_input = lax.all_gather(mid_low, "tensor", axis=0, tiled=True)
        hidden_pre = jnp.einsum(
            "tsd,df->tsf", mlp_input, fc1_use, preferred_element_type=jnp.float32
        ) + fc1_bias_use.astype(jnp.float32)
        activated, gelu_back = jax.vjp(gelu_exact, hidden_pre)
        act_low = activated.astype(jnp.bfloat16)
        mlp_sum = lax.psum_scatter(
            jnp.einsum("tsf,fd->tsd", act_low, fc2_use, preferred_element_type=jnp.float32).astype(
                jnp.bfloat16
            ),
            "tensor",
            scatter_dimension=0,
            tiled=True,
        ).astype(jnp.float32)
        residual = residual_mid + mlp_sum + bias_rows[3]
        stored.append(
            (
                shifted,
                norm_back,
                mid_back,
                gelu_back,
                full_normed,
                queries,
                key_rows,
                value_rows,
                log_total,
                bias_add,
                out_rows,
                mlp_input,
                act_low,
                qkv_full,
                proj_full,
                fc1_use,
                fc2_use,
            )
        )
    valid_rows = valid.astype(jnp.float32)[None, :, None]
    block_out = (residual * valid_rows).astype(jnp.bfloat16)
    grad_stream = cotangent.astype(jnp.float32) * valid_rows
    results = [None] * LAYERS
    for layer_index in reversed(range(LAYERS)):
        (
            shifted,
            norm_back,
            mid_back,
            gelu_back,
            full_normed,
            queries,
            key_rows,
            value_rows,
            log_total,
            bias_add,
            out_rows,
            mlp_input,
            act_low,
            qkv_full,
            proj_full,
            fc1_use,
            fc2_use,
        ) = stored[layer_index]
        grad_bias_last = jnp.sum(grad_stream, axis=(0, 1))
        grad_low = grad_stream.astype(jnp.bfloat16)
        grad_full = lax.all_gather(grad_low, "tensor", axis=0, tiled=True)
        grad_act = jnp.einsum("tsd,fd->tsf", grad_full, fc2_use, preferred_element_type=jnp.float32)
        grad_pre = gelu_back(grad_act)[0].astype(jnp.bfloat16)
        fc2_grad = jnp.einsum("tsf,tsd->fd", act_low, grad_full, preferred_element_type=jnp.float32)
        fc1_grad = jnp.einsum(
            "tsd,tsf->df", mlp_input, grad_pre, preferred_element_type=jnp.float32
        )
        fc1_bias_grad = jnp.sum(grad_pre, axis=(0, 1), dtype=jnp.float32)
        grad_mid = lax.psum_scatter(
            jnp.einsum("tsf,df->tsd", grad_pre, fc1_use, preferred_element_type=jnp.float32).astype(
                jnp.bfloat16
            ),
            "tensor",
            scatter_dimension=0,
            tiled=True,
        ).astype(jnp.float32)
        grad_res, grad_gain_mid, grad_bias_mid = mid_back(grad_mid)
        grad_stream = grad_stream + grad_res
        grad_bias_attn = jnp.sum(grad_stream, axis=(0, 1))
        grad_attn = lax.all_gather(grad_stream.astype(jnp.bfloat16), "tensor", axis=0, tiled=True)
        proj_grad = jnp.einsum(
            "tse,tsd->ed", out_rows, grad_attn, preferred_element_type=jnp.float32
        )
        grad_out = jnp.einsum(
            "tsd,ed->tse", grad_attn, proj_full, preferred_element_type=jnp.float32
        ).astype(jnp.bfloat16)
        grad_out = to_windows(grad_out, shifted).reshape(head_shape)
        grad_query, grad_key, grad_value, score_sums = lax.map(
            lambda pieces: attend_back(pieces, bias_add, scale_factor),
            (queries, key_rows, value_rows, log_total, grad_out),
        )
        table_grad = table_back(jnp.sum(score_sums, axis=0))
        grad_qkv = jnp.stack(
            [
                from_windows(member.reshape(window_shape), shifted)
                for member in (grad_query, grad_key, grad_value)
            ],
            axis=2,
        )
        qv_grad = jnp.stack(
            [
                jnp.sum(grad_qkv[:, :, 0], axis=(0, 1), dtype=jnp.float32),
                jnp.sum(grad_qkv[:, :, 2], axis=(0, 1), dtype=jnp.float32),
            ]
        )
        qkv_grad = jnp.einsum(
            "tsd,tske->dke", full_normed, grad_qkv, preferred_element_type=jnp.float32
        )
        grad_normed = lax.psum_scatter(
            jnp.einsum(
                "tske,dke->tsd", grad_qkv, qkv_full, preferred_element_type=jnp.float32
            ).astype(jnp.bfloat16),
            "tensor",
            scatter_dimension=0,
            tiled=True,
        ).astype(jnp.float32)
        grad_res, grad_gain_first, grad_bias_first = norm_back(grad_normed)
        grad_stream = grad_stream + grad_res
        gain_grads = jnp.stack([grad_gain_first, grad_gain_mid])
        bias_grads = jnp.stack([grad_bias_first, grad_bias_attn, grad_bias_mid, grad_bias_last])
        gain_grads, bias_grads = lax.psum((gain_grads, bias_grads), "tensor")
        shard_grads = (
            lax.psum_scatter(
                gain_grads.astype(jnp.bfloat16), "dp", scatter_dimension=1, tiled=True
            ).astype(jnp.float32),
            lax.psum_scatter(
                bias_grads.astype(jnp.bfloat16), "dp", scatter_dimension=1, tiled=True
            ).astype(jnp.float32),
            lax.psum_scatter(
                qkv_grad.astype(jnp.bfloat16), "dp", scatter_dimension=0, tiled=True
            ).astype(jnp.float32),
            lax.psum_scatter(
                proj_grad.astype(jnp.bfloat16), "dp", scatter_dimension=1, tiled=True
            ).astype(jnp.float32),
            lax.psum_scatter(
                fc1_grad.astype(jnp.bfloat16), "dp", scatter_dimension=0, tiled=True
            ).astype(jnp.float32),
            lax.psum_scatter(
                fc2_grad.astype(jnp.bfloat16), "dp", scatter_dimension=1, tiled=True
            ).astype(jnp.float32),
        )
        small_grads = lax.psum((qv_grad, fc1_bias_grad, table_grad), "dp")
        results[layer_index] = tuple(shard_grads) + tuple(small_grads)
    stacked = [
        jnp.stack([results[which_layer][member] for which_layer in range(LAYERS)])
        for member in range(9)
    ]
    (
        grad_row_gain,
        grad_row_bias,
        grad_w_qkv,
        grad_w_proj,
        grad_w_fc1,
        grad_w_fc2,
        grad_qv_bias,
        grad_fc1_bias,
        grad_rel_table,
    ) = stacked
    return (
        block_out,
        grad_stream,
        grad_row_gain,
        grad_row_bias,
        grad_w_qkv,
        grad_qv_bias,
        grad_w_proj,
        grad_w_fc1,
        grad_fc1_bias,
        grad_w_fc2,
        grad_rel_table,
    )


def unit_stack(w_qkv, w_proj, w_fc1, w_fc2):
    layers, rows = w_qkv.shape[:2]
    qkv = jnp.transpose(w_qkv, (0, 2, 1, 3))
    proj = jnp.swapaxes(w_proj, 1, 2)[:, None]
    fc1 = jnp.transpose(w_fc1.reshape(layers, rows, 4, UC), (0, 2, 1, 3))
    fc2 = jnp.transpose(w_fc2.reshape(layers, 4, UC, rows), (0, 1, 3, 2))
    ff = jnp.stack([fc1, fc2], axis=2).reshape(layers, 8, rows, UC)
    return jnp.concatenate([qkv, proj, ff], axis=1).reshape(layers * NU, rows, UC)


def unit_split(units):
    rows = units.shape[1]
    units = units.reshape(LAYERS, NU, rows, UC)[::-1]
    units = jnp.stack([units[:, BACK_ORDER.index(u)] for u in range(NU)], axis=1)
    qkv = jnp.transpose(units[:, :3], (0, 2, 1, 3))
    proj = jnp.swapaxes(units[:, 3], 1, 2)
    ff = units[:, 4:].reshape(LAYERS, 4, 2, rows, UC)
    fc1 = jnp.transpose(ff[:, :, 0], (0, 2, 1, 3)).reshape(LAYERS, rows, 4 * UC)
    fc2 = jnp.transpose(ff[:, :, 1], (0, 1, 3, 2)).reshape(LAYERS, 4 * UC, rows)
    return qkv, proj, fc1, fc2


def image_shards(tokens, valid, cotangent, row_gain, row_bias, w_qkv, qv_bias, w_proj, w_fc1, fc1_bias, w_fc2, rel_table):
    t, d = lax.axis_index("tensor"), lax.axis_index("dp")
    here = lax.dynamic_slice(valid, (t,), (1,))
    shard = unit_stack(w_qkv, w_proj, w_fc1, w_fc2)
    vecs = jnp.concatenate([row_gain, row_bias], axis=1).reshape(LAYERS * 6, 48)
    vshard = jnp.pad(vecs.T, ((0, 0), (0, 128 - LAYERS * 6)))[None]
    rows = jnp.concatenate([qv_bias.reshape(2 * LAYERS, UC), fc1_bias.reshape(4 * LAYERS, UC)]).astype(F32)
    pay = jnp.concatenate([jnp.pad(rows, ((0, 4), (0, PAY - UC))),
                           jnp.pad(rel_table.reshape(LAYERS * 12, RELS), ((0, 0), (0, PAY - RELS)))])
    block, vec, cot, w, *saved = forward_call(
        jnp.swapaxes(tokens, 0, 1), jnp.swapaxes(cotangent, 0, 1), here, vshard, pay, shard)
    gt, block, total, small = backward_call(cot, here, vec, block, w, *saved)
    qkv_g, proj_g, fc1_g, fc2_g = unit_split(total)
    rowg = lax.dynamic_slice(small[:, 1], (0, 0, d * 48), (LAYERS, 6, 48))
    own = small[:, 0]
    return (jnp.swapaxes(block, 0, 1), jnp.swapaxes(gt, 0, 1), rowg[:, :2], rowg[:, 2:], qkv_g, own[:, 12:14, :UC],
            proj_g, fc1_g, own[:, 14:16].reshape(LAYERS, 4 * UC), fc2_g, own[:, :12, :RELS])


def solution(mesh):
    whole_images = mesh.shape["tensor"] == 2 and mesh.shape["dp"] == 16
    return jax.shard_map(
        image_shards if whole_images else shards,
        mesh=mesh,
        in_specs=(
            P("tensor", "dp", None),
            P("dp"),
            P("tensor", "dp", None),
            P(None, None, "dp"),
            P(None, None, "dp"),
            P(None, "dp", None, "tensor"),
            P(None, None, "tensor"),
            P(None, "tensor", "dp"),
            P(None, "dp", "tensor"),
            P(None, "tensor"),
            P(None, "tensor", "dp"),
            P(None, "tensor", None),
        ),
        out_specs=(
            P("tensor", "dp", None),
            P("tensor", "dp", None),
            P(None, None, "dp"),
            P(None, None, "dp"),
            P(None, "dp", None, "tensor"),
            P(None, None, "tensor"),
            P(None, "tensor", "dp"),
            P(None, "dp", "tensor"),
            P(None, "tensor"),
            P(None, "tensor", "dp"),
            P(None, "tensor", None),
        ),
        check_vma=False,
    )
```

```python
import functools
import numpy as np
import jax
import jax.numpy as jnp
from jax import lax
from jax.experimental import pallas as pl
from jax.experimental.pallas import tpu as pltpu
from jax.sharding import PartitionSpec as P

WIN = 12
LAYERS = 2
HDIM = 32
SIDE = 24
SHIFT = 6
RELS = 529
EPSILON = 1e-05
MASK_FILL = -100.0

D = 768
HEADS = 24
FF = 3072
TOK = 576
WT = 144
UC = 384
NU = 12
HG = 4
NG = HEADS // HG
SCALE = HDIM ** -0.5
BF = jnp.bfloat16
F32 = jnp.float32


def nn(a, b):
    return lax.dot_general(a, b, (((1,), (0,)), ((), ())), preferred_element_type=F32)


def nt(a, b):
    return lax.dot_general(a, b, (((1,), (1,)), ((), ())), preferred_element_type=F32)


def norm_parts(x):
    mean = jnp.mean(x, axis=-1, keepdims=True)
    c = x - mean
    var = jnp.mean(c * c, axis=-1, keepdims=True)
    rstd = lax.rsqrt(var + EPSILON)
    return c * rstd, rstd


def gelu_parts(u):
    phi_big = 0.5 * (1.0 + lax.erf(u * (0.5 ** 0.5)))
    phi = jnp.exp(-0.5 * u * u) * (1.0 / (2.0 * np.pi) ** 0.5)
    return u * phi_big, phi_big + u * phi


def window_order():
    out = []
    for shift in (0, SHIFT):
        p = np.arange(SIDE)
        src = (p + shift) % SIDE
        grid = src[:, None] * SIDE + src[None, :]
        grid = grid.reshape(2, WIN, 2, WIN).transpose(0, 2, 1, 3).reshape(TOK)
        out.append(grid)
    return np.stack(out)


def perm_matrices():
    order = window_order()
    return (order[:, :, None] == np.arange(TOK)[None, None, :]).astype(np.float32)


def shift_mask():
    places = np.arange(SIDE)
    band_of = (places >= SIDE - WIN).astype(np.int32) + (places >= SIDE - SHIFT).astype(np.int32)
    region = band_of[:, None] * 3 + band_of[None, :]
    region = region.reshape(2, WIN, 2, WIN).transpose(0, 2, 1, 3).reshape(4, WT)
    same = region[:, :, None] == region[:, None, :]
    masked = np.where(same, 0.0, MASK_FILL).astype(np.float32)
    return np.tile(np.stack([np.zeros_like(masked), masked]), (1, 1, 1, HG))


def rows_loop(n, body):
    def step(i, c):
        body(i)
        return c
    lax.fori_loop(0, n, step, 0)


def w2d(wbuf, slot):
    return wbuf[slot].reshape(D, 2 * UC)


class Fetch:
    def __init__(self, w_hbm, wbuf, sem, g, slot):
        self.copies = [pltpu.make_async_copy(w_hbm.at[g, t], wbuf.at[slot, :, :, :, :, t * UC:(t + 1) * UC], sem.at[slot, t])
                       for t in range(2)]

    def start(self):
        for cp in self.copies:
            cp.start()

    def wait(self):
        for cp in self.copies:
            cp.wait()


class Place:
    def __init__(self):
        d, self.t = lax.axis_index("dp"), lax.axis_index("tensor")
        self.z = lax.div(d, 4)
        self.y = lax.rem(lax.div(d, 2), 2)
        self.c = lax.rem(d, 2)
        t, y, even = self.t, self.y, self.c == 0
        self.x_side, self.y_side = (1 - t, y), (t, 1 - y)
        self.first = tuple(jnp.where(even, a, b) for a, b in zip(self.x_side, self.y_side))
        self.second = tuple(jnp.where(even, b, a) for a, b in zip(self.x_side, self.y_side))
        self.diagonal = (1 - t, 1 - y)

    def device(self, z, ty, c):
        return {"dp": (z * 2 + ty[1]) * 2 + c, "tensor": ty[0]}

    def side(self, ty):
        return self.device(self.z, ty, self.c)

    def along(self, k):
        return lax.rem(self.z + k, 4)

    def above(self, k):
        return self.device(self.along(k), (self.t, self.y), self.c)

    def sibling(self):
        return self.device(self.z, (self.t, self.y), 1 - self.c)

    def barrier(self):
        sem = pltpu.get_barrier_semaphore()
        peers = [self.above(k) for k in (1, 2, 3)] + [self.side(self.x_side), self.side(self.y_side), self.sibling()]
        for peer in peers:
            pl.semaphore_signal(sem, inc=1, device_id=peer, device_id_type=MESH)
        pl.semaphore_wait(sem, len(peers))


MESH = pl.DeviceIdType.MESH
GATHER_LAGS = (2, 4, 6, 7)
GATHER_SEMS = 12
TICK_EVERY = (12, 6)


class Gather:
    def __init__(self, at, shard, whole, send, recv, local, units):
        self.at, self.shard, self.whole, self.units = at, shard, whole, units
        self.send, self.recv, self.local = send, recv, local

    def copy(self, g, n, src, dst, device):
        slot = lax.rem(g, GATHER_SEMS) if self.units > 1 else 0
        return pltpu.make_async_remote_copy(
            src_ref=src, dst_ref=dst, send_sem=self.send.at[slot, n], recv_sem=self.recv.at[slot, n],
            device_id=device, device_id_type=MESH)

    def mine(self, g):
        p = self.at
        return pltpu.make_async_copy(self.shard.at[g], self.whole.at[g, p.t, p.z, p.y, p.c],
                                     self.local.at[lax.rem(g, GATHER_SEMS) if self.units > 1 else 0])

    def up(self, g, k):
        p = self.at
        return self.copy(g, k - 1, self.shard.at[g], self.whole.at[g, p.t, p.z, p.y, p.c], p.above(k))

    def group(self, g, n, ty, to):
        ref = self.whole.at[g, ty[0], :, ty[1], self.at.c]
        return self.copy(g, n, ref, ref, self.at.side(to))

    def first(self, g):
        return self.group(g, 3, (self.at.t, self.at.y), self.at.first)

    def second(self, g):
        return self.group(g, 4, (self.at.t, self.at.y), self.at.second)

    def onward(self, g):
        return self.group(g, 5, self.at.first, self.at.second)

    def core(self, g):
        ref = self.whole.at[g, :, :, :, self.at.c]
        return self.copy(g, 6, ref, ref, self.at.sibling())

    def stage(self, n, g):
        if n == 0:
            self.mine(g).start()
            for k in (1, 2, 3):
                self.up(g, k).start()
        elif n == 1:
            self.mine(g).wait()
            for k in (1, 2, 3):
                self.up(g, k).wait_recv()
            self.first(g).start()
            self.second(g).start()
        elif n == 2:
            self.first(g).wait_recv()
            self.onward(g).start()
        elif n == 3:
            self.second(g).wait_recv()
            self.onward(g).wait_recv()
            self.core(g).start()
        else:
            self.core(g).wait()
            for k in (1, 2, 3):
                self.up(g, k).wait_send()
            self.first(g).wait_send()
            self.second(g).wait_send()
            self.onward(g).wait_send()

    def tick(self, n):
        for st in (4, 3, 2, 1, 0):
            g = n - (GATHER_LAGS[st - 1] if st else 0)
            if isinstance(g, int):
                if 0 <= g < self.units:
                    self.stage(st, g)
            else:
                @pl.when((g >= 0) & (g < self.units))
                def _(st=st, g=g):
                    self.stage(st, g)


def fold_places():
    lane = np.arange(UC)
    j, xa = lane // WIN, lane % WIN
    return np.where(j < 2 * WIN - 1, j * (2 * WIN - 1) + xa + WIN - 1, -4 * PAY).astype(np.int32)[None]


def fold_matrix(places, xb):
    rows = lax.broadcasted_iota(jnp.int32, (PAY, UC), 0)
    return jnp.where(rows == places - xb, 1.0, 0.0).astype(BF)


def split3(x):
    hi = x.astype(BF)
    rest = x - hi.astype(F32)
    mid = rest.astype(BF)
    return hi, mid, (rest - mid.astype(F32)).astype(BF)


HT = HG * WT
CHUNKS = [slice(i, min(i + 128, HT)) for i in range(0, HT, 128)]


def by_head(x, lanes):
    return jnp.concatenate([jnp.where(lanes == h, x, jnp.zeros_like(x)) for h in range(HG)], axis=0)


def own_blocks(x):
    return jnp.concatenate([x[h * HDIM:(h + 1) * HDIM, h * WT:(h + 1) * WT] for h in range(HG)], axis=0).T


def half_rows(t):
    return pl.ds(pl.multiple_of(t * HALF, HALF), HALF)


def forward_kernel(tok, cot, valid, vshard, pay, places, mask, perm, permt, shard,
                   out, vec, cot_h, w_hbm, x0_h, x1_h, n1_h, qkv_h, pw_h, o_h, n2_h, gg_h,
                   wbuf, x0, x1, n1, qkv, ow, n2, acc, pst, gst, ubuf,
                   xin, vall, pays, ext, bias, scores,
                   wsem, ssem, psem, gsem, gsend, grecv, glocal, vsend, vrecv, vlocal, xsend, xrecv, xlocal):
    at = Place()
    ag = Gather(at, shard, w_hbm, gsend, grecv, glocal, LAYERS * NU)
    vg = Gather(at, vshard, vall, vsend, vrecv, vlocal, 1)
    at.barrier()
    lag = GATHER_LAGS[-1]
    t = at.t
    mine, theirs = half_rows(t), half_rows(1 - t)
    swaps, keeps = [], []
    for n, (src, here, src_keep) in enumerate((
            (tok.at[1 - t], xin.at[mine], tok.at[t]),
            (pay, pays.at[t], pay),
            (cot.at[1 - t], cot_h.at[mine], cot.at[t]))):
        swaps.append(pltpu.make_async_remote_copy(
            src_ref=src, dst_ref=here, send_sem=xsend.at[n], recv_sem=xrecv.at[n],
            device_id=at.side(at.x_side), device_id_type=MESH))
        keeps.append(pltpu.make_async_copy(src_keep, here, xlocal.at[n]))
    for n in range(2):
        swaps[n].start()
        keeps[n].start()
    def both(row):
        return jnp.concatenate([pays[0, pl.ds(row, 1), :UC], pays[1, pl.ds(row, 1), :UC]], axis=1)

    def vrow(l, i):
        return vec[pl.ds(l * 6 + i, 1)]

    def spread(i, c):
        half, l, g = lax.div(i, 6), lax.rem(lax.div(i, 3), 2), lax.rem(i, 3)
        for h in range(HG):
            x = ext[half * 24 + l * 12 + g * HG + h]
            for yb in range(WIN):
                off = (WIN - 1 - yb) * WIN
                bias[l, half * 3 + g, yb * WIN:(yb + 1) * WIN, h * WT:(h + 1) * WT] = x[:, off:off + WT]
        return c

    def norm_first(l):
        def ln1(i):
            r = pl.ds(i * WT, WT)
            xh, _ = norm_parts(x0[l, r])
            ow[l, r] = (xh * vrow(l, 0) + vrow(l, 2)).astype(BF)
        rows_loop(4, ln1)
        n1[l] = nn(perm[l], ow[l]).astype(BF)

    for n in range(lag + 1):
        if n < 5:
            vg.stage(n, 0)
        ag.tick(n)
        if n == 0:
            swaps[1].wait()
            keeps[1].wait()
            table = jnp.concatenate([pays[0, 16:40], pays[1, 16:40]], axis=0)
            parts = jnp.concatenate(split3(table), axis=0)
            for xa in range(WIN):
                y = nn(parts, fold_matrix(places[...], xa))
                ext[:, xa, :] = y[:48] + y[48:96] + y[96:]
        if n == 2:
            lax.fori_loop(0, 6, spread, 0)
        if n == 3:
            lax.fori_loop(6, 12, spread, 0)
        if n == 4:
            vec[...] = vall[0, 0].reshape(D, 128).astype(F32).T[:16]
            swaps[0].wait()
            keeps[0].wait()
            x0[0] = xin[...].astype(F32)
        if n == 5:
            norm_first(0)

    def fetch(g, u):
        return Fetch(w_hbm, wbuf, wsem, g, u % 2)

    def tick_base(l, u):
        before, inside = (4 * NG // every for every in TICK_EVERY)
        return lag + 1 + l * (NU + before) + u + (jnp.where(l == 0, before, inside) if u >= 3 else 0)

    def step_unit(l, u):
        g = l * NU + u
        fetch(g, u).wait()
        ag.tick(tick_base(l, u))

        @pl.when(g + 1 < LAYERS * NU)
        def _():
            fetch(g + 1, u + 1).start()

    fetch(0, 0).start()
    lanes = lax.shift_right_logical(lax.broadcasted_iota(jnp.int32, (WT, HG * HDIM), 1), 5)

    kept = ((x0, x0_h), (x1, x1_h), (n1, n1_h), (qkv, qkv_h), (ow, o_h), (n2, n2_h))

    def save(l, *which):
        for n in which:
            pltpu.make_async_copy(kept[n][0].at[l], kept[n][1].at[l], ssem.at[l]).start()

    def layer(l, carry):
        x0_l, x1_l, n1_l, n2_l, ow_l = x0.at[l], x1.at[l], n1.at[l], n2.at[l], ow.at[l]

        @pl.when(l > 0)
        def _():
            norm_first(l)
        for j in range(3):
            step_unit(l, j)
            y = nn(n1_l[...], w2d(wbuf, j % 2))
            if j != 1:
                y = y + both(l * 2 + j // 2)
            qkv[l, j] = y.astype(BF)
        save(l, 0, 2, 3)

        def attend(it, c):
            w, hg = lax.div(it, NG), lax.rem(it, NG)
            r = pl.ds(pl.multiple_of(w * WT, WT), WT)
            cl = pl.ds(pl.multiple_of(hg * 128, 128), 128)
            slot = lax.rem(it, 2)
            q, k, v = qkv[l, 0, r, cl], qkv[l, 1, r, cl], qkv[l, 2, r, cl]
            put = pltpu.make_async_copy(pst.at[slot], pw_h.at[l, w, hg], psem.at[slot])

            @pl.when((it >= 2) | (l > 0))
            def _():
                put.wait()
            scores[...] = nt(k, by_head(q, lanes))
            for ch in CHUNKS:
                x = scores[:, ch] * SCALE + bias[l, hg, :, ch] + mask[l, w, :, ch]
                x = jnp.exp(x - jnp.max(x, axis=0, keepdims=True))
                pst[slot, :, ch] = (x * (1.0 / jnp.sum(x, axis=0, keepdims=True))).astype(BF)
            ow_l[r, cl] = own_blocks(nn(v.T, pst[slot])).astype(BF)
            put.start()

            every = jnp.where(l == 0, TICK_EVERY[0], TICK_EVERY[1])

            @pl.when(lax.rem(it, every) == every - 1)
            def _():
                ag.tick(tick_base(l, 2) + 1 + lax.div(it, every))
            return c
        lax.fori_loop(0, 4 * NG, attend, 0)

        save(l, 4)

        @pl.when(l == LAYERS - 1)
        def _():
            swaps[2].start()
            keeps[2].start()
        n2_l[...] = nn(permt[l], ow_l[...]).astype(BF)
        step_unit(l, 3)
        acc[...] = nt(n2_l[...], w2d(wbuf, 1))

        def ln2(i):
            r = pl.ds(i * WT, WT)
            x = x0_l[r] + acc[r] + vrow(l, 3)
            x1_l[r] = x
            xh, _ = norm_parts(x)
            n2_l[r] = (xh * vrow(l, 1) + vrow(l, 4)).astype(BF)
            acc[r] = x + vrow(l, 5)
        rows_loop(4, ln2)
        save(l, 1, 5)
        for i in range(4):
            step_unit(l, 4 + 2 * i)
            put = pltpu.make_async_copy(gst.at[i % 2], gg_h.at[l, i], gsem.at[i % 2])
            if i > 1:
                put.wait()
            else:
                @pl.when(l > 0)
                def _():
                    put.wait()
            ubuf[...] = nn(n2_l[...], w2d(wbuf, 0)) + both(4 + l * 4 + i)

            def act(n):
                r = pl.ds(n * 48, 48)
                g, gp = gelu_parts(ubuf[r])
                gst[i % 2, 0, r] = g.astype(BF)
                gst[i % 2, 1, r] = gp.astype(BF)
            rows_loop(12, act)
            put.start()
            step_unit(l, 5 + 2 * i)
            acc[...] += nt(gst[i % 2, 0], w2d(wbuf, 1))

        @pl.when(l == 0)
        def _():
            x0[1] = acc[...]

        @pl.when(l == 1)
        def _():
            out[...] = (acc[...] * valid[at.t].astype(F32)).astype(BF)
        return carry
    lax.fori_loop(0, LAYERS, layer, 0)
    for l in range(LAYERS):
        for ref, dst in kept:
            pltpu.make_async_copy(ref.at[l], dst.at[l], ssem.at[l]).wait()
    for s in range(2):
        pltpu.make_async_copy(pst.at[s], pw_h.at[0, 0, 0], psem.at[s]).wait()
        pltpu.make_async_copy(gst.at[s], gg_h.at[0, s], gsem.at[s]).wait()
    swaps[2].wait()
    keeps[2].wait()


def sds(shape, dtype):
    return jax.ShapeDtypeStruct(shape, dtype)


VM = pl.BlockSpec(memory_space=pltpu.VMEM)
AN = pl.BlockSpec(memory_space=pl.ANY)
SM = pl.BlockSpec(memory_space=pltpu.SMEM)

SAVED = [
    sds((LAYERS, TOK, D), F32), sds((LAYERS, TOK, D), F32), sds((LAYERS, TOK, D), BF),
    sds((LAYERS, 3, TOK, D), BF), sds((LAYERS, 4, NG, WT, HT), BF),
    sds((LAYERS, TOK, D), BF), sds((LAYERS, TOK, D), BF), sds((LAYERS, 4, 2, TOK, 2 * UC), BF),
]


def forward_call(tok, cot, valid, vshard, pay, shard):
    perm = perm_matrices()
    permt = jnp.asarray(perm.transpose(0, 2, 1), BF)
    return pl.pallas_call(
        forward_kernel,
        out_shape=[sds((TOK, D), BF), sds((16, D), F32), sds((TOK, D), BF),
                   sds((LAYERS * NU, 2, 4, 2, 2, 48, UC), BF)] + SAVED,
        in_specs=[AN, AN, SM, AN, AN, VM, VM, VM, VM, AN],
        out_specs=[VM, VM] + [AN] * 10,
        scratch_shapes=[
            pltpu.VMEM((2, 4, 2, 2, 48, 2 * UC), BF),
            pltpu.VMEM((2, TOK, D), F32), pltpu.VMEM((2, TOK, D), F32),
            pltpu.VMEM((2, TOK, D), BF), pltpu.VMEM((2, 3, TOK, D), BF),
            pltpu.VMEM((2, TOK, D), BF), pltpu.VMEM((2, TOK, D), BF),
            pltpu.VMEM((TOK, D), F32), pltpu.VMEM((2, WT, HT), BF),
            pltpu.VMEM((2, 2, TOK, 2 * UC), BF), pltpu.VMEM((TOK, 2 * UC), F32),
            pltpu.VMEM((TOK, D), BF), pltpu.VMEM((1, 2, 4, 2, 2, 48, 128), BF),
            pltpu.VMEM((2, 40, PAY), F32), pltpu.VMEM((48, WIN, UC), F32),
            pltpu.VMEM((LAYERS, NG, WT, HT), F32), pltpu.VMEM((WT, HT), F32),
            pltpu.SemaphoreType.DMA((2, 2)), pltpu.SemaphoreType.DMA((2,)),
            pltpu.SemaphoreType.DMA((2,)), pltpu.SemaphoreType.DMA((2,)),
            pltpu.SemaphoreType.DMA((GATHER_SEMS, 7)), pltpu.SemaphoreType.DMA((GATHER_SEMS, 7)),
            pltpu.SemaphoreType.DMA((GATHER_SEMS,)),
            pltpu.SemaphoreType.DMA((1, 7)), pltpu.SemaphoreType.DMA((1, 7)), pltpu.SemaphoreType.DMA((1,)),
            pltpu.SemaphoreType.DMA((3,)), pltpu.SemaphoreType.DMA((3,)), pltpu.SemaphoreType.DMA((3,)),
        ],
        compiler_params=pltpu.CompilerParams(vmem_limit_bytes=60 * 2**20, collective_id=0, has_side_effects=True),
        name="forward",
    )(tok, cot, valid, vshard, pay, fold_places(), shift_mask(), jnp.asarray(perm, BF), permt, shard)


BACK_ORDER = (5, 4, 7, 6, 9, 8, 11, 10, 3, 0, 1, 2)


def norm_back(x, dn, gain):
    xh, rstd = norm_parts(x)
    dx = dn * gain
    grad = rstd * (dx - jnp.mean(dx, axis=-1, keepdims=True)
                   - xh * jnp.mean(dx * xh, axis=-1, keepdims=True))
    return grad, jnp.sum(dn * xh, axis=0, keepdims=True), jnp.sum(dn, axis=0, keepdims=True)


REDUCE_SLOTS = NU
CORE_SLOTS = 4
PAY = 640
HALF = TOK // 2
VIRT = 16
GAP = (9, 13)
REDUCE_LAGS = (1, 6, 10, 14)


class Reduce:
    def __init__(self, at, own, core_in, first_in, second_in, z_in, total, send, recv):
        self.at, self.own, self.total = at, own, total
        self.core_in, self.first_in, self.second_in, self.z_in = core_in, first_in, second_in, z_in
        self.send, self.recv = send, recv

    def slot(self, v):
        place = lax.rem(v, VIRT)
        return jnp.where(place < GAP[0], place, place - (GAP[1] - GAP[0]))

    def copy(self, v, n, src, dst, device):
        slot = self.slot(v)
        return pltpu.make_async_remote_copy(
            src_ref=src, dst_ref=dst, send_sem=self.send.at[slot, n], recv_sem=self.recv.at[slot, n],
            device_id=device, device_id_type=MESH)

    def core(self, v):
        slot = lax.rem(self.slot(v), CORE_SLOTS)
        return self.copy(v, 0, self.own.at[REDUCE_SLOTS + slot], self.core_in.at[slot], self.at.sibling())

    def put(self, v, value):
        value = value.astype(BF)
        mine, other = self.slot(v), REDUCE_SLOTS + lax.rem(self.slot(v), CORE_SLOTS)
        for t in range(2):
            x = value[:, t * UC:(t + 1) * UC].reshape(4, 2, 2, 48, UC)
            for k in range(2):
                self.own[jnp.where(self.at.c == k, mine, other), t] = x[:, :, k]

    def group(self, v, ty):
        return self.own.at[self.slot(v), ty[0], :, ty[1]]

    def first(self, v, n):
        p = self.at
        ty = p.diagonal if n == 0 else p.second
        return self.copy(v, 1 + n, self.group(v, ty), self.first_in.at[self.slot(v), n], p.side(p.second))

    def second(self, v):
        p = self.at
        return self.copy(v, 3, self.group(v, p.first), self.second_in.at[self.slot(v)], p.side(p.first))

    def up(self, v, k):
        p, slot = self.at, self.slot(v)
        return self.copy(v, 3 + k, self.own.at[slot, p.t, p.along(k), p.y], self.z_in.at[slot, k - 1], p.above(k))

    def add(self, ref, other):
        def one(z):
            ref[z] = ref[z] + other[z]
        rows_loop(4, one)

    def stage(self, n, v):
        p, slot = self.at, self.slot(v)
        if n == 0:
            self.core(v).start()
        elif n == 1:
            self.core(v).wait()

            def one(i):
                t, z = lax.div(i, 4), lax.rem(i, 4)
                self.own[slot, t, z] = self.own[slot, t, z] + self.core_in[lax.rem(self.slot(v), CORE_SLOTS), t, z]
            rows_loop(8, one)
            self.first(v, 0).start()
            self.first(v, 1).start()
        elif n == 2:
            self.first(v, 0).wait_recv()
            self.add(self.group(v, p.first), self.first_in.at[slot, 0])
            self.second(v).start()
            self.first(v, 1).wait_recv()
            self.add(self.group(v, (p.t, p.y)), self.first_in.at[slot, 1])
        elif n == 3:
            self.second(v).wait_recv()
            self.add(self.group(v, (p.t, p.y)), self.second_in.at[slot])
            for k in (1, 2, 3):
                self.up(v, k).start()
        else:
            total = self.own[slot, p.t, p.z, p.y].astype(F32)
            for k in (1, 2, 3):
                self.up(v, k).wait_recv()
                total = total + self.z_in[slot, k - 1].astype(F32)
            ff = jnp.where(lax.rem(slot, 2) == 0, 8, 4) + lax.div(slot, 2)
            unit = jnp.where(slot < 8, ff, jnp.where(slot == 8, 3, slot - 9))
            self.total[LAYERS - 1 - lax.div(v, VIRT), unit] = total
            for n in range(2):
                self.first(v, n).wait_send()
            self.second(v).wait_send()
            for k in (1, 2, 3):
                self.up(v, k).wait_send()

    def tick(self, n):
        for st in (4, 3, 2, 1, 0):
            v = n - (REDUCE_LAGS[st - 1] if st else 0)
            place = lax.rem(v, VIRT)

            @pl.when((v >= 0) & (v < LAYERS * VIRT) & ((place < GAP[0]) | (place >= GAP[1])))
            def _(st=st, v=v):
                self.stage(st, v)


def backward_kernel(cot, valid, vec, places, perm, permt, block, w_hbm, x0_h, x1_h, n1_h, qkv_h, pw_h, o_h, n2_h, gg_h,
                    gt, block2, total, small,
                    e, scores, ds, sums, folded, dsum, sm_core, sm_x, sm_y, sm_z, gin,
                    wbuf, xb, n1, n2, qkv, ow, do, dqkv, acc, em, emt, n2t, pst, gst, ubuf, dub, gbuf,
                    core_in, first_in, second_in, z_in,
                    wsem, lsem, psem, gsem, rsend, rrecv, xsend, xrecv, xlocal, ssend, srecv):
    at = Place()
    t_here = at.t
    mine, theirs = half_rows(t_here), half_rows(1 - t_here)
    rs = Reduce(at, gbuf, core_in, first_in, second_in, z_in, total, rsend, rrecv)

    def fetch(g, pos):
        return Fetch(w_hbm, wbuf, wsem, g, pos % 2)

    def step_unit(l, pos):
        fetch(0, pos).wait()
        if pos + 1 < NU:
            fetch(l * NU + BACK_ORDER[pos + 1], pos + 1).start()
        else:
            @pl.when(l > 0)
            def _():
                fetch((l - 1) * NU + BACK_ORDER[0], 0).start()

    def place_of(pos):
        return pos if pos < GAP[0] else pos + GAP[1] - GAP[0]

    def emit(l, pos, value):
        v = (LAYERS - 1 - l) * VIRT + place_of(pos)
        rs.put(v, value)
        rs.tick(v)

    fetch((LAYERS - 1) * NU + BACK_ORDER[0], 0).start()
    at.barrier()
    block_swap = pltpu.make_async_remote_copy(
        src_ref=block.at[theirs], dst_ref=block2.at[t_here], send_sem=xsend.at[0], recv_sem=xrecv.at[0],
        device_id=at.side(at.x_side), device_id_type=MESH)
    block_keep = pltpu.make_async_copy(block.at[mine], block2.at[t_here], xlocal.at[0])
    block_swap.start()
    block_keep.start()
    total[...] = jnp.zeros_like(total)
    e[...] = cot[...].astype(F32) * valid[at.t].astype(F32)
    sums[...] = jnp.zeros_like(sums)
    lanes = lax.shift_right_logical(lax.broadcasted_iota(jnp.int32, (WT, HG * HDIM), 1), 5)

    def layer(step, carry):
        l = LAYERS - 1 - step
        loads = [pltpu.make_async_copy(src.at[l], dst, lsem.at[n]) for n, (src, dst) in enumerate((
            (n2_h, n2), (x1_h, xb), (o_h, ow), (qkv_h, qkv), (n1_h, n1), (x0_h, xb)))]
        for cp in loads[:5]:
            cp.start()

        def load_gg(k):
            return pltpu.make_async_copy(gg_h.at[l, k], gst.at[k % 2], gsem.at[k % 2])
        load_gg(0).start()
        load_gg(1).start()

        def ends(i):
            r = pl.ds(i * WT, WT)
            x = e[r]
            em[r] = x.astype(BF)
            sums[l, 2, 5:6] += jnp.sum(x, axis=0, keepdims=True)
        rows_loop(4, ends)
        emt[...] = em[...].T
        loads[0].wait()
        n2t[...] = n2[...].T
        for i in range(4):
            step_unit(l, 2 * i)
            load_gg(i).wait()
            ubuf[...] = nn(em[...], w2d(wbuf, 0))

            def act(n, c):
                r = pl.ds(n * 48, 48)
                du = (ubuf[r] * gst[i % 2, 1, r].astype(F32)).astype(BF)
                dub[r] = du
                return c + jnp.sum(du.astype(F32), axis=0, keepdims=True)
            y = lax.fori_loop(0, 12, act, jnp.zeros((1, 2 * UC), F32))
            for t in range(2):
                sums[l, t, 14 + i // 2:15 + i // 2, (i % 2) * UC:(i % 2 + 1) * UC] = y[:, t * UC:(t + 1) * UC]
            emit(l, 2 * i, nn(emt[...], gst[i % 2, 0]))
            if i < 2:
                load_gg(i + 2).start()
            step_unit(l, 2 * i + 1)
            y = nt(dub[...], w2d(wbuf, 1))
            if i == 0:
                acc[...] = y
            else:
                acc[...] += y
            emit(l, 2 * i + 1, nn(n2t[...], dub[...]))
        loads[1].wait()

        def ln2(i):
            r = pl.ds(i * WT, WT)
            grad, gsum, bsum = norm_back(xb[r], acc[r], vec[pl.ds(l * 6 + 1, 1)])
            x = e[r] + grad
            e[r] = x
            em[r] = x.astype(BF)
            sums[l, 2, 1:2] += gsum
            sums[l, 2, 4:5] += bsum
            sums[l, 2, 3:4] += jnp.sum(x, axis=0, keepdims=True)
        rows_loop(4, ln2)
        loads[5].start()
        n2[...] = nn(perm[l], em[...]).astype(BF)
        emt[...] = n2[...].T
        step_unit(l, 8)
        loads[2].wait()
        do[...] = nn(n2[...], w2d(wbuf, 0)).astype(BF)
        emit(l, 8, nn(emt[...], ow[...]))
        loads[3].wait()

        def load_pw(it):
            w, hg = lax.div(it, NG), lax.rem(it, NG)
            return pltpu.make_async_copy(pw_h.at[l, w, hg], pst.at[lax.rem(it, 2)], psem.at[lax.rem(it, 2)])
        load_pw(0).start()
        dsum[l] = jnp.zeros((NG, WT, HT), F32)

        def attend(it, c):
            w, hg = lax.div(it, NG), lax.rem(it, NG)
            r = pl.ds(pl.multiple_of(w * WT, WT), WT)
            cl = pl.ds(pl.multiple_of(hg * 128, 128), 128)
            slot = lax.rem(it, 2)

            @pl.when(it + 1 < 4 * NG)
            def _():
                load_pw(it + 1).start()
            q, k, v, d = qkv[0, r, cl], qkv[1, r, cl], qkv[2, r, cl], do[r, cl]
            q4, d4 = by_head(q, lanes), by_head(d, lanes)
            scores[...] = nt(v, d4)
            load_pw(it).wait()
            for ch in CHUNKS:
                p = pst[slot, :, ch].astype(F32)
                x = scores[:, ch]
                mean = jnp.sum(p * x, axis=0, keepdims=True) / jnp.sum(p, axis=0, keepdims=True)
                x = (p * (x - mean)).astype(BF)
                ds[:, ch] = x
                dsum[l, hg, :, ch] += x.astype(F32)
            dqkv[0, r, cl] = (own_blocks(nn(k.T, ds[...])) * SCALE).astype(BF)
            dqkv[1, r, cl] = (nn(ds[...], q4) * SCALE).astype(BF)
            dqkv[2, r, cl] = nn(pst[slot], d4).astype(BF)

            @pl.when(lax.rem(it, 6) == 5)
            def _():
                rs.tick(step * VIRT + GAP[0] + lax.div(it, 6))
            return c
        lax.fori_loop(0, 4 * NG, attend, 0)

        for n, j in ((0, 0), (1, 2)):
            y = jnp.sum(dqkv[j].astype(F32), axis=0, keepdims=True)
            for t in range(2):
                sums[l, t, 12 + n:13 + n, :UC] = y[:, t * UC:(t + 1) * UC]
        loads[4].wait()
        emt[...] = n1[...].T
        for j in range(3):
            emit(l, 9 + j, nn(emt[...], dqkv[j]))
        for j in range(3):
            step_unit(l, 9 + j)
            y = nt(dqkv[j], w2d(wbuf, (9 + j) % 2))
            if j == 0:
                acc[...] = y
            else:
                acc[...] += y
        acc[...] = nn(permt[l], acc[...].astype(BF))
        loads[5].wait()

        def ln1(i):
            r = pl.ds(i * WT, WT)
            grad, gsum, bsum = norm_back(xb[r], acc[r], vec[pl.ds(l * 6, 1)])
            e[r] += grad
            sums[l, 2, 0:1] += gsum
            sums[l, 2, 2:3] += bsum
        rows_loop(4, ln1)
        return carry
    lax.fori_loop(0, LAYERS, layer, 0)
    em[...] = e[...].astype(BF)
    grad_swap = pltpu.make_async_remote_copy(
        src_ref=em.at[theirs], dst_ref=gin, send_sem=xsend.at[1], recv_sem=xrecv.at[1],
        device_id=at.side(at.x_side), device_id_type=MESH)
    grad_swap.start()
    gt[t_here] = e[mine]

    base = LAYERS * VIRT

    def fold(i, c):
        for h in range(HG):
            x = jnp.zeros((2 * WIN, UC), F32)
            for pair in range(WIN // 2):
                part = dsum[lax.div(i, NG), lax.rem(i, NG), 2 * pair * WIN:2 * (pair + 1) * WIN, h * WT:(h + 1) * WT]
                part = jnp.concatenate([part, jnp.zeros((2 * WIN, UC - WT), F32)], axis=1)
                x = x + pltpu.roll(part, (WIN - 1 - 2 * pair) * WIN, 1)
            folded[i * HG + h] = x[:WIN] + pltpu.roll(x[WIN:], UC - WIN, 1)

        @pl.when(lax.rem(i, 2) == 1)
        def _():
            rs.tick(base + lax.div(i, 2))
        return c
    lax.fori_loop(0, LAYERS * NG, fold, 0)
    y = jnp.zeros((2 * LAYERS * HEADS, PAY), F32)
    for xb in range(WIN):
        hi, lo, _ = split3(folded[:, xb, :])
        y = y + nt(jnp.concatenate([hi, lo], axis=0), fold_matrix(places[...], xb))
    y = y[:LAYERS * HEADS] + y[LAYERS * HEADS:]
    for l in range(LAYERS):
        for t in range(2):
            sums[l, t, :12, :PAY] = y[l * HEADS + t * 12:l * HEADS + t * 12 + 12]

    def small_copy(n, src, dst, device):
        return pltpu.make_async_remote_copy(src_ref=src, dst_ref=dst, send_sem=ssend.at[n], recv_sem=srecv.at[n],
                                            device_id=device, device_id_type=MESH)
    c = at.c
    core_swap = small_copy(0, sums.at[1 - c], sm_core, at.sibling())
    core_swap.start()
    base = base + LAYERS * NG // 2
    rs.tick(base)
    core_swap.wait_recv()
    for n in range(3):
        sums[c, n] += sm_core[n]
    x_swaps = [small_copy(1, sums.at[c, 1 - t_here], sm_x.at[0], at.side(at.x_side)),
               small_copy(2, sums.at[c, 2], sm_x.at[1], at.side(at.x_side))]
    for cp in x_swaps:
        cp.start()
    rs.tick(base + 1)
    for cp in x_swaps:
        cp.wait_recv()
    sm_y[0, 0] = sums[c, t_here] + sm_x[0]
    sm_y[0, 1] = sums[c, 2] + sm_x[1]
    y_swap = small_copy(3, sm_y.at[0], sm_y.at[1], at.side(at.y_side))
    y_swap.start()
    rs.tick(base + 2)
    y_swap.wait_recv()
    sm_z[at.z] = (sm_y[0] + sm_y[1]).astype(BF)
    z_swaps = [small_copy(3 + k, sm_z.at[at.z], sm_z.at[at.z], at.above(k)) for k in (1, 2, 3)]
    for cp in z_swaps:
        cp.start()
    rs.tick(base + 3)
    for cp in z_swaps:
        cp.wait_recv()
    small[c] = (sm_z[0].astype(F32) + sm_z[1].astype(F32)) + (sm_z[2].astype(F32) + sm_z[3].astype(F32))
    last = small_copy(7, small.at[c], small.at[c], at.sibling())
    last.start()
    grad_swap.wait()
    gt[1 - t_here] = gin[...].astype(F32)
    for n in range(4, REDUCE_LAGS[-1] - LAYERS * NG // 2):
        rs.tick(base + n)
    last.wait()
    for cp in [core_swap, y_swap] + x_swaps + z_swaps:
        cp.wait_send()
    block_swap.wait()
    block_keep.wait()


def backward_call(cot, valid, vec, block, w, *saved):
    perm = perm_matrices()
    permt = jnp.asarray(perm.transpose(0, 2, 1), BF)
    return pl.pallas_call(
        backward_kernel,
        out_shape=[sds((2, HALF, D), F32), sds((2, HALF, D), BF), sds((LAYERS, NU, 48, UC), F32),
                   sds((LAYERS, 2, 16, D), F32)],
        in_specs=[VM, SM, VM, VM, VM, VM, AN, AN] + [AN] * 8,
        out_specs=[VM, AN, VM, VM],
        scratch_shapes=[
            pltpu.VMEM((TOK, D), F32), pltpu.VMEM((WT, HT), F32), pltpu.VMEM((WT, HT), BF),
            pltpu.VMEM((LAYERS, 3, 16, D), F32), pltpu.VMEM((LAYERS * HEADS, WIN, UC), F32),
            pltpu.VMEM((LAYERS, NG, WT, HT), F32), pltpu.VMEM((3, 16, D), F32), pltpu.VMEM((2, 16, D), F32),
            pltpu.VMEM((2, 2, 16, D), F32), pltpu.VMEM((4, 2, 16, D), BF), pltpu.VMEM((HALF, D), BF),
            pltpu.VMEM((2, 4, 2, 2, 48, 2 * UC), BF),
            pltpu.VMEM((TOK, D), F32), pltpu.VMEM((TOK, D), BF), pltpu.VMEM((TOK, D), BF),
            pltpu.VMEM((3, TOK, D), BF), pltpu.VMEM((TOK, D), BF), pltpu.VMEM((TOK, D), BF),
            pltpu.VMEM((3, TOK, D), BF), pltpu.VMEM((TOK, D), F32), pltpu.VMEM((TOK, D), BF),
            pltpu.VMEM((D, TOK), BF), pltpu.VMEM((D, TOK), BF), pltpu.VMEM((2, WT, HT), BF),
            pltpu.VMEM((2, 2, TOK, 2 * UC), BF), pltpu.VMEM((TOK, 2 * UC), F32), pltpu.VMEM((TOK, 2 * UC), BF),
            pltpu.VMEM((REDUCE_SLOTS + CORE_SLOTS, 2, 4, 2, 48, UC), BF),
            pltpu.VMEM((CORE_SLOTS, 2, 4, 2, 48, UC), BF), pltpu.VMEM((REDUCE_SLOTS, 2, 4, 48, UC), BF),
            pltpu.VMEM((REDUCE_SLOTS, 4, 48, UC), BF), pltpu.VMEM((REDUCE_SLOTS, 3, 48, UC), BF),
            pltpu.SemaphoreType.DMA((2, 2)), pltpu.SemaphoreType.DMA((6,)),
            pltpu.SemaphoreType.DMA((2,)), pltpu.SemaphoreType.DMA((2,)),
            pltpu.SemaphoreType.DMA((REDUCE_SLOTS, 7)), pltpu.SemaphoreType.DMA((REDUCE_SLOTS, 7)),
            pltpu.SemaphoreType.DMA((2,)), pltpu.SemaphoreType.DMA((2,)), pltpu.SemaphoreType.DMA((1,)),
            pltpu.SemaphoreType.DMA((8,)), pltpu.SemaphoreType.DMA((8,)),
        ],
        compiler_params=pltpu.CompilerParams(vmem_limit_bytes=62 * 2**20, collective_id=1, has_side_effects=True),
        name="backward",
    )(cot, valid, vec, fold_places(), jnp.asarray(perm, BF), permt, block, w, *saved)


def layer_norm(values, row_gain, row_shift):
    average = jnp.mean(values, axis=-1, keepdims=True)
    centred = values - average
    variance = jnp.mean(centred * centred, axis=-1, keepdims=True)
    return centred * lax.rsqrt(variance + EPSILON) * row_gain + row_shift


def gelu_exact(values):
    return jax.nn.gelu(values, approximate=False)


def to_windows(rows_data, shifted):
    slot_count = rows_data.shape[1]
    trailing = rows_data.shape[2:]
    image_grid = rows_data.reshape((SIDE, SIDE, slot_count) + trailing)
    if shifted:
        image_grid = jnp.roll(image_grid, (-SHIFT, -SHIFT), axis=(0, 1))
    image_grid = image_grid.reshape((2, WIN, 2, WIN, slot_count) + trailing)
    axes_order = (4, 0, 2, 1, 3) + tuple(range(5, 5 + len(trailing)))
    return jnp.transpose(image_grid, axes_order).reshape((slot_count, 4, WIN * WIN) + trailing)


def from_windows(window_data, shifted):
    slot_count = window_data.shape[0]
    trailing = window_data.shape[3:]
    image_grid = window_data.reshape((slot_count, 2, 2, WIN, WIN) + trailing)
    axes_order = (1, 3, 2, 4, 0) + tuple(range(5, 5 + len(trailing)))
    image_grid = jnp.transpose(image_grid, axes_order).reshape((SIDE, SIDE, slot_count) + trailing)
    if shifted:
        image_grid = jnp.roll(image_grid, (SHIFT, SHIFT), axis=(0, 1))
    return image_grid.reshape((SIDE * SIDE, slot_count) + trailing)


def plan_mask():
    places = jnp.arange(SIDE, dtype=jnp.int32)
    band_of = (places >= SIDE - WIN).astype(jnp.int32) + (places >= SIDE - SHIFT).astype(jnp.int32)
    region = band_of[:, None] * 3 + band_of[None, :]
    region = region.reshape(2, WIN, 2, WIN).transpose(0, 2, 1, 3).reshape(4, WIN * WIN)
    same_region = region[:, :, None] == region[:, None, :]
    return jnp.where(same_region, 0.0, MASK_FILL).astype(jnp.float32)


def offset_table():
    places = jnp.arange(WIN, dtype=jnp.int32)
    targets = jnp.arange(2 * WIN - 1, dtype=jnp.int32)
    offsets = places[:, None] - places[None, :] + WIN - 1
    return (targets[None, None, :] == offsets[:, :, None]).astype(jnp.float32)


def table_bias(table_rows):
    one_hot = offset_table()
    shaped = table_rows.reshape(table_rows.shape[0], 2 * WIN - 1, 2 * WIN - 1)
    spread = jnp.einsum(
        "acr,bds,hrs->habcd", one_hot, one_hot, shaped, precision=lax.Precision.HIGHEST
    )
    return spread.reshape(table_rows.shape[0], WIN * WIN, WIN * WIN)


def table_back(score_sum):
    one_hot = offset_table()
    shaped = score_sum.reshape(score_sum.shape[0], WIN, WIN, WIN, WIN)
    folded = jnp.einsum(
        "acr,bds,habcd->hrs", one_hot, one_hot, shaped, precision=lax.Precision.HIGHEST
    )
    return folded.reshape(score_sum.shape[0], RELS)


def attend_image(pieces, bias_add, scale_factor):
    queries, key_rows, value_rows = pieces
    scores = (
        jnp.einsum("wqhc,wkhc->whqk", queries, key_rows, preferred_element_type=jnp.float32)
        * scale_factor
        + bias_add
    )
    row_top = jnp.max(scores, axis=-1, keepdims=True)
    log_total = row_top + jnp.log(jnp.sum(jnp.exp(scores - row_top), axis=-1, keepdims=True))
    prob_rows = jnp.exp(scores - log_total)
    blended = jnp.einsum(
        "whqk,wkhc->wqhc",
        prob_rows.astype(jnp.bfloat16),
        value_rows,
        preferred_element_type=jnp.float32,
    )
    return (blended.astype(jnp.bfloat16), log_total[..., 0])


def attend_back(pieces, bias_add, scale_factor):
    queries, key_rows, value_rows, log_total, grad_out = pieces
    scores = (
        jnp.einsum("wqhc,wkhc->whqk", queries, key_rows, preferred_element_type=jnp.float32)
        * scale_factor
        + bias_add
    )
    prob_rows = jnp.exp(scores - log_total[..., None])
    prob_low = prob_rows.astype(jnp.bfloat16)
    grad_prob = jnp.einsum(
        "wqhc,wkhc->whqk", grad_out, value_rows, preferred_element_type=jnp.float32
    )
    grad_value = jnp.einsum(
        "whqk,wqhc->wkhc", prob_low, grad_out, preferred_element_type=jnp.float32
    ).astype(jnp.bfloat16)
    grad_score = (
        prob_rows * (grad_prob - jnp.sum(grad_prob * prob_rows, axis=-1, keepdims=True))
    ).astype(jnp.bfloat16)
    grad_query = (
        jnp.einsum("whqk,wkhc->wqhc", grad_score, key_rows, preferred_element_type=jnp.float32)
        * scale_factor
    ).astype(jnp.bfloat16)
    grad_key = (
        jnp.einsum("whqk,wqhc->wkhc", grad_score, queries, preferred_element_type=jnp.float32)
        * scale_factor
    ).astype(jnp.bfloat16)
    score_sum = jnp.sum(grad_score, axis=0, dtype=jnp.float32)
    return (grad_query, grad_key, grad_value, score_sum)


def shards(
    tokens,
    valid,
    cotangent,
    row_gain,
    row_bias,
    w_qkv,
    qv_bias,
    w_proj,
    w_fc1,
    fc1_bias,
    w_fc2,
    rel_table,
):
    slot_count = tokens.shape[1]
    heads_here = rel_table.shape[1]
    head_shape = (slot_count, 4, WIN * WIN, heads_here, HDIM)
    window_shape = (slot_count, 4, WIN * WIN, heads_here * HDIM)
    scale_factor = HDIM ** (-0.5)
    residual = tokens.astype(jnp.float32)
    stored = []
    for layer_index in range(LAYERS):
        shifted = layer_index % 2 == 1
        gain_rows, bias_rows, qkv_full, proj_full, fc1_full, fc2_full = (
            lax.all_gather(row_gain[layer_index], "dp", axis=1, tiled=True),
            lax.all_gather(row_bias[layer_index], "dp", axis=1, tiled=True),
            lax.all_gather(w_qkv[layer_index], "dp", axis=0, tiled=True),
            lax.all_gather(w_proj[layer_index], "dp", axis=1, tiled=True),
            lax.all_gather(w_fc1[layer_index], "dp", axis=0, tiled=True),
            lax.all_gather(w_fc2[layer_index], "dp", axis=1, tiled=True),
        )
        gain_rows = gain_rows.astype(jnp.float32)
        bias_rows = bias_rows.astype(jnp.float32)
        normed, norm_back = jax.vjp(layer_norm, residual, gain_rows[0], bias_rows[0])
        full_normed = lax.all_gather(normed.astype(jnp.bfloat16), "tensor", axis=0, tiled=True)
        projected = jnp.einsum(
            "tsd,dke->tske", full_normed, qkv_full, preferred_element_type=jnp.float32
        )
        pair_bias = qv_bias[layer_index].astype(jnp.float32)
        queries = to_windows(
            (projected[:, :, 0] + pair_bias[0]).astype(jnp.bfloat16), shifted
        ).reshape(head_shape)
        key_rows = to_windows(projected[:, :, 1].astype(jnp.bfloat16), shifted).reshape(head_shape)
        value_rows = to_windows(
            (projected[:, :, 2] + pair_bias[1]).astype(jnp.bfloat16), shifted
        ).reshape(head_shape)
        bias_add = table_bias(rel_table[layer_index])[None]
        if shifted:
            bias_add = bias_add + plan_mask()[:, None]
        blended, log_total = lax.map(
            lambda pieces: attend_image(pieces, bias_add, scale_factor),
            (queries, key_rows, value_rows),
        )
        out_rows = from_windows(blended.reshape(window_shape), shifted)
        attention = lax.psum_scatter(
            jnp.einsum(
                "tse,ed->tsd", out_rows, proj_full, preferred_element_type=jnp.float32
            ).astype(jnp.bfloat16),
            "tensor",
            scatter_dimension=0,
            tiled=True,
        ).astype(jnp.float32)
        residual_mid = residual + attention + bias_rows[1]
        normed_mid, mid_back = jax.vjp(layer_norm, residual_mid, gain_rows[1], bias_rows[2])
        mid_low = normed_mid.astype(jnp.bfloat16)
        fc1_use, fc2_use, fc1_bias_use = (fc1_full, fc2_full, fc1_bias[layer_index])
        mlp_input = lax.all_gather(mid_low, "tensor", axis=0, tiled=True)
        hidden_pre = jnp.einsum(
            "tsd,df->tsf", mlp_input, fc1_use, preferred_element_type=jnp.float32
        ) + fc1_bias_use.astype(jnp.float32)
        activated, gelu_back = jax.vjp(gelu_exact, hidden_pre)
        act_low = activated.astype(jnp.bfloat16)
        mlp_sum = lax.psum_scatter(
            jnp.einsum("tsf,fd->tsd", act_low, fc2_use, preferred_element_type=jnp.float32).astype(
                jnp.bfloat16
            ),
            "tensor",
            scatter_dimension=0,
            tiled=True,
        ).astype(jnp.float32)
        residual = residual_mid + mlp_sum + bias_rows[3]
        stored.append(
            (
                shifted,
                norm_back,
                mid_back,
                gelu_back,
                full_normed,
                queries,
                key_rows,
                value_rows,
                log_total,
                bias_add,
                out_rows,
                mlp_input,
                act_low,
                qkv_full,
                proj_full,
                fc1_use,
                fc2_use,
            )
        )
    valid_rows = valid.astype(jnp.float32)[None, :, None]
    block_out = (residual * valid_rows).astype(jnp.bfloat16)
    grad_stream = cotangent.astype(jnp.float32) * valid_rows
    results = [None] * LAYERS
    for layer_index in reversed(range(LAYERS)):
        (
            shifted,
            norm_back,
            mid_back,
            gelu_back,
            full_normed,
            queries,
            key_rows,
            value_rows,
            log_total,
            bias_add,
            out_rows,
            mlp_input,
            act_low,
            qkv_full,
            proj_full,
            fc1_use,
            fc2_use,
        ) = stored[layer_index]
        grad_bias_last = jnp.sum(grad_stream, axis=(0, 1))
        grad_low = grad_stream.astype(jnp.bfloat16)
        grad_full = lax.all_gather(grad_low, "tensor", axis=0, tiled=True)
        grad_act = jnp.einsum("tsd,fd->tsf", grad_full, fc2_use, preferred_element_type=jnp.float32)
        grad_pre = gelu_back(grad_act)[0].astype(jnp.bfloat16)
        fc2_grad = jnp.einsum("tsf,tsd->fd", act_low, grad_full, preferred_element_type=jnp.float32)
        fc1_grad = jnp.einsum(
            "tsd,tsf->df", mlp_input, grad_pre, preferred_element_type=jnp.float32
        )
        fc1_bias_grad = jnp.sum(grad_pre, axis=(0, 1), dtype=jnp.float32)
        grad_mid = lax.psum_scatter(
            jnp.einsum("tsf,df->tsd", grad_pre, fc1_use, preferred_element_type=jnp.float32).astype(
                jnp.bfloat16
            ),
            "tensor",
            scatter_dimension=0,
            tiled=True,
        ).astype(jnp.float32)
        grad_res, grad_gain_mid, grad_bias_mid = mid_back(grad_mid)
        grad_stream = grad_stream + grad_res
        grad_bias_attn = jnp.sum(grad_stream, axis=(0, 1))
        grad_attn = lax.all_gather(grad_stream.astype(jnp.bfloat16), "tensor", axis=0, tiled=True)
        proj_grad = jnp.einsum(
            "tse,tsd->ed", out_rows, grad_attn, preferred_element_type=jnp.float32
        )
        grad_out = jnp.einsum(
            "tsd,ed->tse", grad_attn, proj_full, preferred_element_type=jnp.float32
        ).astype(jnp.bfloat16)
        grad_out = to_windows(grad_out, shifted).reshape(head_shape)
        grad_query, grad_key, grad_value, score_sums = lax.map(
            lambda pieces: attend_back(pieces, bias_add, scale_factor),
            (queries, key_rows, value_rows, log_total, grad_out),
        )
        table_grad = table_back(jnp.sum(score_sums, axis=0))
        grad_qkv = jnp.stack(
            [
                from_windows(member.reshape(window_shape), shifted)
                for member in (grad_query, grad_key, grad_value)
            ],
            axis=2,
        )
        qv_grad = jnp.stack(
            [
                jnp.sum(grad_qkv[:, :, 0], axis=(0, 1), dtype=jnp.float32),
                jnp.sum(grad_qkv[:, :, 2], axis=(0, 1), dtype=jnp.float32),
            ]
        )
        qkv_grad = jnp.einsum(
            "tsd,tske->dke", full_normed, grad_qkv, preferred_element_type=jnp.float32
        )
        grad_normed = lax.psum_scatter(
            jnp.einsum(
                "tske,dke->tsd", grad_qkv, qkv_full, preferred_element_type=jnp.float32
            ).astype(jnp.bfloat16),
            "tensor",
            scatter_dimension=0,
            tiled=True,
        ).astype(jnp.float32)
        grad_res, grad_gain_first, grad_bias_first = norm_back(grad_normed)
        grad_stream = grad_stream + grad_res
        gain_grads = jnp.stack([grad_gain_first, grad_gain_mid])
        bias_grads = jnp.stack([grad_bias_first, grad_bias_attn, grad_bias_mid, grad_bias_last])
        gain_grads, bias_grads = lax.psum((gain_grads, bias_grads), "tensor")
        shard_grads = (
            lax.psum_scatter(
                gain_grads.astype(jnp.bfloat16), "dp", scatter_dimension=1, tiled=True
            ).astype(jnp.float32),
            lax.psum_scatter(
                bias_grads.astype(jnp.bfloat16), "dp", scatter_dimension=1, tiled=True
            ).astype(jnp.float32),
            lax.psum_scatter(
                qkv_grad.astype(jnp.bfloat16), "dp", scatter_dimension=0, tiled=True
            ).astype(jnp.float32),
            lax.psum_scatter(
                proj_grad.astype(jnp.bfloat16), "dp", scatter_dimension=1, tiled=True
            ).astype(jnp.float32),
            lax.psum_scatter(
                fc1_grad.astype(jnp.bfloat16), "dp", scatter_dimension=0, tiled=True
            ).astype(jnp.float32),
            lax.psum_scatter(
                fc2_grad.astype(jnp.bfloat16), "dp", scatter_dimension=1, tiled=True
            ).astype(jnp.float32),
        )
        small_grads = lax.psum((qv_grad, fc1_bias_grad, table_grad), "dp")
        results[layer_index] = tuple(shard_grads) + tuple(small_grads)
    stacked = [
        jnp.stack([results[which_layer][member] for which_layer in range(LAYERS)])
        for member in range(9)
    ]
    (
        grad_row_gain,
        grad_row_bias,
        grad_w_qkv,
        grad_w_proj,
        grad_w_fc1,
        grad_w_fc2,
        grad_qv_bias,
        grad_fc1_bias,
        grad_rel_table,
    ) = stacked
    return (
        block_out,
        grad_stream,
        grad_row_gain,
        grad_row_bias,
        grad_w_qkv,
        grad_qv_bias,
        grad_w_proj,
        grad_w_fc1,
        grad_fc1_bias,
        grad_w_fc2,
        grad_rel_table,
    )


def unit_stack(w_qkv, w_proj, w_fc1, w_fc2):
    layers, rows = w_qkv.shape[:2]
    qkv = jnp.transpose(w_qkv, (0, 2, 1, 3))
    proj = jnp.swapaxes(w_proj, 1, 2)[:, None]
    fc1 = jnp.transpose(w_fc1.reshape(layers, rows, 4, UC), (0, 2, 1, 3))
    fc2 = jnp.transpose(w_fc2.reshape(layers, 4, UC, rows), (0, 1, 3, 2))
    ff = jnp.stack([fc1, fc2], axis=2).reshape(layers, 8, rows, UC)
    return jnp.concatenate([qkv, proj, ff], axis=1).reshape(layers * NU, rows, UC)


def unit_split(units):
    rows = units.shape[2]
    qkv = jnp.transpose(units[:, :3], (0, 2, 1, 3))
    proj = jnp.swapaxes(units[:, 3], 1, 2)
    fc1 = jnp.transpose(units[:, 4:8], (0, 2, 1, 3)).reshape(LAYERS, rows, 4 * UC)
    fc2 = jnp.transpose(units[:, 8:], (0, 1, 3, 2)).reshape(LAYERS, 4 * UC, rows)
    return qkv, proj, fc1, fc2


def image_shards(tokens, valid, cotangent, row_gain, row_bias, w_qkv, qv_bias, w_proj, w_fc1, fc1_bias, w_fc2, rel_table):
    d = lax.axis_index("dp")
    shard = unit_stack(w_qkv, w_proj, w_fc1, w_fc2)
    vecs = jnp.concatenate([row_gain, row_bias], axis=1).reshape(LAYERS * 6, 48)
    vshard = jnp.pad(vecs.T, ((0, 0), (0, 128 - LAYERS * 6)))[None]
    rows = jnp.concatenate([qv_bias.reshape(2 * LAYERS, UC), fc1_bias.reshape(4 * LAYERS, UC)]).astype(F32)
    pay = jnp.concatenate([jnp.pad(rows, ((0, 4), (0, PAY - UC))),
                           jnp.pad(rel_table.reshape(LAYERS * 12, RELS), ((0, 0), (0, PAY - RELS)))])
    block, vec, cot, w, *saved = forward_call(
        jnp.swapaxes(tokens, 0, 1), jnp.swapaxes(cotangent, 0, 1), valid, vshard, pay, shard)
    gt, block, total, small = backward_call(cot, valid, vec, block, w, *saved)
    qkv_g, proj_g, fc1_g, fc2_g = unit_split(total)
    rowg = lax.dynamic_slice(small[:, 1], (0, 0, d * 48), (LAYERS, 6, 48))
    own = small[:, 0]
    return (jnp.swapaxes(block, 0, 1), jnp.swapaxes(gt, 0, 1), rowg[:, :2], rowg[:, 2:], qkv_g, own[:, 12:14, :UC],
            proj_g, fc1_g, own[:, 14:16].reshape(LAYERS, 4 * UC), fc2_g, own[:, :12, :RELS])


def solution(mesh):
    whole_images = mesh.shape["tensor"] == 2 and mesh.shape["dp"] == 16
    return jax.shard_map(
        image_shards if whole_images else shards,
        mesh=mesh,
        in_specs=(
            P("tensor", "dp", None),
            P("dp"),
            P("tensor", "dp", None),
            P(None, None, "dp"),
            P(None, None, "dp"),
            P(None, "dp", None, "tensor"),
            P(None, None, "tensor"),
            P(None, "tensor", "dp"),
            P(None, "dp", "tensor"),
            P(None, "tensor"),
            P(None, "tensor", "dp"),
            P(None, "tensor", None),
        ),
        out_specs=(
            P("tensor", "dp", None),
            P("tensor", "dp", None),
            P(None, None, "dp"),
            P(None, None, "dp"),
            P(None, "dp", None, "tensor"),
            P(None, None, "tensor"),
            P(None, "tensor", "dp"),
            P(None, "dp", "tensor"),
            P(None, "tensor"),
            P(None, "tensor", "dp"),
            P(None, "tensor", None),
        ),
        check_vma=False,
    )
```

```python
import functools
import numpy as np
import jax
import jax.numpy as jnp
from jax import lax
from jax.experimental import pallas as pl
from jax.experimental.pallas import tpu as pltpu
from jax.sharding import PartitionSpec as P

WIN = 12
LAYERS = 2
HDIM = 32
SIDE = 24
SHIFT = 6
RELS = 529
EPSILON = 1e-05
MASK_FILL = -100.0

D = 768
HEADS = 24
FF = 3072
TOK = 576
WT = 144
UC = 384
NU = 12
HG = 4
NG = HEADS // HG
SCALE = HDIM ** -0.5
BF = jnp.bfloat16
F32 = jnp.float32


def nn(a, b):
    return lax.dot_general(a, b, (((1,), (0,)), ((), ())), preferred_element_type=F32)


def nt(a, b):
    return lax.dot_general(a, b, (((1,), (1,)), ((), ())), preferred_element_type=F32)


def norm_parts(x):
    mean = jnp.mean(x, axis=-1, keepdims=True)
    c = x - mean
    var = jnp.mean(c * c, axis=-1, keepdims=True)
    rstd = lax.rsqrt(var + EPSILON)
    return c * rstd, rstd


def gelu_parts(u):
    phi_big = 0.5 * (1.0 + lax.erf(u * (0.5 ** 0.5)))
    phi = jnp.exp(-0.5 * u * u) * (1.0 / (2.0 * np.pi) ** 0.5)
    return u * phi_big, phi_big + u * phi


def window_order():
    out = []
    for shift in (0, SHIFT):
        p = np.arange(SIDE)
        src = (p + shift) % SIDE
        grid = src[:, None] * SIDE + src[None, :]
        grid = grid.reshape(2, WIN, 2, WIN).transpose(0, 2, 1, 3).reshape(TOK)
        out.append(grid)
    return np.stack(out)


def perm_matrices():
    order = window_order()
    return (order[:, :, None] == np.arange(TOK)[None, None, :]).astype(np.float32)


def shift_mask():
    places = np.arange(SIDE)
    band_of = (places >= SIDE - WIN).astype(np.int32) + (places >= SIDE - SHIFT).astype(np.int32)
    region = band_of[:, None] * 3 + band_of[None, :]
    region = region.reshape(2, WIN, 2, WIN).transpose(0, 2, 1, 3).reshape(4, WT)
    same = region[:, :, None] == region[:, None, :]
    masked = np.where(same, 0.0, MASK_FILL).astype(np.float32)
    return np.tile(np.stack([np.zeros_like(masked), masked]), (1, 1, 1, HG))


def rows_loop(n, body):
    def step(i, c):
        body(i)
        return c
    lax.fori_loop(0, n, step, 0)


def w2d(wbuf, slot):
    return wbuf[slot].reshape(D, 2 * UC)


class Fetch:
    def __init__(self, w_hbm, wbuf, sem, g, slot):
        self.copies = [pltpu.make_async_copy(w_hbm.at[g, t], wbuf.at[slot, :, :, :, :, t * UC:(t + 1) * UC], sem.at[slot, t])
                       for t in range(2)]

    def start(self):
        for cp in self.copies:
            cp.start()

    def wait(self):
        for cp in self.copies:
            cp.wait()


class Place:
    def __init__(self):
        d, self.t = lax.axis_index("dp"), lax.axis_index("tensor")
        self.z = lax.div(d, 4)
        self.y = lax.rem(lax.div(d, 2), 2)
        self.c = lax.rem(d, 2)
        t, y, even = self.t, self.y, self.c == 0
        self.x_side, self.y_side = (1 - t, y), (t, 1 - y)
        self.first = tuple(jnp.where(even, a, b) for a, b in zip(self.x_side, self.y_side))
        self.second = tuple(jnp.where(even, b, a) for a, b in zip(self.x_side, self.y_side))
        self.diagonal = (1 - t, 1 - y)

    def device(self, z, ty, c):
        return {"dp": (z * 2 + ty[1]) * 2 + c, "tensor": ty[0]}

    def side(self, ty):
        return self.device(self.z, ty, self.c)

    def along(self, k):
        return lax.rem(self.z + k, 4)

    def above(self, k):
        return self.device(self.along(k), (self.t, self.y), self.c)

    def sibling(self):
        return self.device(self.z, (self.t, self.y), 1 - self.c)

    def barrier(self):
        sem = pltpu.get_barrier_semaphore()
        peers = [self.above(k) for k in (1, 2, 3)] + [self.side(self.x_side), self.side(self.y_side), self.sibling()]
        for peer in peers:
            pl.semaphore_signal(sem, inc=1, device_id=peer, device_id_type=MESH)
        pl.semaphore_wait(sem, len(peers))


MESH = pl.DeviceIdType.MESH
GATHER_LAGS = (2, 4, 6, 7)
GATHER_SEMS = 12
TICK_EVERY = (12, 6)


class Gather:
    def __init__(self, at, shard, whole, send, recv, local, units):
        self.at, self.shard, self.whole, self.units = at, shard, whole, units
        self.send, self.recv, self.local = send, recv, local

    def copy(self, g, n, src, dst, device):
        slot = lax.rem(g, GATHER_SEMS) if self.units > 1 else 0
        return pltpu.make_async_remote_copy(
            src_ref=src, dst_ref=dst, send_sem=self.send.at[slot, n], recv_sem=self.recv.at[slot, n],
            device_id=device, device_id_type=MESH)

    def mine(self, g):
        p = self.at
        return pltpu.make_async_copy(self.shard.at[g], self.whole.at[g, p.t, p.z, p.y, p.c],
                                     self.local.at[lax.rem(g, GATHER_SEMS) if self.units > 1 else 0])

    def up(self, g, k):
        p = self.at
        return self.copy(g, k - 1, self.shard.at[g], self.whole.at[g, p.t, p.z, p.y, p.c], p.above(k))

    def group(self, g, n, ty, to):
        ref = self.whole.at[g, ty[0], :, ty[1], self.at.c]
        return self.copy(g, n, ref, ref, self.at.side(to))

    def first(self, g):
        return self.group(g, 3, (self.at.t, self.at.y), self.at.first)

    def second(self, g):
        return self.group(g, 4, (self.at.t, self.at.y), self.at.second)

    def onward(self, g):
        return self.group(g, 5, self.at.first, self.at.second)

    def core(self, g):
        ref = self.whole.at[g, :, :, :, self.at.c]
        return self.copy(g, 6, ref, ref, self.at.sibling())

    def stage(self, n, g):
        if n == 0:
            self.mine(g).start()
            for k in (1, 2, 3):
                self.up(g, k).start()
        elif n == 1:
            self.mine(g).wait()
            for k in (1, 2, 3):
                self.up(g, k).wait_recv()
            self.first(g).start()
            self.second(g).start()
        elif n == 2:
            self.first(g).wait_recv()
            self.onward(g).start()
        elif n == 3:
            self.second(g).wait_recv()
            self.onward(g).wait_recv()
            self.core(g).start()
        else:
            self.core(g).wait()
            for k in (1, 2, 3):
                self.up(g, k).wait_send()
            self.first(g).wait_send()
            self.second(g).wait_send()
            self.onward(g).wait_send()

    def tick(self, n):
        for st in (4, 3, 2, 1, 0):
            g = n - (GATHER_LAGS[st - 1] if st else 0)
            if isinstance(g, int):
                if 0 <= g < self.units:
                    self.stage(st, g)
            else:
                @pl.when((g >= 0) & (g < self.units))
                def _(st=st, g=g):
                    self.stage(st, g)


def fold_places():
    lane = np.arange(UC)
    j, xa = lane // WIN, lane % WIN
    return np.where(j < 2 * WIN - 1, j * (2 * WIN - 1) + xa + WIN - 1, -4 * PAY).astype(np.int32)[None]


def fold_matrix(places, xb):
    rows = lax.broadcasted_iota(jnp.int32, (PAY, UC), 0)
    return jnp.where(rows == places - xb, 1.0, 0.0).astype(BF)


def split3(x):
    hi = x.astype(BF)
    rest = x - hi.astype(F32)
    mid = rest.astype(BF)
    return hi, mid, (rest - mid.astype(F32)).astype(BF)


HT = HG * WT
CHUNKS = [slice(i, min(i + 128, HT)) for i in range(0, HT, 128)]


def by_head(x, lanes):
    return jnp.concatenate([jnp.where(lanes == h, x, jnp.zeros_like(x)) for h in range(HG)], axis=0)


def own_blocks(x):
    return jnp.concatenate([x[h * HDIM:(h + 1) * HDIM, h * WT:(h + 1) * WT] for h in range(HG)], axis=0).T


def half_rows(t):
    return pl.ds(pl.multiple_of(t * HALF, HALF), HALF)


def forward_kernel(tok, cot, valid, vshard, pay, places, mask, perm, permt, shard,
                   out, vec, cot_h, w_hbm, x0_h, x1_h, n1_h, qkv_h, pw_h, o_h, n2_h, gg_h,
                   wbuf, x0, x1, n1, qkv, ow, n2, acc, pst, gst, ubuf,
                   xin, vall, pays, ext, bias, scores,
                   wsem, ssem, psem, gsem, gsend, grecv, glocal, vsend, vrecv, vlocal, xsend, xrecv, xlocal):
    at = Place()
    ag = Gather(at, shard, w_hbm, gsend, grecv, glocal, LAYERS * NU)
    vg = Gather(at, vshard, vall, vsend, vrecv, vlocal, 1)
    at.barrier()
    lag = GATHER_LAGS[-1]
    t = at.t
    mine, theirs = half_rows(t), half_rows(1 - t)
    swaps, keeps = [], []
    for n, (src, here, src_keep) in enumerate((
            (tok.at[1 - t], xin.at[mine], tok.at[t]),
            (pay, pays.at[t], pay),
            (cot.at[1 - t], cot_h.at[mine], cot.at[t]))):
        swaps.append(pltpu.make_async_remote_copy(
            src_ref=src, dst_ref=here, send_sem=xsend.at[n], recv_sem=xrecv.at[n],
            device_id=at.side(at.x_side), device_id_type=MESH))
        keeps.append(pltpu.make_async_copy(src_keep, here, xlocal.at[n]))
    for n in range(2):
        swaps[n].start()
        keeps[n].start()
    def both(row):
        return jnp.concatenate([pays[0, pl.ds(row, 1), :UC], pays[1, pl.ds(row, 1), :UC]], axis=1)

    def vrow(l, i):
        return vec[pl.ds(l * 6 + i, 1)]

    def spread(i, c):
        half, l, g = lax.div(i, 6), lax.rem(lax.div(i, 3), 2), lax.rem(i, 3)
        for h in range(HG):
            x = ext[half * 24 + l * 12 + g * HG + h]
            for yb in range(WIN):
                off = (WIN - 1 - yb) * WIN
                bias[l, half * 3 + g, yb * WIN:(yb + 1) * WIN, h * WT:(h + 1) * WT] = x[:, off:off + WT]
        return c

    def norm_first(l):
        def ln1(i):
            r = pl.ds(i * WT, WT)
            xh, _ = norm_parts(x0[l, r])
            ow[l, r] = (xh * vrow(l, 0) + vrow(l, 2)).astype(BF)
        rows_loop(4, ln1)
        n1[l] = nn(perm[l], ow[l]).astype(BF)

    for n in range(lag + 1):
        if n < 5:
            vg.stage(n, 0)
        ag.tick(n)
        if n == 0:
            swaps[1].wait()
            keeps[1].wait()
            table = jnp.concatenate([pays[0, 16:40], pays[1, 16:40]], axis=0)
            parts = jnp.concatenate(split3(table), axis=0)
            for xa in range(WIN):
                y = nn(parts, fold_matrix(places[...], xa))
                ext[:, xa, :] = y[:48] + y[48:96] + y[96:]
        if n == 2:
            lax.fori_loop(0, 6, spread, 0)
        if n == 3:
            lax.fori_loop(6, 12, spread, 0)
        if n == 4:
            vec[...] = vall[0, 0].reshape(D, 128).astype(F32).T[:16]
            swaps[0].wait()
            keeps[0].wait()
            x0[0] = xin[...].astype(F32)
        if n == 5:
            norm_first(0)

    def fetch(g, u):
        return Fetch(w_hbm, wbuf, wsem, g, u % 2)

    def tick_base(l, u):
        before, inside = (4 * NG // every for every in TICK_EVERY)
        return lag + 1 + l * (NU + before) + u + (jnp.where(l == 0, before, inside) if u >= 3 else 0)

    def step_unit(l, u):
        g = l * NU + u
        fetch(g, u).wait()
        ag.tick(tick_base(l, u))

        @pl.when(g + 1 < LAYERS * NU)
        def _():
            fetch(g + 1, u + 1).start()

    fetch(0, 0).start()
    lanes = lax.shift_right_logical(lax.broadcasted_iota(jnp.int32, (WT, HG * HDIM), 1), 5)

    kept = ((x0, x0_h), (x1, x1_h), (n1, n1_h), (qkv, qkv_h), (ow, o_h), (n2, n2_h))

    def save(l, *which):
        for n in which:
            pltpu.make_async_copy(kept[n][0].at[l], kept[n][1].at[l], ssem.at[l]).start()

    def layer(l, carry):
        x0_l, x1_l, n1_l, n2_l, ow_l = x0.at[l], x1.at[l], n1.at[l], n2.at[l], ow.at[l]

        @pl.when(l > 0)
        def _():
            norm_first(l)
        for j in range(3):
            step_unit(l, j)
            y = nn(n1_l[...], w2d(wbuf, j % 2))
            if j != 1:
                y = y + both(l * 2 + j // 2)
            qkv[l, j] = y.astype(BF)
        save(l, 0, 2, 3)

        def attend(it, c):
            w, hg = lax.div(it, NG), lax.rem(it, NG)
            r = pl.ds(pl.multiple_of(w * WT, WT), WT)
            cl = pl.ds(pl.multiple_of(hg * 128, 128), 128)
            slot = lax.rem(it, 2)
            q, k, v = qkv[l, 0, r, cl], qkv[l, 1, r, cl], qkv[l, 2, r, cl]
            put = pltpu.make_async_copy(pst.at[slot], pw_h.at[l, w, hg], psem.at[slot])

            @pl.when((it >= 2) | (l > 0))
            def _():
                put.wait()
            scores[...] = nt(k, by_head(q, lanes))
            for ch in CHUNKS:
                x = scores[:, ch] * SCALE + bias[l, hg, :, ch] + mask[l, w, :, ch]
                x = jnp.exp(x - jnp.max(x, axis=0, keepdims=True))
                pst[slot, :, ch] = (x * (1.0 / jnp.sum(x, axis=0, keepdims=True))).astype(BF)
            ow_l[r, cl] = own_blocks(nn(v.T, pst[slot])).astype(BF)
            put.start()

            every = jnp.where(l == 0, TICK_EVERY[0], TICK_EVERY[1])

            @pl.when(lax.rem(it, every) == every - 1)
            def _():
                ag.tick(tick_base(l, 2) + 1 + lax.div(it, every))
            return c
        lax.fori_loop(0, 4 * NG, attend, 0)

        save(l, 4)

        @pl.when(l == LAYERS - 1)
        def _():
            swaps[2].start()
            keeps[2].start()
        n2_l[...] = nn(permt[l], ow_l[...]).astype(BF)
        step_unit(l, 3)
        acc[...] = nt(n2_l[...], w2d(wbuf, 1))

        def ln2(i):
            r = pl.ds(i * WT, WT)
            x = x0_l[r] + acc[r] + vrow(l, 3)
            x1_l[r] = x
            xh, _ = norm_parts(x)
            n2_l[r] = (xh * vrow(l, 1) + vrow(l, 4)).astype(BF)
            acc[r] = x + vrow(l, 5)
        rows_loop(4, ln2)
        save(l, 1, 5)
        for i in range(4):
            step_unit(l, 4 + 2 * i)
            put = pltpu.make_async_copy(gst.at[i % 2], gg_h.at[l, i], gsem.at[i % 2])
            if i > 1:
                put.wait()
            else:
                @pl.when(l > 0)
                def _():
                    put.wait()
            ubuf[...] = nn(n2_l[...], w2d(wbuf, 0)) + both(4 + l * 4 + i)

            def act(n):
                r = pl.ds(n * 48, 48)
                g, gp = gelu_parts(ubuf[r])
                gst[i % 2, 0, r] = g.astype(BF)
                gst[i % 2, 1, r] = gp.astype(BF)
            rows_loop(12, act)
            put.start()
            step_unit(l, 5 + 2 * i)
            acc[...] += nt(gst[i % 2, 0], w2d(wbuf, 1))

        @pl.when(l == 0)
        def _():
            x0[1] = acc[...]

        @pl.when(l == 1)
        def _():
            out[...] = (acc[...] * valid[at.t].astype(F32)).astype(BF)
        return carry
    lax.fori_loop(0, LAYERS, layer, 0)
    for l in range(LAYERS):
        for ref, dst in kept:
            pltpu.make_async_copy(ref.at[l], dst.at[l], ssem.at[l]).wait()
    for s in range(2):
        pltpu.make_async_copy(pst.at[s], pw_h.at[0, 0, 0], psem.at[s]).wait()
        pltpu.make_async_copy(gst.at[s], gg_h.at[0, s], gsem.at[s]).wait()
    swaps[2].wait()
    keeps[2].wait()


def sds(shape, dtype):
    return jax.ShapeDtypeStruct(shape, dtype)


VM = pl.BlockSpec(memory_space=pltpu.VMEM)
AN = pl.BlockSpec(memory_space=pl.ANY)
SM = pl.BlockSpec(memory_space=pltpu.SMEM)

SAVED = [
    sds((LAYERS, TOK, D), F32), sds((LAYERS, TOK, D), F32), sds((LAYERS, TOK, D), BF),
    sds((LAYERS, 3, TOK, D), BF), sds((LAYERS, 4, NG, WT, HT), BF),
    sds((LAYERS, TOK, D), BF), sds((LAYERS, TOK, D), BF), sds((LAYERS, 4, 2, TOK, 2 * UC), BF),
]


def forward_call(tok, cot, valid, vshard, pay, shard):
    perm = perm_matrices()
    permt = jnp.asarray(perm.transpose(0, 2, 1), BF)
    return pl.pallas_call(
        forward_kernel,
        out_shape=[sds((TOK, D), BF), sds((16, D), F32), sds((TOK, D), BF),
                   sds((LAYERS * NU, 2, 4, 2, 2, 48, UC), BF)] + SAVED,
        in_specs=[AN, AN, SM, AN, AN, VM, VM, VM, VM, AN],
        out_specs=[VM, VM] + [AN] * 10,
        scratch_shapes=[
            pltpu.VMEM((2, 4, 2, 2, 48, 2 * UC), BF),
            pltpu.VMEM((2, TOK, D), F32), pltpu.VMEM((2, TOK, D), F32),
            pltpu.VMEM((2, TOK, D), BF), pltpu.VMEM((2, 3, TOK, D), BF),
            pltpu.VMEM((2, TOK, D), BF), pltpu.VMEM((2, TOK, D), BF),
            pltpu.VMEM((TOK, D), F32), pltpu.VMEM((2, WT, HT), BF),
            pltpu.VMEM((2, 2, TOK, 2 * UC), BF), pltpu.VMEM((TOK, 2 * UC), F32),
            pltpu.VMEM((TOK, D), BF), pltpu.VMEM((1, 2, 4, 2, 2, 48, 128), BF),
            pltpu.VMEM((2, 40, PAY), F32), pltpu.VMEM((48, WIN, UC), F32),
            pltpu.VMEM((LAYERS, NG, WT, HT), F32), pltpu.VMEM((WT, HT), F32),
            pltpu.SemaphoreType.DMA((2, 2)), pltpu.SemaphoreType.DMA((2,)),
            pltpu.SemaphoreType.DMA((2,)), pltpu.SemaphoreType.DMA((2,)),
            pltpu.SemaphoreType.DMA((GATHER_SEMS, 7)), pltpu.SemaphoreType.DMA((GATHER_SEMS, 7)),
            pltpu.SemaphoreType.DMA((GATHER_SEMS,)),
            pltpu.SemaphoreType.DMA((1, 7)), pltpu.SemaphoreType.DMA((1, 7)), pltpu.SemaphoreType.DMA((1,)),
            pltpu.SemaphoreType.DMA((3,)), pltpu.SemaphoreType.DMA((3,)), pltpu.SemaphoreType.DMA((3,)),
        ],
        compiler_params=pltpu.CompilerParams(vmem_limit_bytes=60 * 2**20, collective_id=0, has_side_effects=True),
        name="forward",
    )(tok, cot, valid, vshard, pay, fold_places(), shift_mask(), jnp.asarray(perm, BF), permt, shard)


BACK_ORDER = (5, 4, 7, 6, 9, 8, 11, 10, 3, 0, 1, 2)


def norm_back(x, dn, gain):
    xh, rstd = norm_parts(x)
    dx = dn * gain
    grad = rstd * (dx - jnp.mean(dx, axis=-1, keepdims=True)
                   - xh * jnp.mean(dx * xh, axis=-1, keepdims=True))
    return grad, jnp.sum(dn * xh, axis=0, keepdims=True), jnp.sum(dn, axis=0, keepdims=True)


REDUCE_SLOTS = NU
CORE_SLOTS = 4
PAY = 640
HALF = TOK // 2
VIRT = 16
GAP = (9, 13)
REDUCE_LAGS = (1, 6, 10, 14)


class Reduce:
    def __init__(self, at, own, core_in, first_in, second_in, z_in, total, send, recv):
        self.at, self.own, self.total = at, own, total
        self.core_in, self.first_in, self.second_in, self.z_in = core_in, first_in, second_in, z_in
        self.send, self.recv = send, recv

    def slot(self, v):
        place = lax.rem(v, VIRT)
        return jnp.where(place < GAP[0], place, place - (GAP[1] - GAP[0]))

    def copy(self, v, n, src, dst, device):
        slot = self.slot(v)
        return pltpu.make_async_remote_copy(
            src_ref=src, dst_ref=dst, send_sem=self.send.at[slot, n], recv_sem=self.recv.at[slot, n],
            device_id=device, device_id_type=MESH)

    def core(self, v):
        slot = lax.rem(self.slot(v), CORE_SLOTS)
        return self.copy(v, 0, self.own.at[REDUCE_SLOTS + slot], self.core_in.at[slot], self.at.sibling())

    def put(self, v, value):
        value = value.astype(BF)
        mine, other = self.slot(v), REDUCE_SLOTS + lax.rem(self.slot(v), CORE_SLOTS)
        for t in range(2):
            x = value[:, t * UC:(t + 1) * UC].reshape(4, 2, 2, 48, UC)
            for k in range(2):
                self.own[jnp.where(self.at.c == k, mine, other), t] = x[:, :, k]

    def group(self, v, ty):
        return self.own.at[self.slot(v), ty[0], :, ty[1]]

    def first(self, v, n):
        p = self.at
        ty = p.diagonal if n == 0 else p.second
        return self.copy(v, 1 + n, self.group(v, ty), self.first_in.at[self.slot(v), n], p.side(p.second))

    def second(self, v):
        p = self.at
        return self.copy(v, 3, self.group(v, p.first), self.second_in.at[self.slot(v)], p.side(p.first))

    def up(self, v, k):
        p, slot = self.at, self.slot(v)
        return self.copy(v, 3 + k, self.own.at[slot, p.t, p.along(k), p.y], self.z_in.at[slot, k - 1], p.above(k))

    def add(self, ref, other):
        def one(z):
            ref[z] = ref[z] + other[z]
        rows_loop(4, one)

    def stage(self, n, v):
        p, slot = self.at, self.slot(v)
        if n == 0:
            self.core(v).start()
        elif n == 1:
            self.core(v).wait()

            def one(i):
                t, z = lax.div(i, 4), lax.rem(i, 4)
                self.own[slot, t, z] = self.own[slot, t, z] + self.core_in[lax.rem(self.slot(v), CORE_SLOTS), t, z]
            rows_loop(8, one)
            self.first(v, 0).start()
            self.first(v, 1).start()
        elif n == 2:
            self.first(v, 0).wait_recv()
            self.add(self.group(v, p.first), self.first_in.at[slot, 0])
            self.second(v).start()
            self.first(v, 1).wait_recv()
            self.add(self.group(v, (p.t, p.y)), self.first_in.at[slot, 1])
        elif n == 3:
            self.second(v).wait_recv()
            self.add(self.group(v, (p.t, p.y)), self.second_in.at[slot])
            for k in (1, 2, 3):
                self.up(v, k).start()
        else:
            total = self.own[slot, p.t, p.z, p.y].astype(F32)
            for k in (1, 2, 3):
                self.up(v, k).wait_recv()
                total = total + self.z_in[slot, k - 1].astype(F32)
            ff = jnp.where(lax.rem(slot, 2) == 0, 8, 4) + lax.div(slot, 2)
            unit = jnp.where(slot < 8, ff, jnp.where(slot == 8, 3, slot - 9))
            self.total[LAYERS - 1 - lax.div(v, VIRT), unit] = total
            for n in range(2):
                self.first(v, n).wait_send()
            self.second(v).wait_send()
            for k in (1, 2, 3):
                self.up(v, k).wait_send()

    def tick(self, n):
        for st in (4, 3, 2, 1, 0):
            v = n - (REDUCE_LAGS[st - 1] if st else 0)
            place = lax.rem(v, VIRT)

            @pl.when((v >= 0) & (v < LAYERS * VIRT) & ((place < GAP[0]) | (place >= GAP[1])))
            def _(st=st, v=v):
                self.stage(st, v)


def backward_kernel(cot, valid, vec, places, perm, permt, block, w_hbm, x0_h, x1_h, n1_h, qkv_h, pw_h, o_h, n2_h, gg_h,
                    gt, block2, total, small,
                    e, scores, ds, sums, folded, dsum, sm_core, sm_x, sm_y, sm_z, gin,
                    wbuf, xb, n1, n2, qkv, ow, do, dqkv, acc, em, emt, n2t, pst, gst, ubuf, dub, gbuf,
                    core_in, first_in, second_in, z_in,
                    wsem, lsem, psem, gsem, rsend, rrecv, xsend, xrecv, xlocal, ssend, srecv):
    at = Place()
    t_here = at.t
    mine, theirs = half_rows(t_here), half_rows(1 - t_here)
    rs = Reduce(at, gbuf, core_in, first_in, second_in, z_in, total, rsend, rrecv)

    def fetch(g, pos):
        return Fetch(w_hbm, wbuf, wsem, g, pos % 2)

    def step_unit(l, pos):
        fetch(0, pos).wait()
        if pos + 1 < NU:
            fetch(l * NU + BACK_ORDER[pos + 1], pos + 1).start()
        else:
            @pl.when(l > 0)
            def _():
                fetch((l - 1) * NU + BACK_ORDER[0], 0).start()

    def place_of(pos):
        return pos if pos < GAP[0] else pos + GAP[1] - GAP[0]

    def emit(l, pos, value):
        v = (LAYERS - 1 - l) * VIRT + place_of(pos)
        rs.put(v, value)
        rs.tick(v)

    fetch((LAYERS - 1) * NU + BACK_ORDER[0], 0).start()
    at.barrier()
    block_swap = pltpu.make_async_remote_copy(
        src_ref=block.at[theirs], dst_ref=block2.at[t_here], send_sem=xsend.at[0], recv_sem=xrecv.at[0],
        device_id=at.side(at.x_side), device_id_type=MESH)
    block_keep = pltpu.make_async_copy(block.at[mine], block2.at[t_here], xlocal.at[0])
    block_swap.start()
    block_keep.start()
    total[...] = jnp.zeros_like(total)
    e[...] = cot[...].astype(F32) * valid[at.t].astype(F32)
    sums[...] = jnp.zeros_like(sums)
    lanes = lax.shift_right_logical(lax.broadcasted_iota(jnp.int32, (WT, HG * HDIM), 1), 5)

    def layer(step, carry):
        l = LAYERS - 1 - step
        loads = [pltpu.make_async_copy(src.at[l], dst, lsem.at[n]) for n, (src, dst) in enumerate((
            (n2_h, n2), (x1_h, xb), (o_h, ow), (qkv_h, qkv), (n1_h, n1), (x0_h, xb)))]
        for cp in loads[:5]:
            cp.start()

        def load_gg(k):
            return pltpu.make_async_copy(gg_h.at[l, k], gst.at[k % 2], gsem.at[k % 2])
        load_gg(0).start()
        load_gg(1).start()

        def ends(i):
            r = pl.ds(i * WT, WT)
            x = e[r]
            em[r] = x.astype(BF)
            sums[l, 2, 5:6] += jnp.sum(x, axis=0, keepdims=True)
        rows_loop(4, ends)
        emt[...] = em[...].T
        loads[0].wait()
        n2t[...] = n2[...].T
        for i in range(4):
            step_unit(l, 2 * i)
            load_gg(i).wait()
            ubuf[...] = nn(em[...], w2d(wbuf, 0))

            def act(n, c):
                r = pl.ds(n * 48, 48)
                du = (ubuf[r] * gst[i % 2, 1, r].astype(F32)).astype(BF)
                dub[r] = du
                return c + jnp.sum(du.astype(F32), axis=0, keepdims=True)
            y = lax.fori_loop(0, 12, act, jnp.zeros((1, 2 * UC), F32))
            for t in range(2):
                sums[l, t, 14 + i // 2:15 + i // 2, (i % 2) * UC:(i % 2 + 1) * UC] = y[:, t * UC:(t + 1) * UC]
            emit(l, 2 * i, nn(emt[...], gst[i % 2, 0]))
            if i < 2:
                load_gg(i + 2).start()
            step_unit(l, 2 * i + 1)
            y = nt(dub[...], w2d(wbuf, 1))
            if i == 0:
                acc[...] = y
            else:
                acc[...] += y
            emit(l, 2 * i + 1, nn(n2t[...], dub[...]))
        loads[1].wait()

        def ln2(i):
            r = pl.ds(i * WT, WT)
            grad, gsum, bsum = norm_back(xb[r], acc[r], vec[pl.ds(l * 6 + 1, 1)])
            x = e[r] + grad
            e[r] = x
            em[r] = x.astype(BF)
            sums[l, 2, 1:2] += gsum
            sums[l, 2, 4:5] += bsum
            sums[l, 2, 3:4] += jnp.sum(x, axis=0, keepdims=True)
        rows_loop(4, ln2)
        loads[5].start()
        n2[...] = nn(perm[l], em[...]).astype(BF)
        emt[...] = n2[...].T
        step_unit(l, 8)
        loads[2].wait()
        do[...] = nn(n2[...], w2d(wbuf, 0)).astype(BF)
        emit(l, 8, nn(emt[...], ow[...]))
        loads[3].wait()

        def load_pw(it):
            w, hg = lax.div(it, NG), lax.rem(it, NG)
            return pltpu.make_async_copy(pw_h.at[l, w, hg], pst.at[lax.rem(it, 2)], psem.at[lax.rem(it, 2)])
        load_pw(0).start()
        dsum[l] = jnp.zeros((NG, WT, HT), F32)

        def attend(it, c):
            w, hg = lax.div(it, NG), lax.rem(it, NG)
            r = pl.ds(pl.multiple_of(w * WT, WT), WT)
            cl = pl.ds(pl.multiple_of(hg * 128, 128), 128)
            slot = lax.rem(it, 2)

            @pl.when(it + 1 < 4 * NG)
            def _():
                load_pw(it + 1).start()
            q, k, v, d = qkv[0, r, cl], qkv[1, r, cl], qkv[2, r, cl], do[r, cl]
            q4, d4 = by_head(q, lanes), by_head(d, lanes)
            scores[...] = nt(v, d4)
            load_pw(it).wait()
            for ch in CHUNKS:
                p = pst[slot, :, ch].astype(F32)
                x = scores[:, ch]
                mean = jnp.sum(p * x, axis=0, keepdims=True) / jnp.sum(p, axis=0, keepdims=True)
                x = (p * (x - mean)).astype(BF)
                ds[:, ch] = x
                dsum[l, hg, :, ch] += x.astype(F32)
            dqkv[0, r, cl] = (own_blocks(nn(k.T, ds[...])) * SCALE).astype(BF)
            dqkv[1, r, cl] = (nn(ds[...], q4) * SCALE).astype(BF)
            dqkv[2, r, cl] = nn(pst[slot], d4).astype(BF)

            @pl.when(lax.rem(it, 6) == 5)
            def _():
                rs.tick(step * VIRT + GAP[0] + lax.div(it, 6))
            return c
        lax.fori_loop(0, 4 * NG, attend, 0)

        for n, j in ((0, 0), (1, 2)):
            y = jnp.sum(dqkv[j].astype(F32), axis=0, keepdims=True)
            for t in range(2):
                sums[l, t, 12 + n:13 + n, :UC] = y[:, t * UC:(t + 1) * UC]
        loads[4].wait()
        emt[...] = n1[...].T
        for j in range(3):
            emit(l, 9 + j, nn(emt[...], dqkv[j]))
        for j in range(3):
            step_unit(l, 9 + j)
            y = nt(dqkv[j], w2d(wbuf, (9 + j) % 2))
            if j == 0:
                acc[...] = y
            else:
                acc[...] += y
        acc[...] = nn(permt[l], acc[...].astype(BF))
        loads[5].wait()

        def ln1(i):
            r = pl.ds(i * WT, WT)
            grad, gsum, bsum = norm_back(xb[r], acc[r], vec[pl.ds(l * 6, 1)])
            e[r] += grad
            sums[l, 2, 0:1] += gsum
            sums[l, 2, 2:3] += bsum
        rows_loop(4, ln1)
        return carry
    lax.fori_loop(0, LAYERS, layer, 0)
    em[...] = e[...].astype(BF)
    grad_swap = pltpu.make_async_remote_copy(
        src_ref=em.at[theirs], dst_ref=gin, send_sem=xsend.at[1], recv_sem=xrecv.at[1],
        device_id=at.side(at.x_side), device_id_type=MESH)
    grad_swap.start()
    gt[t_here] = e[mine]

    base = LAYERS * VIRT

    def fold(i, c):
        for h in range(HG):
            x = jnp.zeros((2 * WIN, UC), F32)
            for pair in range(WIN // 2):
                part = dsum[lax.div(i, NG), lax.rem(i, NG), 2 * pair * WIN:2 * (pair + 1) * WIN, h * WT:(h + 1) * WT]
                part = jnp.concatenate([part, jnp.zeros((2 * WIN, UC - WT), F32)], axis=1)
                x = x + pltpu.roll(part, (WIN - 1 - 2 * pair) * WIN, 1)
            folded[i * HG + h] = x[:WIN] + pltpu.roll(x[WIN:], UC - WIN, 1)

        @pl.when(lax.rem(i, 2) == 1)
        def _():
            rs.tick(base + lax.div(i, 2))
        return c
    lax.fori_loop(0, LAYERS * NG, fold, 0)
    y = jnp.zeros((2 * LAYERS * HEADS, PAY), F32)
    for xb in range(WIN):
        hi, lo, _ = split3(folded[:, xb, :])
        y = y + nt(jnp.concatenate([hi, lo], axis=0), fold_matrix(places[...], xb))
    y = y[:LAYERS * HEADS] + y[LAYERS * HEADS:]
    for l in range(LAYERS):
        for t in range(2):
            sums[l, t, :12, :PAY] = y[l * HEADS + t * 12:l * HEADS + t * 12 + 12]

    def small_copy(n, src, dst, device):
        return pltpu.make_async_remote_copy(src_ref=src, dst_ref=dst, send_sem=ssend.at[n], recv_sem=srecv.at[n],
                                            device_id=device, device_id_type=MESH)
    c = at.c
    core_swap = small_copy(0, sums.at[1 - c], sm_core, at.sibling())
    core_swap.start()
    base = base + LAYERS * NG // 2
    rs.tick(base)
    rs.tick(base + 1)
    core_swap.wait_recv()
    for n in range(3):
        sums[c, n] += sm_core[n]
    x_swaps = [small_copy(1, sums.at[c, 1 - t_here], sm_x.at[0], at.side(at.x_side)),
               small_copy(2, sums.at[c, 2], sm_x.at[1], at.side(at.x_side))]
    for cp in x_swaps:
        cp.start()
    rs.tick(base + 2)
    rs.tick(base + 3)
    for cp in x_swaps:
        cp.wait_recv()
    sm_y[0, 0] = sums[c, t_here] + sm_x[0]
    sm_y[0, 1] = sums[c, 2] + sm_x[1]
    y_swap = small_copy(3, sm_y.at[0], sm_y.at[1], at.side(at.y_side))
    y_swap.start()
    rs.tick(base + 4)
    rs.tick(base + 5)
    y_swap.wait_recv()
    sm_z[at.z] = (sm_y[0] + sm_y[1]).astype(BF)
    z_swaps = [small_copy(3 + k, sm_z.at[at.z], sm_z.at[at.z], at.above(k)) for k in (1, 2, 3)]
    for cp in z_swaps:
        cp.start()
    rs.tick(base + 6)
    for cp in z_swaps:
        cp.wait_recv()
    small[c] = (sm_z[0].astype(F32) + sm_z[1].astype(F32)) + (sm_z[2].astype(F32) + sm_z[3].astype(F32))
    last = small_copy(7, small.at[c], small.at[c], at.sibling())
    last.start()
    grad_swap.wait()
    gt[1 - t_here] = gin[...].astype(F32)
    for n in range(7, REDUCE_LAGS[-1] - LAYERS * NG // 2):
        rs.tick(base + n)
    last.wait()
    for cp in [core_swap, y_swap] + x_swaps + z_swaps:
        cp.wait_send()
    block_swap.wait()
    block_keep.wait()


def backward_call(cot, valid, vec, block, w, *saved):
    perm = perm_matrices()
    permt = jnp.asarray(perm.transpose(0, 2, 1), BF)
    return pl.pallas_call(
        backward_kernel,
        out_shape=[sds((2, HALF, D), F32), sds((2, HALF, D), BF), sds((LAYERS, NU, 48, UC), F32),
                   sds((LAYERS, 2, 16, D), F32)],
        in_specs=[VM, SM, VM, VM, VM, VM, AN, AN] + [AN] * 8,
        out_specs=[VM, AN, VM, VM],
        scratch_shapes=[
            pltpu.VMEM((TOK, D), F32), pltpu.VMEM((WT, HT), F32), pltpu.VMEM((WT, HT), BF),
            pltpu.VMEM((LAYERS, 3, 16, D), F32), pltpu.VMEM((LAYERS * HEADS, WIN, UC), F32),
            pltpu.VMEM((LAYERS, NG, WT, HT), F32), pltpu.VMEM((3, 16, D), F32), pltpu.VMEM((2, 16, D), F32),
            pltpu.VMEM((2, 2, 16, D), F32), pltpu.VMEM((4, 2, 16, D), BF), pltpu.VMEM((HALF, D), BF),
            pltpu.VMEM((2, 4, 2, 2, 48, 2 * UC), BF),
            pltpu.VMEM((TOK, D), F32), pltpu.VMEM((TOK, D), BF), pltpu.VMEM((TOK, D), BF),
            pltpu.VMEM((3, TOK, D), BF), pltpu.VMEM((TOK, D), BF), pltpu.VMEM((TOK, D), BF),
            pltpu.VMEM((3, TOK, D), BF), pltpu.VMEM((TOK, D), F32), pltpu.VMEM((TOK, D), BF),
            pltpu.VMEM((D, TOK), BF), pltpu.VMEM((D, TOK), BF), pltpu.VMEM((2, WT, HT), BF),
            pltpu.VMEM((2, 2, TOK, 2 * UC), BF), pltpu.VMEM((TOK, 2 * UC), F32), pltpu.VMEM((TOK, 2 * UC), BF),
            pltpu.VMEM((REDUCE_SLOTS + CORE_SLOTS, 2, 4, 2, 48, UC), BF),
            pltpu.VMEM((CORE_SLOTS, 2, 4, 2, 48, UC), BF), pltpu.VMEM((REDUCE_SLOTS, 2, 4, 48, UC), BF),
            pltpu.VMEM((REDUCE_SLOTS, 4, 48, UC), BF), pltpu.VMEM((REDUCE_SLOTS, 3, 48, UC), BF),
            pltpu.SemaphoreType.DMA((2, 2)), pltpu.SemaphoreType.DMA((6,)),
            pltpu.SemaphoreType.DMA((2,)), pltpu.SemaphoreType.DMA((2,)),
            pltpu.SemaphoreType.DMA((REDUCE_SLOTS, 7)), pltpu.SemaphoreType.DMA((REDUCE_SLOTS, 7)),
            pltpu.SemaphoreType.DMA((2,)), pltpu.SemaphoreType.DMA((2,)), pltpu.SemaphoreType.DMA((1,)),
            pltpu.SemaphoreType.DMA((8,)), pltpu.SemaphoreType.DMA((8,)),
        ],
        compiler_params=pltpu.CompilerParams(vmem_limit_bytes=62 * 2**20, collective_id=1, has_side_effects=True),
        name="backward",
    )(cot, valid, vec, fold_places(), jnp.asarray(perm, BF), permt, block, w, *saved)


def layer_norm(values, row_gain, row_shift):
    average = jnp.mean(values, axis=-1, keepdims=True)
    centred = values - average
    variance = jnp.mean(centred * centred, axis=-1, keepdims=True)
    return centred * lax.rsqrt(variance + EPSILON) * row_gain + row_shift


def gelu_exact(values):
    return jax.nn.gelu(values, approximate=False)


def to_windows(rows_data, shifted):
    slot_count = rows_data.shape[1]
    trailing = rows_data.shape[2:]
    image_grid = rows_data.reshape((SIDE, SIDE, slot_count) + trailing)
    if shifted:
        image_grid = jnp.roll(image_grid, (-SHIFT, -SHIFT), axis=(0, 1))
    image_grid = image_grid.reshape((2, WIN, 2, WIN, slot_count) + trailing)
    axes_order = (4, 0, 2, 1, 3) + tuple(range(5, 5 + len(trailing)))
    return jnp.transpose(image_grid, axes_order).reshape((slot_count, 4, WIN * WIN) + trailing)


def from_windows(window_data, shifted):
    slot_count = window_data.shape[0]
    trailing = window_data.shape[3:]
    image_grid = window_data.reshape((slot_count, 2, 2, WIN, WIN) + trailing)
    axes_order = (1, 3, 2, 4, 0) + tuple(range(5, 5 + len(trailing)))
    image_grid = jnp.transpose(image_grid, axes_order).reshape((SIDE, SIDE, slot_count) + trailing)
    if shifted:
        image_grid = jnp.roll(image_grid, (SHIFT, SHIFT), axis=(0, 1))
    return image_grid.reshape((SIDE * SIDE, slot_count) + trailing)


def plan_mask():
    places = jnp.arange(SIDE, dtype=jnp.int32)
    band_of = (places >= SIDE - WIN).astype(jnp.int32) + (places >= SIDE - SHIFT).astype(jnp.int32)
    region = band_of[:, None] * 3 + band_of[None, :]
    region = region.reshape(2, WIN, 2, WIN).transpose(0, 2, 1, 3).reshape(4, WIN * WIN)
    same_region = region[:, :, None] == region[:, None, :]
    return jnp.where(same_region, 0.0, MASK_FILL).astype(jnp.float32)


def offset_table():
    places = jnp.arange(WIN, dtype=jnp.int32)
    targets = jnp.arange(2 * WIN - 1, dtype=jnp.int32)
    offsets = places[:, None] - places[None, :] + WIN - 1
    return (targets[None, None, :] == offsets[:, :, None]).astype(jnp.float32)


def table_bias(table_rows):
    one_hot = offset_table()
    shaped = table_rows.reshape(table_rows.shape[0], 2 * WIN - 1, 2 * WIN - 1)
    spread = jnp.einsum(
        "acr,bds,hrs->habcd", one_hot, one_hot, shaped, precision=lax.Precision.HIGHEST
    )
    return spread.reshape(table_rows.shape[0], WIN * WIN, WIN * WIN)


def table_back(score_sum):
    one_hot = offset_table()
    shaped = score_sum.reshape(score_sum.shape[0], WIN, WIN, WIN, WIN)
    folded = jnp.einsum(
        "acr,bds,habcd->hrs", one_hot, one_hot, shaped, precision=lax.Precision.HIGHEST
    )
    return folded.reshape(score_sum.shape[0], RELS)


def attend_image(pieces, bias_add, scale_factor):
    queries, key_rows, value_rows = pieces
    scores = (
        jnp.einsum("wqhc,wkhc->whqk", queries, key_rows, preferred_element_type=jnp.float32)
        * scale_factor
        + bias_add
    )
    row_top = jnp.max(scores, axis=-1, keepdims=True)
    log_total = row_top + jnp.log(jnp.sum(jnp.exp(scores - row_top), axis=-1, keepdims=True))
    prob_rows = jnp.exp(scores - log_total)
    blended = jnp.einsum(
        "whqk,wkhc->wqhc",
        prob_rows.astype(jnp.bfloat16),
        value_rows,
        preferred_element_type=jnp.float32,
    )
    return (blended.astype(jnp.bfloat16), log_total[..., 0])


def attend_back(pieces, bias_add, scale_factor):
    queries, key_rows, value_rows, log_total, grad_out = pieces
    scores = (
        jnp.einsum("wqhc,wkhc->whqk", queries, key_rows, preferred_element_type=jnp.float32)
        * scale_factor
        + bias_add
    )
    prob_rows = jnp.exp(scores - log_total[..., None])
    prob_low = prob_rows.astype(jnp.bfloat16)
    grad_prob = jnp.einsum(
        "wqhc,wkhc->whqk", grad_out, value_rows, preferred_element_type=jnp.float32
    )
    grad_value = jnp.einsum(
        "whqk,wqhc->wkhc", prob_low, grad_out, preferred_element_type=jnp.float32
    ).astype(jnp.bfloat16)
    grad_score = (
        prob_rows * (grad_prob - jnp.sum(grad_prob * prob_rows, axis=-1, keepdims=True))
    ).astype(jnp.bfloat16)
    grad_query = (
        jnp.einsum("whqk,wkhc->wqhc", grad_score, key_rows, preferred_element_type=jnp.float32)
        * scale_factor
    ).astype(jnp.bfloat16)
    grad_key = (
        jnp.einsum("whqk,wqhc->wkhc", grad_score, queries, preferred_element_type=jnp.float32)
        * scale_factor
    ).astype(jnp.bfloat16)
    score_sum = jnp.sum(grad_score, axis=0, dtype=jnp.float32)
    return (grad_query, grad_key, grad_value, score_sum)


def shards(
    tokens,
    valid,
    cotangent,
    row_gain,
    row_bias,
    w_qkv,
    qv_bias,
    w_proj,
    w_fc1,
    fc1_bias,
    w_fc2,
    rel_table,
):
    slot_count = tokens.shape[1]
    heads_here = rel_table.shape[1]
    head_shape = (slot_count, 4, WIN * WIN, heads_here, HDIM)
    window_shape = (slot_count, 4, WIN * WIN, heads_here * HDIM)
    scale_factor = HDIM ** (-0.5)
    residual = tokens.astype(jnp.float32)
    stored = []
    for layer_index in range(LAYERS):
        shifted = layer_index % 2 == 1
        gain_rows, bias_rows, qkv_full, proj_full, fc1_full, fc2_full = (
            lax.all_gather(row_gain[layer_index], "dp", axis=1, tiled=True),
            lax.all_gather(row_bias[layer_index], "dp", axis=1, tiled=True),
            lax.all_gather(w_qkv[layer_index], "dp", axis=0, tiled=True),
            lax.all_gather(w_proj[layer_index], "dp", axis=1, tiled=True),
            lax.all_gather(w_fc1[layer_index], "dp", axis=0, tiled=True),
            lax.all_gather(w_fc2[layer_index], "dp", axis=1, tiled=True),
        )
        gain_rows = gain_rows.astype(jnp.float32)
        bias_rows = bias_rows.astype(jnp.float32)
        normed, norm_back = jax.vjp(layer_norm, residual, gain_rows[0], bias_rows[0])
        full_normed = lax.all_gather(normed.astype(jnp.bfloat16), "tensor", axis=0, tiled=True)
        projected = jnp.einsum(
            "tsd,dke->tske", full_normed, qkv_full, preferred_element_type=jnp.float32
        )
        pair_bias = qv_bias[layer_index].astype(jnp.float32)
        queries = to_windows(
            (projected[:, :, 0] + pair_bias[0]).astype(jnp.bfloat16), shifted
        ).reshape(head_shape)
        key_rows = to_windows(projected[:, :, 1].astype(jnp.bfloat16), shifted).reshape(head_shape)
        value_rows = to_windows(
            (projected[:, :, 2] + pair_bias[1]).astype(jnp.bfloat16), shifted
        ).reshape(head_shape)
        bias_add = table_bias(rel_table[layer_index])[None]
        if shifted:
            bias_add = bias_add + plan_mask()[:, None]
        blended, log_total = lax.map(
            lambda pieces: attend_image(pieces, bias_add, scale_factor),
            (queries, key_rows, value_rows),
        )
        out_rows = from_windows(blended.reshape(window_shape), shifted)
        attention = lax.psum_scatter(
            jnp.einsum(
                "tse,ed->tsd", out_rows, proj_full, preferred_element_type=jnp.float32
            ).astype(jnp.bfloat16),
            "tensor",
            scatter_dimension=0,
            tiled=True,
        ).astype(jnp.float32)
        residual_mid = residual + attention + bias_rows[1]
        normed_mid, mid_back = jax.vjp(layer_norm, residual_mid, gain_rows[1], bias_rows[2])
        mid_low = normed_mid.astype(jnp.bfloat16)
        fc1_use, fc2_use, fc1_bias_use = (fc1_full, fc2_full, fc1_bias[layer_index])
        mlp_input = lax.all_gather(mid_low, "tensor", axis=0, tiled=True)
        hidden_pre = jnp.einsum(
            "tsd,df->tsf", mlp_input, fc1_use, preferred_element_type=jnp.float32
        ) + fc1_bias_use.astype(jnp.float32)
        activated, gelu_back = jax.vjp(gelu_exact, hidden_pre)
        act_low = activated.astype(jnp.bfloat16)
        mlp_sum = lax.psum_scatter(
            jnp.einsum("tsf,fd->tsd", act_low, fc2_use, preferred_element_type=jnp.float32).astype(
                jnp.bfloat16
            ),
            "tensor",
            scatter_dimension=0,
            tiled=True,
        ).astype(jnp.float32)
        residual = residual_mid + mlp_sum + bias_rows[3]
        stored.append(
            (
                shifted,
                norm_back,
                mid_back,
                gelu_back,
                full_normed,
                queries,
                key_rows,
                value_rows,
                log_total,
                bias_add,
                out_rows,
                mlp_input,
                act_low,
                qkv_full,
                proj_full,
                fc1_use,
                fc2_use,
            )
        )
    valid_rows = valid.astype(jnp.float32)[None, :, None]
    block_out = (residual * valid_rows).astype(jnp.bfloat16)
    grad_stream = cotangent.astype(jnp.float32) * valid_rows
    results = [None] * LAYERS
    for layer_index in reversed(range(LAYERS)):
        (
            shifted,
            norm_back,
            mid_back,
            gelu_back,
            full_normed,
            queries,
            key_rows,
            value_rows,
            log_total,
            bias_add,
            out_rows,
            mlp_input,
            act_low,
            qkv_full,
            proj_full,
            fc1_use,
            fc2_use,
        ) = stored[layer_index]
        grad_bias_last = jnp.sum(grad_stream, axis=(0, 1))
        grad_low = grad_stream.astype(jnp.bfloat16)
        grad_full = lax.all_gather(grad_low, "tensor", axis=0, tiled=True)
        grad_act = jnp.einsum("tsd,fd->tsf", grad_full, fc2_use, preferred_element_type=jnp.float32)
        grad_pre = gelu_back(grad_act)[0].astype(jnp.bfloat16)
        fc2_grad = jnp.einsum("tsf,tsd->fd", act_low, grad_full, preferred_element_type=jnp.float32)
        fc1_grad = jnp.einsum(
            "tsd,tsf->df", mlp_input, grad_pre, preferred_element_type=jnp.float32
        )
        fc1_bias_grad = jnp.sum(grad_pre, axis=(0, 1), dtype=jnp.float32)
        grad_mid = lax.psum_scatter(
            jnp.einsum("tsf,df->tsd", grad_pre, fc1_use, preferred_element_type=jnp.float32).astype(
                jnp.bfloat16
            ),
            "tensor",
            scatter_dimension=0,
            tiled=True,
        ).astype(jnp.float32)
        grad_res, grad_gain_mid, grad_bias_mid = mid_back(grad_mid)
        grad_stream = grad_stream + grad_res
        grad_bias_attn = jnp.sum(grad_stream, axis=(0, 1))
        grad_attn = lax.all_gather(grad_stream.astype(jnp.bfloat16), "tensor", axis=0, tiled=True)
        proj_grad = jnp.einsum(
            "tse,tsd->ed", out_rows, grad_attn, preferred_element_type=jnp.float32
        )
        grad_out = jnp.einsum(
            "tsd,ed->tse", grad_attn, proj_full, preferred_element_type=jnp.float32
        ).astype(jnp.bfloat16)
        grad_out = to_windows(grad_out, shifted).reshape(head_shape)
        grad_query, grad_key, grad_value, score_sums = lax.map(
            lambda pieces: attend_back(pieces, bias_add, scale_factor),
            (queries, key_rows, value_rows, log_total, grad_out),
        )
        table_grad = table_back(jnp.sum(score_sums, axis=0))
        grad_qkv = jnp.stack(
            [
                from_windows(member.reshape(window_shape), shifted)
                for member in (grad_query, grad_key, grad_value)
            ],
            axis=2,
        )
        qv_grad = jnp.stack(
            [
                jnp.sum(grad_qkv[:, :, 0], axis=(0, 1), dtype=jnp.float32),
                jnp.sum(grad_qkv[:, :, 2], axis=(0, 1), dtype=jnp.float32),
            ]
        )
        qkv_grad = jnp.einsum(
            "tsd,tske->dke", full_normed, grad_qkv, preferred_element_type=jnp.float32
        )
        grad_normed = lax.psum_scatter(
            jnp.einsum(
                "tske,dke->tsd", grad_qkv, qkv_full, preferred_element_type=jnp.float32
            ).astype(jnp.bfloat16),
            "tensor",
            scatter_dimension=0,
            tiled=True,
        ).astype(jnp.float32)
        grad_res, grad_gain_first, grad_bias_first = norm_back(grad_normed)
        grad_stream = grad_stream + grad_res
        gain_grads = jnp.stack([grad_gain_first, grad_gain_mid])
        bias_grads = jnp.stack([grad_bias_first, grad_bias_attn, grad_bias_mid, grad_bias_last])
        gain_grads, bias_grads = lax.psum((gain_grads, bias_grads), "tensor")
        shard_grads = (
            lax.psum_scatter(
                gain_grads.astype(jnp.bfloat16), "dp", scatter_dimension=1, tiled=True
            ).astype(jnp.float32),
            lax.psum_scatter(
                bias_grads.astype(jnp.bfloat16), "dp", scatter_dimension=1, tiled=True
            ).astype(jnp.float32),
            lax.psum_scatter(
                qkv_grad.astype(jnp.bfloat16), "dp", scatter_dimension=0, tiled=True
            ).astype(jnp.float32),
            lax.psum_scatter(
                proj_grad.astype(jnp.bfloat16), "dp", scatter_dimension=1, tiled=True
            ).astype(jnp.float32),
            lax.psum_scatter(
                fc1_grad.astype(jnp.bfloat16), "dp", scatter_dimension=0, tiled=True
            ).astype(jnp.float32),
            lax.psum_scatter(
                fc2_grad.astype(jnp.bfloat16), "dp", scatter_dimension=1, tiled=True
            ).astype(jnp.float32),
        )
        small_grads = lax.psum((qv_grad, fc1_bias_grad, table_grad), "dp")
        results[layer_index] = tuple(shard_grads) + tuple(small_grads)
    stacked = [
        jnp.stack([results[which_layer][member] for which_layer in range(LAYERS)])
        for member in range(9)
    ]
    (
        grad_row_gain,
        grad_row_bias,
        grad_w_qkv,
        grad_w_proj,
        grad_w_fc1,
        grad_w_fc2,
        grad_qv_bias,
        grad_fc1_bias,
        grad_rel_table,
    ) = stacked
    return (
        block_out,
        grad_stream,
        grad_row_gain,
        grad_row_bias,
        grad_w_qkv,
        grad_qv_bias,
        grad_w_proj,
        grad_w_fc1,
        grad_fc1_bias,
        grad_w_fc2,
        grad_rel_table,
    )


def unit_stack(w_qkv, w_proj, w_fc1, w_fc2):
    layers, rows = w_qkv.shape[:2]
    qkv = jnp.transpose(w_qkv, (0, 2, 1, 3))
    proj = jnp.swapaxes(w_proj, 1, 2)[:, None]
    fc1 = jnp.transpose(w_fc1.reshape(layers, rows, 4, UC), (0, 2, 1, 3))
    fc2 = jnp.transpose(w_fc2.reshape(layers, 4, UC, rows), (0, 1, 3, 2))
    ff = jnp.stack([fc1, fc2], axis=2).reshape(layers, 8, rows, UC)
    return jnp.concatenate([qkv, proj, ff], axis=1).reshape(layers * NU, rows, UC)


def unit_split(units):
    rows = units.shape[2]
    qkv = jnp.transpose(units[:, :3], (0, 2, 1, 3))
    proj = jnp.swapaxes(units[:, 3], 1, 2)
    fc1 = jnp.transpose(units[:, 4:8], (0, 2, 1, 3)).reshape(LAYERS, rows, 4 * UC)
    fc2 = jnp.transpose(units[:, 8:], (0, 1, 3, 2)).reshape(LAYERS, 4 * UC, rows)
    return qkv, proj, fc1, fc2


def image_shards(tokens, valid, cotangent, row_gain, row_bias, w_qkv, qv_bias, w_proj, w_fc1, fc1_bias, w_fc2, rel_table):
    d = lax.axis_index("dp")
    shard = unit_stack(w_qkv, w_proj, w_fc1, w_fc2)
    vecs = jnp.concatenate([row_gain, row_bias], axis=1).reshape(LAYERS * 6, 48)
    vshard = jnp.pad(vecs.T, ((0, 0), (0, 128 - LAYERS * 6)))[None]
    rows = jnp.concatenate([qv_bias.reshape(2 * LAYERS, UC), fc1_bias.reshape(4 * LAYERS, UC)]).astype(F32)
    pay = jnp.concatenate([jnp.pad(rows, ((0, 4), (0, PAY - UC))),
                           jnp.pad(rel_table.reshape(LAYERS * 12, RELS), ((0, 0), (0, PAY - RELS)))])
    block, vec, cot, w, *saved = forward_call(
        jnp.swapaxes(tokens, 0, 1), jnp.swapaxes(cotangent, 0, 1), valid, vshard, pay, shard)
    gt, block, total, small = backward_call(cot, valid, vec, block, w, *saved)
    qkv_g, proj_g, fc1_g, fc2_g = unit_split(total)
    rowg = lax.dynamic_slice(small[:, 1], (0, 0, d * 48), (LAYERS, 6, 48))
    own = small[:, 0]
    return (jnp.swapaxes(block, 0, 1), jnp.swapaxes(gt, 0, 1), rowg[:, :2], rowg[:, 2:], qkv_g, own[:, 12:14, :UC],
            proj_g, fc1_g, own[:, 14:16].reshape(LAYERS, 4 * UC), fc2_g, own[:, :12, :RELS])


def solution(mesh):
    whole_images = mesh.shape["tensor"] == 2 and mesh.shape["dp"] == 16
    return jax.shard_map(
        image_shards if whole_images else shards,
        mesh=mesh,
        in_specs=(
            P("tensor", "dp", None),
            P("dp"),
            P("tensor", "dp", None),
            P(None, None, "dp"),
            P(None, None, "dp"),
            P(None, "dp", None, "tensor"),
            P(None, None, "tensor"),
            P(None, "tensor", "dp"),
            P(None, "dp", "tensor"),
            P(None, "tensor"),
            P(None, "tensor", "dp"),
            P(None, "tensor", None),
        ),
        out_specs=(
            P("tensor", "dp", None),
            P("tensor", "dp", None),
            P(None, None, "dp"),
            P(None, None, "dp"),
            P(None, "dp", None, "tensor"),
            P(None, None, "tensor"),
            P(None, "tensor", "dp"),
            P(None, "dp", "tensor"),
            P(None, "tensor"),
            P(None, "tensor", "dp"),
            P(None, "tensor", None),
        ),
        check_vma=False,
    )
```
